32 devices in a mesh: dp: 8 (over y, x, core), tensor: 4 (over z).
Axes of the slice: x: 2, y: 2, z: 4, core: 2. Of those that a mesh axis runs over, the one named last changes fastest.
Arguments:
- block_input: bfloat16 [8192, 1536], P(('dp', 'tensor')), may hold values from -6 to 6
- attn_gain: bfloat16 [1536], P('dp'), may hold values from 0.5 to 1.5
- w_query: bfloat16 [1536, 1536], P('dp', 'tensor'), may hold values from -0.15625 to 0.15625
- w_key: bfloat16 [1536, 1536], P('dp', 'tensor'), may hold values from -0.15625 to 0.15625
- w_value: bfloat16 [1536, 1536], P('dp', 'tensor'), may hold values from -0.15625 to 0.15625
- w_forget: bfloat16 [1536, 24], P(None, 'tensor'), may hold values from -0.15625 to 0.15625
- forget_bias: float32 [24], P('tensor'), may hold values from -1 to 7
- w_output: bfloat16 [1536, 1536], P('tensor', 'dp'), may hold values from -0.625 to 0.625
- mlp_gain: bfloat16 [1536], P('dp'), may hold values from 0.5 to 1.5
- w_gate: bfloat16 [1536, 4096], P('dp', 'tensor'), may hold values from -0.15625 to 0.15625
- w_up: bfloat16 [1536, 4096], P('dp', 'tensor'), may hold values from -0.15625 to 0.15625
- w_down: bfloat16 [4096, 1536], P('tensor', 'dp'), may hold values from -0.09375 to 0.09375
- segment_ids: int32 [8, 1024], P('dp'), may hold values from 0 to 3, never falling along the last dimension, each value on 1 to 512 neighbouring positions
- cotangent: bfloat16 [8192, 1536], P(('dp', 'tensor')), may hold values from -6 to 6
Outputs:
- output: bfloat16 [8192, 1536], P(('dp', 'tensor'))
- input_grad: float32 [8192, 1536], P(('dp', 'tensor'))
- grad_attn_gain: float32 [1536], P('dp')
- grad_w_query: float32 [1536, 1536], P('dp', 'tensor')
- grad_w_key: float32 [1536, 1536], P('dp', 'tensor')
- grad_w_value: float32 [1536, 1536], P('dp', 'tensor')
- grad_w_forget: float32 [1536, 24], P(None, 'tensor')
- grad_forget_bias: float32 [24], P('tensor')
- grad_w_output: float32 [1536, 1536], P('tensor', 'dp')
- grad_mlp_gain: float32 [1536], P('dp')
- grad_w_gate: float32 [1536, 4096], P('dp', 'tensor')
- grad_w_up: float32 [1536, 4096], P('dp', 'tensor')
- grad_w_down: float32 [4096, 1536], P('tensor', 'dp')
The draws below stay inside these ranges and needn't reach their ends.
Inputs may be any that keep to these rules, and one draw needn't show every extreme that they name: Each row of segment_ids numbers the documents of one sequence in order, never falling; a document has 1 to 512 tokens, and the longest of a row has exactly 512.
All inputs are finite; a program needn't handle non-finite values.
Results may differ from the reference program's by a relative error of at most 0.018.
Values may be sent and summed in bfloat16 or wider, within the bound.
No kernel may reach another device: no remote copies, remote signals or barrier semaphores. Data moves between devices by JAX's collectives and lax.ppermute only.
A program may use at most 128 MiB of HBM per device.

```python
import math
import jax
import jax.numpy as jnp
import numpy as np
from jax import lax

D = 1536
H = 24
FF = 4096
SEQ_LEN = 1024
TOKENS = 8192
N_DP = 8


def levels(rng, dims, split, least, largest):
    def one(axis_at, shards_of):
        draws = jax.random.uniform(jax.random.fold_in(jax.random.fold_in(rng, 6), axis_at), (shards_of,), jnp.float32, least / len(split), largest / len(split))
        return jnp.repeat(jnp.exp(draws), dims[axis_at] // shards_of).reshape((-1,) + (1,) * (len(dims) - axis_at - 1))

    level = one(*split[0])
    for cut in split[1:]:
        level = level * one(*cut)
    return level


def profile(amount, total, reach, slope):
    weights = [(1 << 20) // math.isqrt(standing ** slope) + 1 for standing in range(2, amount + 1)]
    surplus, counts = total - reach - (amount - 1), [1] * (amount - 1)
    while surplus > 0:
        candidates = [i for i in range(amount - 1) if counts[i] < reach]
        pool, budget = sum([weights[i] for i in candidates]), surplus
        for i in candidates:
            more = min(reach - counts[i], max(1, budget * weights[i] // pool), surplus)
            counts[i] = counts[i] + more
            surplus = surplus - more
    return np.array([reach] + counts)


def ragged(key, number_of, total, reach, skew):
    if number_of == 2:
        one = jax.random.randint(key, (), max(1, total - reach), min(reach, total - 1) + 1)
        return jnp.stack([one, total - one])
    tallies = jnp.asarray(profile(number_of, total, reach, skew), jnp.int32)
    couples = (number_of - 1) // 2
    giver, taker = tallies[1:1 + 2 * couples:2], tallies[2:2 + 2 * couples:2]
    slack = jnp.minimum(giver - 1, reach - taker)
    moved = jax.random.randint(jax.random.fold_in(key, 1), (couples,), 0, 1 << 20) % (slack + 1)
    tallies = tallies.at[1:1 + 2 * couples:2].set(giver - moved).at[2:2 + 2 * couples:2].set(taker + moved)
    return tallies[jax.random.permutation(jax.random.fold_in(key, 2), number_of)]


def normal_values(stream_key, dims, spread, most, pieces=(), held_as=jnp.bfloat16):
    loudness = levels(stream_key, dims, pieces, -0.22, 0.18) if pieces else 1.0
    result = jax.random.normal(stream_key, dims, jnp.float32) * spread * loudness
    return jnp.minimum(jnp.maximum(result, -most), most).astype(held_as)


def setup_inputs(seed: int = 0) -> dict:
    seeds = jax.random.split(jax.random.key(seed), 15)
    return {
        "block_input": normal_values(seeds[0], (TOKENS, D), 1.0, 6.0, ((0, 32),)),
        "attn_gain": jnp.clip(1.0 + 0.1 * jax.random.normal(seeds[1], (D,), jnp.float32), 0.5, 1.5).astype(jnp.bfloat16),
        "w_query": normal_values(seeds[2], (D, D), D ** -0.5, 0.15625, ((0, 8), (1, 4))),
        "w_key": normal_values(seeds[3], (D, D), D ** -0.5, 0.15625, ((0, 8), (1, 4))),
        "w_value": normal_values(seeds[4], (D, D), D ** -0.5, 0.15625, ((0, 8), (1, 4))),
        "w_forget": normal_values(seeds[5], (D, H), D ** -0.5, 0.15625, ((1, 4),)),
        "forget_bias": jnp.clip(-1.0 + 8.0 * jax.random.uniform(seeds[6], (H,), jnp.float32) ** levels(seeds[6], (H,), ((0, 4),), -0.2, 0.2), -1.0, 7.0),
        "w_output": normal_values(seeds[7], (D, D), (D // 16) ** -0.5, 0.625, ((0, 4), (1, 8))),
        "mlp_gain": jnp.clip(1.0 + 0.1 * jax.random.normal(seeds[8], (D,), jnp.float32), 0.5, 1.5).astype(jnp.bfloat16),
        "w_gate": normal_values(seeds[9], (D, FF), D ** -0.5, 0.15625, ((0, 8), (1, 4))),
        "w_up": normal_values(seeds[10], (D, FF), D ** -0.5, 0.15625, ((0, 8), (1, 4))),
        "w_down": normal_values(seeds[11], (FF, D), FF ** -0.5, 0.09375, ((0, 4), (1, 8))),
        "segment_ids": jax.vmap(lambda own: jnp.searchsorted(jnp.cumsum(ragged(own, max(4, SEQ_LEN // 256), SEQ_LEN, SEQ_LEN // 2, 1)), jnp.arange(SEQ_LEN), side="right"))(jax.random.split(seeds[12], N_DP)).reshape((N_DP, SEQ_LEN)).astype(jnp.int32),
        "cotangent": normal_values(seeds[13], (TOKENS, D), 1.0, 6.0, ((0, 32),)),
    }


EPS = 1e-06
HIGH = lax.Precision.HIGHEST

@jax.custom_vjp
def low(v):
    return lax.optimization_barrier(v.astype(jnp.bfloat16)).astype(jnp.float32)

@jax.custom_vjp
def low_back(v):
    return v

def low_keep(v):
    return (low(v), None)

def low_pass(kept, grad):
    return (grad,)

def back_keep(v):
    return (v, None)

def back_low(kept, grad):
    return (low(grad),)
low.defvjp(low_keep, low_pass)
low_back.defvjp(back_keep, back_low)

def product(left, right):
    return jnp.dot(left, right, precision=HIGH)

def norm_rows(value, gain):
    scale = lax.rsqrt(lax.optimization_barrier(jnp.mean(value * value, axis=-1, keepdims=True)) + EPS)
    return value * scale * gain

def one_sequence(pack):
    query, keys, values, cumul, seg_row = pack
    length = query.shape[0]
    block = min(512, length)
    starts = jnp.arange(length // block, dtype=jnp.int32) * block
    columns = jnp.arange(length, dtype=jnp.int32)

    def one_block(start):
        query_rows = lax.dynamic_slice_in_dim(query, start, block, 0)
        raw = jnp.einsum('qhd,khd->hqk', query_rows, keys, precision=HIGH)
        cum_rows = lax.dynamic_slice_in_dim(cumul, start, block, 0)
        scores = low_back(raw * 0.125) + cum_rows.T[:, :, None] - cumul.T[:, None, :]
        positions = start + jnp.arange(block, dtype=jnp.int32)
        seg_rows = lax.dynamic_slice_in_dim(seg_row, start, block, 0)
        allowed = (columns[None, :] <= positions[:, None]) & (seg_rows[:, None] == seg_row[None, :])
        scores = jnp.where(allowed[None], scores, -jnp.inf)
        probs = jax.nn.softmax(scores, axis=-1)
        return jnp.einsum('hqk,khd->qhd', low(probs), values, precision=HIGH)
    outs = lax.map(jax.checkpoint(one_block), starts)
    return outs.reshape(length, query.shape[1], query.shape[2])

def layer(block_input, attn_gain, w_query, w_key, w_value, w_forget, forget_bias, w_output, mlp_gain, w_gate, w_up, w_down, segment_ids):
    count, length = segment_ids.shape
    heads = w_forget.shape[1]
    head_size = w_query.shape[1] // heads
    normed = low(norm_rows(block_input, attn_gain))
    query = low(low_back(product(normed, w_query)))
    keys = low(low_back(product(normed, w_key)))
    values = low(low_back(product(normed, w_value)))
    logit = low_back(product(normed, w_forget)) + forget_bias
    cumul = jnp.cumsum(jax.nn.log_sigmoid(logit).reshape(count, length, heads), axis=1)

    def by_heads(array):
        return array.reshape(count, length, heads, head_size)
    mixed = lax.map(jax.checkpoint(one_sequence), (by_heads(query), by_heads(keys), by_heads(values), cumul, segment_ids))
    mixed = low(low_back(mixed.reshape(count * length, heads * head_size)))
    hidden_res = block_input + low_back(product(mixed, w_output))
    second = low(norm_rows(hidden_res, mlp_gain))
    gate = low_back(product(second, w_gate))
    upper = low_back(product(second, w_up))
    hidden = low(low_back(jax.nn.silu(gate) * upper))
    return hidden_res + low_back(product(hidden, w_down))

def reference(block_input, attn_gain, w_query, w_key, w_value, w_forget, forget_bias, w_output, mlp_gain, w_gate, w_up, w_down, segment_ids, cotangent):
    floats = (block_input.astype(jnp.float32), attn_gain.astype(jnp.float32), w_query.astype(jnp.float32), w_key.astype(jnp.float32), w_value.astype(jnp.float32), w_forget.astype(jnp.float32), forget_bias.astype(jnp.float32), w_output.astype(jnp.float32), mlp_gain.astype(jnp.float32), w_gate.astype(jnp.float32), w_up.astype(jnp.float32), w_down.astype(jnp.float32))
    output, pullback = jax.vjp(lambda *params: layer(*params, segment_ids), *floats)
    grads = pullback(cotangent.astype(jnp.float32))
    return (output.astype(jnp.bfloat16), grads[0], grads[1], grads[2], grads[3], grads[4], grads[5], grads[6], grads[7], grads[8], grads[9], grads[10], grads[11])
```

```python
import functools

import jax
import jax.numpy as jnp
from jax import lax
from jax.experimental import pallas as pl
from jax.experimental.pallas import tpu as pltpu
from jax.sharding import PartitionSpec as P

HEAD = 64
PAIR = 2 * HEAD
EPS = 1e-06
F32 = jnp.float32
BF16 = jnp.bfloat16
NT = (((1,), (1,)), ((), ()))
TN = (((0,), (0,)), ((), ()))
AXES = ("dp", "tensor")


def nn(a, b):
    return jnp.dot(a, b, preferred_element_type=F32)


def nt(a, b):
    return lax.dot_general(a, b, NT, preferred_element_type=F32)


def tn(a, b):
    return lax.dot_general(a, b, TN, preferred_element_type=F32)


def send(value, move):
    tensor = lax.axis_size("tensor")
    pairs = []
    for d in range(lax.axis_size("dp")):
        for t in range(tensor):
            to = move(d, t)
            if to is not None:
                pairs.append((d * tensor + t, to[0] * tensor + to[1]))
    return lax.ppermute(value, AXES, pairs)


def to_home(d, t):
    return (d ^ 1, t ^ 2) if (d & 1) != (t >> 1) else (d, t)


def over_core(d, t):
    return (d ^ 1, t)


def over_z(d, t):
    return (d, t ^ 1)


def over_chip(bit):
    return lambda d, t: (d ^ (2 << bit), t)


def spread_one(d, t):
    return (d ^ 1, t) if d & 1 else (d ^ 1, t ^ 2)


def spread_two(d, t):
    return (d, t ^ 2) if d & 1 else None


def collect_one(d, t):
    return (d ^ 1, t ^ 2) if d & 1 else (d ^ 1, t)


def after(value, *others):
    return lax.optimization_barrier((value, *others))[0]


def gather_chips(even, odd, bits):
    evens, odds = {0: even}, {0: odd}
    for bit in range(bits):
        for at, piece in list(evens.items()):
            evens[at | (1 << bit)] = send(piece, over_chip(bit))
    for bit in reversed(range(bits)):
        for at, piece in list(odds.items()):
            odds[at | (1 << bit)] = send(piece, over_chip(bit))
    rows = []
    for at in range(1 << bits):
        rows += [evens[at], odds[at]]
    return jnp.concatenate(rows, axis=0)


def scatter_chips(blocks, order):
    blocks = dict(enumerate(blocks))
    for bit in order:
        kept = {}
        for at in sorted(blocks):
            if not at >> bit & 1:
                there = send(blocks[at | (1 << bit)], over_chip(bit))
                kept[at] = (blocks[at].astype(F32) + there.astype(F32)).astype(BF16)
        blocks = kept
    return blocks[0]


def gather_group(own):
    z = send(own, over_z)
    core = send(own, over_core)
    both = send(z, over_core)
    return own, core, z, both


def scatter_group(halves):
    far = halves(1)
    rows = far.shape[0] // 2
    far_in = send(far[rows:].astype(BF16), over_core)
    far_sum = (far[:rows] + far_in.astype(F32)).astype(BF16)
    far_got = send(far_sum, over_z)
    near = halves(0)
    near_in = send(near[rows:].astype(BF16), over_core)
    return near[:rows] + near_in.astype(F32) + far_got.astype(F32)


def block_of(pos_ref, at, size):
    return pl.ds(pl.multiple_of(pos_ref[at] * size, size), size)


def forward_kernel(quarter, pos_ref, qkv_ref, bias_ref, segr_ref, segc_ref, mixed_ref, lse_ref, cum_ref, cumr_ref):
    pair = pl.program_id(0)
    pairs = pl.num_programs(0)
    width = pairs * PAIR
    lane = lax.broadcasted_iota(jnp.int32, (quarter, PAIR), 1)
    count = segr_ref.shape[1] // quarter

    @pl.when(pair == 0)
    def _():
        rows = lax.broadcasted_iota(jnp.int32, (quarter, quarter), 0)
        cols = lax.broadcasted_iota(jnp.int32, (quarter, quarter), 1)
        lower = (cols <= rows).astype(F32)
        carry = jnp.zeros((1, PAIR), F32)
        for a in range(count):
            logit = qkv_ref[block_of(pos_ref, a, quarter), 3 * width : 3 * width + PAIR] + bias_ref[...]
            logsig = jnp.minimum(logit, 0.0) - jnp.log1p(jnp.exp(-jnp.abs(logit)))
            cum = jnp.dot(lower, logsig, precision=lax.Precision.HIGHEST, preferred_element_type=F32) + carry
            carry = cum[quarter - 1 :, :]
            cum_ref[a * quarter : (a + 1) * quarter, :] = cum
            cumr_ref[:, a * quarter : (a + 1) * quarter] = cum.T[: cumr_ref.shape[0], :]
        lse_ref[...] = jnp.zeros(lse_ref.shape, F32)

    def columns(part):
        return pl.ds(pl.multiple_of(part * width + pair * PAIR, PAIR), PAIR)

    diag_rows = lax.broadcasted_iota(jnp.int32, (quarter, quarter), 0)
    diag_cols = lax.broadcasted_iota(jnp.int32, (quarter, quarter), 1)
    for a in range(count):
        query = (qkv_ref[block_of(pos_ref, a, quarter), columns(0)].astype(BF16) * 0.125).astype(BF16)
        seg_q = segc_ref[a * quarter : (a + 1) * quarter, :]
        spans = range(max(0, a - 512 // quarter), a + 1)
        outs = []
        for h in range(2):
            head = pair * 2 + h
            mine = (lane >= HEAD) if h else (lane < HEAD)
            query_h = jnp.where(mine, query, jnp.zeros_like(query))
            scores = []
            for b in spans:
                keys = qkv_ref[block_of(pos_ref, b, quarter), columns(1)].astype(BF16)
                s = nt(query_h, keys) - cumr_ref[pl.ds(head, 1), b * quarter : (b + 1) * quarter]
                allowed = seg_q == segr_ref[:, b * quarter : (b + 1) * quarter]
                if a == b:
                    allowed &= diag_cols <= diag_rows
                scores.append(jnp.where(allowed, s, -jnp.inf))
            top = functools.reduce(jnp.maximum, [jnp.max(s, axis=1, keepdims=True) for s in scores])
            expd = [jnp.exp(s - top) for s in scores]
            total = functools.reduce(jnp.add, [jnp.sum(e, axis=1, keepdims=True) for e in expd])
            scale = 1.0 / total
            out = None
            for e, b in zip(expd, spans):
                values = qkv_ref[block_of(pos_ref, b, quarter), columns(2)].astype(BF16)
                part = nn((e * scale).astype(BF16), values)
                out = part if out is None else out + part
            outs.append(out)
            lse = top + jnp.log(total)
            at = pl.ds(a * quarter, quarter)
            lse_ref[at, :] = jnp.where(lane == head, lse, lse_ref[at, :])
        mixed_ref[block_of(pos_ref, a, quarter), columns(0)] = jnp.where(lane < HEAD, outs[0], outs[1]).astype(BF16)


def backward_kernel(
    quarter, pos_ref, qkv_ref, bias_ref, segr_ref, segc_ref, lse_ref, cum_ref, gmix_ref,
    grad_ref, gbias_ref, lser_ref, gcol_ref, grow_ref, gk_ref, gv_ref,
):
    pair = pl.program_id(0)
    pairs = pl.num_programs(0)
    width = pairs * PAIR
    lane = lax.broadcasted_iota(jnp.int32, (quarter, PAIR), 1)
    count = segr_ref.shape[1] // quarter
    rows8 = lser_ref.shape[0]

    @pl.when(pair == 0)
    def _():
        for a in range(count):
            at = slice(a * quarter, (a + 1) * quarter)
            lser_ref[:, at] = lse_ref[at, :].T[:rows8, :]
        gcol_ref[...] = jnp.zeros(gcol_ref.shape, F32)
        grow_ref[...] = jnp.zeros(grow_ref.shape, F32)

    def columns(part):
        return pl.ds(pl.multiple_of(part * width + pair * PAIR, PAIR), PAIR)

    diag_rows = lax.broadcasted_iota(jnp.int32, (quarter, quarter), 0)
    diag_cols = lax.broadcasted_iota(jnp.int32, (quarter, quarter), 1)
    gk_ref[...] = jnp.zeros(gk_ref.shape, F32)
    gv_ref[...] = jnp.zeros(gv_ref.shape, F32)
    for a in range(count):
        here = slice(a * quarter, (a + 1) * quarter)
        query = (qkv_ref[block_of(pos_ref, a, quarter), columns(0)].astype(BF16) * 0.125).astype(BF16)
        gout = gmix_ref[block_of(pos_ref, a, quarter), columns(0)]
        seg_q = segr_ref[:, here]
        spans = range(max(0, a - 512 // quarter), a + 1)
        grad_query = None
        for h in range(2):
            head = pair * 2 + h
            mine = (lane >= HEAD) if h else (lane < HEAD)
            query_h = jnp.where(mine, query, jnp.zeros_like(query))
            gout_h = jnp.where(mine, gout, jnp.zeros_like(gout))
            lse = lser_ref[pl.ds(head, 1), here]
            probs, gprobs = [], []
            inner = None
            for b in spans:
                there = slice(b * quarter, (b + 1) * quarter)
                keys = qkv_ref[block_of(pos_ref, b, quarter), columns(1)].astype(BF16)
                values = qkv_ref[block_of(pos_ref, b, quarter), columns(2)].astype(BF16)
                cum_k = jnp.sum(jnp.where(lane == head, cum_ref[there, :], 0.0), axis=1, keepdims=True)
                s = nt(keys, query_h) - cum_k
                allowed = segc_ref[there, :] == seg_q
                if a == b:
                    allowed &= diag_rows <= diag_cols
                p = jnp.where(allowed, jnp.exp(s - lse), 0.0)
                g = nt(values, gout_h)
                probs.append(p)
                gprobs.append(g)
                part = jnp.sum(p * g, axis=0, keepdims=True)
                inner = part if inner is None else inner + part
            row_sum = None
            for p, g, b in zip(probs, gprobs, spans):
                there = slice(b * quarter, (b + 1) * quarter)
                keys = (qkv_ref[block_of(pos_ref, b, quarter), columns(1)].astype(BF16) * 0.125).astype(BF16)
                keys_h = jnp.where(mine, keys, jnp.zeros_like(keys))
                gs = p * (g - inner)
                part = jnp.sum(gs, axis=0, keepdims=True)
                row_sum = part if row_sum is None else row_sum + part
                col_sum = jnp.sum(gs, axis=1, keepdims=True)
                gcol_ref[there, :] += jnp.where(lane == head, col_sum, 0.0)
                low = gs.astype(BF16)
                gk_ref[there, :] += nn(low, query_h)
                gv_ref[there, :] += nn(p.astype(BF16), gout_h)
                part = tn(low, keys_h)
                grad_query = part if grad_query is None else grad_query + part
            grow_ref[pl.ds(head, 1), here] = row_sum
        grad_ref[block_of(pos_ref, a, quarter), columns(0)] = grad_query.astype(BF16)
    for a in range(count):
        here = slice(a * quarter, (a + 1) * quarter)
        grad_ref[block_of(pos_ref, a, quarter), columns(1)] = gk_ref[here, :].astype(BF16)
        grad_ref[block_of(pos_ref, a, quarter), columns(2)] = gv_ref[here, :].astype(BF16)

    @pl.when(pair == pairs - 1)
    def _():
        upper = (diag_cols >= diag_rows).astype(F32)
        carry = jnp.zeros((1, PAIR), F32)
        bias = jnp.zeros((1, PAIR), F32)
        pad = jnp.zeros((PAIR - rows8, quarter), F32)
        for a in reversed(range(count)):
            here = slice(a * quarter, (a + 1) * quarter)
            logit = qkv_ref[block_of(pos_ref, a, quarter), 3 * width : 3 * width + PAIR] + bias_ref[...]
            grow = jnp.concatenate([grow_ref[:, here], pad], axis=0).T
            gcum = jnp.where(lane < 2 * pairs, grow - gcol_ref[here, :], 0.0)
            back = jnp.dot(upper, gcum, precision=lax.Precision.HIGHEST, preferred_element_type=F32) + carry
            carry = back[:1, :]
            glogit = back * (1.0 / (1.0 + jnp.exp(logit)))
            glogit = jnp.where(lane < 2 * pairs, glogit, 0.0)
            bias = bias + jnp.sum(glogit, axis=0, keepdims=True)
            grad_ref[block_of(pos_ref, a, quarter), 3 * width : 3 * width + PAIR] = glogit.astype(BF16)
        gbias_ref[...] = bias


def full_spec(shape):
    return pl.BlockSpec(shape, lambda *_: (0,) * len(shape))


def attend(pos, qkv, bias, seg_row, seg_col, quarter):
    length = qkv.shape[0]
    width = (qkv.shape[1] - PAIR) // 3
    pairs = width // PAIR
    return pl.pallas_call(
        functools.partial(forward_kernel, quarter),
        grid=(pairs,),
        out_shape=(
            jax.ShapeDtypeStruct((length, width), BF16),
            jax.ShapeDtypeStruct((length, PAIR), F32),
            jax.ShapeDtypeStruct((length, PAIR), F32),
        ),
        in_specs=[
            pl.BlockSpec(memory_space=pltpu.SMEM),
            full_spec(qkv.shape),
            full_spec(bias.shape),
            full_spec(seg_row.shape),
            full_spec(seg_col.shape),
        ],
        out_specs=(full_spec((length, width)), full_spec((length, PAIR)), full_spec((length, PAIR))),
        scratch_shapes=[pltpu.VMEM((8, length), F32)],
        compiler_params=pltpu.CompilerParams(vmem_limit_bytes=48 * 2**20, dimension_semantics=("arbitrary",)),
    )(pos, qkv, bias, seg_row, seg_col)


def attend_back(pos, qkv, bias, seg_row, seg_col, lse, cum, grad_mixed, quarter):
    length = qkv.shape[0]
    width = (qkv.shape[1] - PAIR) // 3
    pairs = width // PAIR
    return pl.pallas_call(
        functools.partial(backward_kernel, quarter),
        grid=(pairs,),
        out_shape=(
            jax.ShapeDtypeStruct(qkv.shape, BF16),
            jax.ShapeDtypeStruct((1, PAIR), F32),
        ),
        in_specs=[
            pl.BlockSpec(memory_space=pltpu.SMEM),
            full_spec(qkv.shape),
            full_spec(bias.shape),
            full_spec(seg_row.shape),
            full_spec(seg_col.shape),
            full_spec(lse.shape),
            full_spec(cum.shape),
            full_spec(grad_mixed.shape),
        ],
        out_specs=(full_spec(qkv.shape), full_spec((1, PAIR))),
        scratch_shapes=[
            pltpu.VMEM((8, length), F32),
            pltpu.VMEM((length, PAIR), F32),
            pltpu.VMEM((8, length), F32),
            pltpu.VMEM((length, PAIR), F32),
            pltpu.VMEM((length, PAIR), F32),
        ],
        compiler_params=pltpu.CompilerParams(vmem_limit_bytes=48 * 2**20, dimension_semantics=("arbitrary",)),
    )(pos, qkv, bias, seg_row, seg_col, lse, cum, grad_mixed)


def unit_rows(value):
    scale = lax.rsqrt(jnp.mean(value * value, axis=-1, keepdims=True) + EPS)
    return value * scale, scale


def unit_back(value, scale, weighted):
    inner = jnp.mean(weighted * value, axis=-1, keepdims=True)
    return scale * weighted - value * (scale * scale * scale) * inner


def per_device(
    block_input, attn_gain, w_query, w_key, w_value, w_forget, forget_bias, w_output,
    mlp_gain, w_gate, w_up, w_down, segment_ids, cotangent,
):
    width = block_input.shape[1]
    quarter = block_input.shape[0]
    heads = w_forget.shape[1]
    share = w_query.shape[0]
    chips = lax.axis_size("dp") // 2
    bits = chips.bit_length() - 1
    d = lax.axis_index("dp")
    t = lax.axis_index("tensor")
    core, chip = d & 1, d >> 1
    first = core == 0
    at_home = core == t >> 1
    wide = width // chips

    def reorder(rows):
        return jnp.concatenate(
            [lax.dynamic_slice_in_dim(rows, (chip ^ r) * wide, wide, 1) for r in range(chips)], axis=1
        )

    def spread(pack):
        one = send(pack, spread_one)
        two = send(pack, spread_two)
        even = jnp.where(first, pack, one)
        odd = jnp.where(first, one, two)
        return even, odd

    gain_one = attn_gain.astype(F32)[:, None]
    gain_two = mlp_gain.astype(F32)[:, None]
    forget_own = lax.dynamic_slice_in_dim(w_forget, d * share, share, 0)
    pack_one = jnp.concatenate(
        [
            (w_query.astype(F32) * gain_one).astype(BF16),
            (w_key.astype(F32) * gain_one).astype(BF16),
            (w_value.astype(F32) * gain_one).astype(BF16),
            (forget_own.astype(F32) * gain_one).astype(BF16),
            attn_gain[:, None],
            jnp.zeros((share, PAIR - heads - 1), BF16),
        ],
        axis=1,
    )
    even_one, odd_one = spread(pack_one)

    x_own = send(after(reorder(block_input), pack_one), to_home)
    x_blocks = gather_group(x_own)
    x_all = jnp.concatenate(x_blocks, axis=0)
    cot_own = send(after(reorder(cotangent), x_own), to_home)
    seg_other = send(segment_ids, over_core)
    seg_row = jnp.where(at_home, segment_ids, seg_other)
    seg_col = seg_row.reshape(-1, 1)
    bias_other = send(forget_bias, lambda d, t: (d, t ^ 2))
    bias = jnp.where(first, forget_bias, bias_other)
    bias = jnp.pad(bias, (0, PAIR - heads))[None, :]
    place = (t & 1) + 2 * core
    pos = jnp.stack([((a ^ place) >> 1) | (((a ^ place) & 1) << 1) for a in range(4)]).astype(jnp.int32)

    pack_two = jnp.concatenate([w_output.T, w_down.T], axis=1)
    even_two, odd_two = spread(after(pack_two, x_own))
    pack_three = jnp.concatenate(
        [(w_gate.astype(F32) * gain_two).astype(BF16), (w_up.astype(F32) * gain_two).astype(BF16)], axis=1
    )
    even_three, odd_three = spread(after(pack_three, even_two))

    full_one = gather_chips(even_one, odd_one, bits)
    full_two = gather_chips(after(even_two, full_one), after(odd_two, full_one), bits)
    full_three = gather_chips(after(even_three, full_two), after(odd_three, full_two), bits)
    inner_width = w_output.shape[0]
    wo_t, wd_t = full_two[:, :inner_width], full_two[:, inner_width:]
    hidden_width = w_gate.shape[1]

    x_hat = unit_rows(x_all.astype(F32))[0].astype(BF16)
    resid = x_own.astype(F32)
    first_scale = unit_rows(resid)[1]
    qkv = nn(x_hat, full_one)
    mixed, lse, cum = attend(pos, qkv, bias, seg_row, seg_col, quarter)

    def half(array, which):
        rows = array.shape[0] // 2
        return array[which * rows : (which + 1) * rows]

    hidden_res = resid + scatter_group(lambda which: nt(half(mixed, which), wo_t))
    second, second_scale = unit_rows(hidden_res)
    second_all = jnp.concatenate(gather_group(second.astype(BF16)), axis=0)
    cot_all = jnp.concatenate(gather_group(cot_own), axis=0)

    gate = nn(second_all, full_three[:, :hidden_width])
    upper = nn(second_all, full_three[:, hidden_width:])
    grad_hidden = nn(cot_all, wd_t).astype(BF16).astype(F32)
    sigma = jax.nn.sigmoid(gate)
    swish = gate * sigma
    hidden = (swish * upper).astype(BF16)
    grad_gate = (grad_hidden * upper * sigma * (1.0 + gate * (1.0 - sigma))).astype(BF16)
    grad_up = (grad_hidden * swish).astype(BF16)
    grad_both = jnp.concatenate([grad_gate, grad_up], axis=1)

    def second_part(which):
        return nt(half(grad_both, which), full_three)

    parts = {}

    def second_half(which):
        parts[which] = second_part(which)
        return parts[which]

    grad_second = scatter_group(second_half)
    gain_two_part = functools.reduce(
        jnp.add, [jnp.sum(half(second_all, w).astype(F32) * parts[w], axis=0) for w in (0, 1)]
    )
    grad_res = cot_own.astype(F32) + unit_back(hidden_res, second_scale, grad_second)
    branch_all = jnp.concatenate(gather_group(grad_res.astype(BF16)), axis=0)

    mlp_out = scatter_group(lambda which: nt(half(hidden, which), wd_t))
    out_home = (hidden_res + mlp_out).astype(BF16)
    output = reorder(send(out_home, to_home))

    def chip_grads(left, right):
        return [tn(left[:, r * wide : (r + 1) * wide], right).astype(BF16) for r in range(chips)]

    up_order, down_order = list(range(bits)), list(reversed(range(bits)))

    def finish(total):
        even, odd = total[:share], total[share:]
        one = send(jnp.where(first, odd, even), collect_one)
        two = send(odd, spread_two)
        return jnp.where(first, even, two).astype(F32) + one.astype(F32)

    split = hidden_width // 2
    gate_sum = finish(scatter_chips(chip_grads(second_all, grad_gate), up_order))
    up_sum = finish(scatter_chips(chip_grads(second_all, grad_up), down_order))
    down_sum = jnp.concatenate(
        [
            finish(scatter_chips(chip_grads(cot_all, hidden[:, :split]), up_order)),
            finish(scatter_chips(chip_grads(cot_all, hidden[:, split:]), down_order)),
        ],
        axis=1,
    )

    grad_mixed = nn(branch_all, wo_t).astype(BF16)
    output_sum = finish(scatter_chips(chip_grads(branch_all, mixed), up_order))
    grad_qkv, grad_bias = attend_back(pos, qkv, bias, seg_row, seg_col, lse, cum, grad_mixed, quarter)
    first_parts = {}

    def first_half(which):
        first_parts[which] = nt(half(grad_qkv, which), full_one)
        return first_parts[which]

    grad_first = scatter_group(first_half)
    gain_one_part = functools.reduce(
        jnp.add, [jnp.sum(half(x_hat, w).astype(F32) * first_parts[w], axis=0) for w in (0, 1)]
    )
    back_home = (grad_res + unit_back(resid, first_scale, grad_first)).astype(BF16)
    input_grad = reorder(send(back_home, to_home)).astype(F32)

    cut = qkv.shape[1] // 2
    qkv_sum = jnp.concatenate(
        [
            finish(scatter_chips(chip_grads(x_hat, grad_qkv[:, :cut]), up_order)),
            finish(scatter_chips(chip_grads(x_hat, grad_qkv[:, cut:]), down_order)),
        ],
        axis=1,
    )
    qkv_sum = qkv_sum * gain_one

    three = 3 * inner_width
    gain_row = full_one[:, three + heads].astype(F32)
    forget_part = tn(grad_qkv[:, three:], x_hat)[:heads] * gain_row[None, :]
    small = jnp.concatenate([forget_part, gain_one_part[None], gain_two_part[None]], axis=0)
    small = reorder(small)
    small = jnp.concatenate([small, jnp.pad(grad_bias[:, :PAIR], ((0, 0), (0, width - PAIR)))], axis=0)
    for bit in range(bits):
        small = small + send(small, over_chip(bit))
    one = send(small, collect_one)
    two = send(small, spread_two)
    small = jnp.where(first, small, two) + one
    grad_forget = small[:heads].T
    grad_bias_out = small[heads + 2, :heads]
    gains = small[heads : heads + 2]
    gains = gains + send(gains, over_z)
    gains = gains + send(gains, lambda d, t: (d, t ^ 2))
    gains = lax.dynamic_slice_in_dim(gains, d * share, share, 1)
    grad_gain_one = gains[0] / attn_gain.astype(F32)
    grad_gain_two = gains[1] / mlp_gain.astype(F32)

    return (
        output,
        input_grad,
        grad_gain_one,
        qkv_sum[:, :inner_width],
        qkv_sum[:, inner_width : 2 * inner_width],
        qkv_sum[:, 2 * inner_width : three],
        grad_forget,
        grad_bias_out,
        output_sum.T,
        grad_gain_two,
        gate_sum * gain_two,
        up_sum * gain_two,
        down_sum.T,
    )


def solution(mesh):
    return jax.shard_map(
        per_device,
        mesh=mesh,
        in_specs=(
            P(("dp", "tensor"), None),
            P("dp"),
            P("dp", "tensor"),
            P("dp", "tensor"),
            P("dp", "tensor"),
            P(None, "tensor"),
            P("tensor"),
            P("tensor", "dp"),
            P("dp"),
            P("dp", "tensor"),
            P("dp", "tensor"),
            P("tensor", "dp"),
            P("dp", None),
            P(("dp", "tensor"), None),
        ),
        out_specs=(
            P(("dp", "tensor"), None),
            P(("dp", "tensor"), None),
            P("dp"),
            P("dp", "tensor"),
            P("dp", "tensor"),
            P("dp", "tensor"),
            P(None, "tensor"),
            P("tensor"),
            P("tensor", "dp"),
            P("dp"),
            P("dp", "tensor"),
            P("dp", "tensor"),
            P("tensor", "dp"),
        ),
        check_vma=False,
    )
```

```python
import functools

import jax
import jax.numpy as jnp
from jax import lax
from jax.experimental import pallas as pl
from jax.experimental.pallas import tpu as pltpu
from jax.sharding import PartitionSpec as P

HEAD = 64
PAIR = 2 * HEAD
EPS = 1e-06
F32 = jnp.float32
BF16 = jnp.bfloat16
NT = (((1,), (1,)), ((), ()))
TN = (((0,), (0,)), ((), ()))
AXES = ("dp", "tensor")


def nn(a, b):
    return jnp.dot(a, b, preferred_element_type=F32)


def nt(a, b):
    return lax.dot_general(a, b, NT, preferred_element_type=F32)


def tn(a, b):
    return lax.dot_general(a, b, TN, preferred_element_type=F32)


class Box:
    def __init__(self, v):
        self.v = v


def val(value):
    return value.v if isinstance(value, Box) else value


def boxes(tree):
    if isinstance(tree, Box):
        return [tree]
    assert isinstance(tree, (list, tuple)), type(tree)
    return [b for item in tree for b in boxes(item)]


def send(value, move):
    tensor = lax.axis_size("tensor")
    pairs = []
    for d in range(lax.axis_size("dp")):
        for t in range(tensor):
            to = move(d, t)
            if to is not None:
                pairs.append((d * tensor + t, to[0] * tensor + to[1]))
    return Box(lax.ppermute(val(value), AXES, pairs))


def to_home(d, t):
    return (d ^ 1, t ^ 2) if (d & 1) != (t >> 1) else (d, t)


def over_core(d, t):
    return (d ^ 1, t)


def over_z(d, t):
    return (d, t ^ 1)


def over_chip(bit):
    return lambda d, t: (d ^ (2 << bit), t)


def over_half(d, t):
    return (d, t ^ 2)


def over_core_half(d, t):
    return (d ^ 1, t ^ 2)


def hold(value, *others):
    held = boxes(others)
    result, new = lax.optimization_barrier((jax.tree.map(val, value, is_leaf=lambda x: isinstance(x, Box)), [b.v for b in held]))
    for b, v in zip(held, new):
        b.v = v
    if isinstance(value, Box):
        value.v = result
        return value
    return result


def meet(critical, *others):
    return hold(hold(critical), *others)


def rows_of(pieces):
    return jnp.concatenate([val(p) for p in pieces], axis=0)


def block_of(pos_ref, at, size):
    return pl.ds(pl.multiple_of(pos_ref[at] * size, size), size)


def lane_of(pair, h):
    return jnp.where(pair == 2, 2 + HEAD * h, HEAD * pair + h)


def pack_kernel(core_ref, query_ref, key_ref, value_ref, forget_ref, gain_ref, bias_ref, mine_ref, other_ref):
    share = gain_ref.shape[1]
    diagonal = lax.broadcasted_iota(jnp.int32, (share, share), 0) == lax.broadcasted_iota(jnp.int32, (share, share), 1)
    gain = jnp.sum(jnp.where(diagonal, gain_ref[...].astype(F32), 0.0), axis=1, keepdims=True)
    lane = lax.broadcasted_iota(jnp.int32, (share, PAIR), 1)
    low_lanes = lane < HEAD
    first = core_ref[0] == 0
    parts = [ref[...].astype(F32) * gain for ref in (query_ref, key_ref, value_ref)]
    forget = forget_ref[...].astype(F32) * gain
    bias = bias_ref[...]
    pieces = []
    for _ in range(3):
        piece = bias.astype(BF16).astype(F32)
        pieces.append(piece)
        bias = bias - piece
    halves = []
    for h in range(2):
        three = [p if h == 0 else pltpu.roll(p, p.shape[1] // 2, 1) for p in parts]
        tiles = [p[:, :PAIR] for p in three]
        lone = [p[:, PAIR : 2 * PAIR] for p in three]
        tiles.append(jnp.where(low_lanes, lone[0], pltpu.roll(lone[1], HEAD, 1)))
        rest = jnp.where(lane < HEAD + 3, pltpu.roll(forget, HEAD - 3 * h, 1), gain)
        for k, piece in enumerate(pieces):
            at = HEAD + 4 + 3 * k
            moved = jnp.broadcast_to(pltpu.roll(piece, at - 3 * h, 1), (share, PAIR))
            rest = jnp.where((lane >= at) & (lane < at + 3), moved, rest)
        rest = jnp.where(lane < HEAD + 13, rest, 0.0)
        tiles.append(jnp.where(low_lanes, lone[2], rest))
        halves.append(tiles)
    for k in range(5):
        at = slice(k * PAIR, (k + 1) * PAIR)
        mine_ref[:, at] = jnp.where(first, halves[0][k], halves[1][k]).astype(BF16)
        other_ref[:, at] = jnp.where(first, halves[1][k], halves[0][k]).astype(BF16)


def forward_kernel(
    quarter, pos_ref, x0_ref, x1_ref, x2_ref, x3_ref, wa_ref, wb_ref, bias_ref, segr_ref, segc_ref,
    mixed_ref, xhat_ref, qkv_ref, logit_ref, lse_ref, cum_ref, cumr_ref, rel_ref,
):
    pair = pl.program_id(0)
    width = 3 * PAIR
    lane = lax.broadcasted_iota(jnp.int32, (quarter, PAIR), 1)
    low_lanes = lane < HEAD
    count = segr_ref.shape[1] // quarter

    @pl.when(pair == 0)
    def _():
        for r, x_ref in enumerate((x0_ref, x1_ref, x2_ref, x3_ref)):
            at = slice(r * quarter, (r + 1) * quarter)
            x = x_ref[...].astype(F32)
            low = (x * lax.rsqrt(jnp.mean(x * x, axis=1, keepdims=True) + EPS)).astype(BF16)
            xhat_ref[at, :] = low
            near_all = nn(low, wa_ref[...])
            far_all = nn(low, wb_ref[...])

            def near(k):
                return near_all[:, k * PAIR : (k + 1) * PAIR]

            def far(k):
                return far_all[:, k * PAIR : (k + 1) * PAIR]

            for k in range(3):
                qkv_ref[at, k * width : k * width + PAIR] = near(k).astype(BF16)
                qkv_ref[at, k * width + PAIR : k * width + 2 * PAIR] = far(k).astype(BF16)

            def both(one, two):
                return jnp.where(low_lanes, one, two).astype(BF16)

            qkv_ref[at, 2 * PAIR : 3 * PAIR] = both(near(3), pltpu.roll(far(3), HEAD, 1))
            qkv_ref[at, width + 2 * PAIR : width + 3 * PAIR] = both(pltpu.roll(near(3), HEAD, 1), far(3))
            qkv_ref[at, 2 * width + 2 * PAIR : 2 * width + 3 * PAIR] = both(near(4), pltpu.roll(far(4), HEAD, 1))
            rel_ref[at, :] = jnp.where(low_lanes, pltpu.roll(near(4), HEAD, 1), far(4)) + bias_ref[...]
        rows = lax.broadcasted_iota(jnp.int32, (quarter, quarter), 0)
        cols = lax.broadcasted_iota(jnp.int32, (quarter, quarter), 1)
        lower = (cols <= rows).astype(F32)
        carry = jnp.zeros((1, PAIR), F32)
        for a in range(count):
            logit = rel_ref[block_of(pos_ref, a, quarter), :]
            here = slice(a * quarter, (a + 1) * quarter)
            logit_ref[here, :] = logit
            logsig = jnp.minimum(logit, 0.0) - jnp.log1p(jnp.exp(-jnp.abs(logit)))
            cum = jnp.dot(lower, logsig, precision=lax.Precision.HIGHEST, preferred_element_type=F32) + carry
            carry = cum[quarter - 1 :, :]
            cum_ref[here, :] = cum
            cumr_ref[:, here] = cum.T
        lse_ref[...] = jnp.zeros(lse_ref.shape, F32)

    def columns(part):
        return pl.ds(pl.multiple_of(part * width + pair * PAIR, PAIR), PAIR)

    diag_rows = lax.broadcasted_iota(jnp.int32, (quarter, quarter), 0)
    diag_cols = lax.broadcasted_iota(jnp.int32, (quarter, quarter), 1)
    for a in range(count):
        query = (qkv_ref[block_of(pos_ref, a, quarter), columns(0)] * 0.125).astype(BF16)
        seg_q = segc_ref[a * quarter : (a + 1) * quarter, :]
        spans = range(max(0, a - 512 // quarter), a + 1)
        outs = []
        for h in range(2):
            head = lane_of(pair, h)
            mine = (lane >= HEAD) if h else low_lanes
            query_h = jnp.where(mine, query, jnp.zeros_like(query))
            scores = []
            for b in spans:
                keys = qkv_ref[block_of(pos_ref, b, quarter), columns(1)]
                s = nt(query_h, keys) - cumr_ref[pl.ds(head, 1), b * quarter : (b + 1) * quarter]
                allowed = seg_q == segr_ref[:, b * quarter : (b + 1) * quarter]
                if a == b:
                    allowed &= diag_cols <= diag_rows
                scores.append(jnp.where(allowed, s, -jnp.inf))
            top = functools.reduce(jnp.maximum, [jnp.max(s, axis=1, keepdims=True) for s in scores])
            expd = [jnp.exp(s - top) for s in scores]
            total = functools.reduce(jnp.add, [jnp.sum(e, axis=1, keepdims=True) for e in expd])
            scale = 1.0 / total
            out = None
            for e, b in zip(expd, spans):
                values = qkv_ref[block_of(pos_ref, b, quarter), columns(2)]
                part = nn((e * scale).astype(BF16), values)
                out = part if out is None else out + part
            outs.append(out)
            lse = top + jnp.log(total)
            at = pl.ds(a * quarter, quarter)
            lse_ref[at, :] = jnp.where(lane == head, lse, lse_ref[at, :])
        mixed_ref[block_of(pos_ref, a, quarter), columns(0)] = jnp.where(low_lanes, outs[0], outs[1]).astype(BF16)


def backward_kernel(
    quarter, pos_ref, qkv_ref, logit_ref, segr_ref, segc_ref, lse_ref, cum_ref, gmix_ref,
    gnear_ref, gfar_ref, gbias_ref, lser_ref, gcol_ref, grow_ref, grad_ref, gk_ref, gv_ref,
):
    pair = pl.program_id(0)
    pairs = pl.num_programs(0)
    width = 3 * PAIR
    lane = lax.broadcasted_iota(jnp.int32, (quarter, PAIR), 1)
    low_lanes = lane < HEAD
    count = segr_ref.shape[1] // quarter

    @pl.when(pair == 0)
    def _():
        for a in range(count):
            at = slice(a * quarter, (a + 1) * quarter)
            lser_ref[:, at] = lse_ref[at, :].T
        gcol_ref[...] = jnp.zeros(gcol_ref.shape, F32)
        grow_ref[...] = jnp.zeros(grow_ref.shape, F32)

    def columns(part):
        return pl.ds(pl.multiple_of(part * width + pair * PAIR, PAIR), PAIR)

    diag_rows = lax.broadcasted_iota(jnp.int32, (quarter, quarter), 0)
    diag_cols = lax.broadcasted_iota(jnp.int32, (quarter, quarter), 1)
    gk_ref[...] = jnp.zeros(gk_ref.shape, F32)
    gv_ref[...] = jnp.zeros(gv_ref.shape, F32)
    for a in range(count):
        here = slice(a * quarter, (a + 1) * quarter)
        query = (qkv_ref[block_of(pos_ref, a, quarter), columns(0)] * 0.125).astype(BF16)
        gout = gmix_ref[block_of(pos_ref, a, quarter), columns(0)]
        seg_q = segr_ref[:, here]
        spans = range(max(0, a - 512 // quarter), a + 1)
        grad_query = None
        for h in range(2):
            head = lane_of(pair, h)
            mine = (lane >= HEAD) if h else low_lanes
            query_h = jnp.where(mine, query, jnp.zeros_like(query))
            gout_h = jnp.where(mine, gout, jnp.zeros_like(gout))
            lse = lser_ref[pl.ds(head, 1), here]
            probs, gprobs = [], []
            inner = None
            for b in spans:
                there = slice(b * quarter, (b + 1) * quarter)
                keys = qkv_ref[block_of(pos_ref, b, quarter), columns(1)]
                values = qkv_ref[block_of(pos_ref, b, quarter), columns(2)]
                cum_k = jnp.sum(jnp.where(lane == head, cum_ref[there, :], 0.0), axis=1, keepdims=True)
                s = nt(keys, query_h) - cum_k
                allowed = segc_ref[there, :] == seg_q
                if a == b:
                    allowed &= diag_rows <= diag_cols
                p = jnp.where(allowed, jnp.exp(s - lse), 0.0)
                g = nt(values, gout_h)
                probs.append(p)
                gprobs.append(g)
                part = jnp.sum(p * g, axis=0, keepdims=True)
                inner = part if inner is None else inner + part
            row_sum = None
            for p, g, b in zip(probs, gprobs, spans):
                there = slice(b * quarter, (b + 1) * quarter)
                keys = (qkv_ref[block_of(pos_ref, b, quarter), columns(1)] * 0.125).astype(BF16)
                keys_h = jnp.where(mine, keys, jnp.zeros_like(keys))
                gs = p * (g - inner)
                part = jnp.sum(gs, axis=0, keepdims=True)
                row_sum = part if row_sum is None else row_sum + part
                col_sum = jnp.sum(gs, axis=1, keepdims=True)
                gcol_ref[there, :] += jnp.where(lane == head, col_sum, 0.0)
                low = gs.astype(BF16)
                gk_ref[there, :] += nn(low, query_h)
                gv_ref[there, :] += nn(p.astype(BF16), gout_h)
                part = tn(low, keys_h)
                grad_query = part if grad_query is None else grad_query + part
            grow_ref[pl.ds(head, 1), here] = row_sum
        grad_ref[block_of(pos_ref, a, quarter), columns(0)] = grad_query
    for a in range(count):
        here = slice(a * quarter, (a + 1) * quarter)
        grad_ref[block_of(pos_ref, a, quarter), columns(1)] = gk_ref[here, :]
        grad_ref[block_of(pos_ref, a, quarter), columns(2)] = gv_ref[here, :]

    @pl.when(pair == pairs - 1)
    def _():
        upper = (diag_cols >= diag_rows).astype(F32)
        carry = jnp.zeros((1, PAIR), F32)
        bias = jnp.zeros((1, PAIR), F32)
        real = (lane % HEAD) < pairs
        for a in reversed(range(count)):
            here = slice(a * quarter, (a + 1) * quarter)
            at = block_of(pos_ref, a, quarter)
            logit = logit_ref[here, :]
            gcum = jnp.where(real, grow_ref[:, here].T - gcol_ref[here, :], 0.0)
            back = jnp.dot(upper, gcum, precision=lax.Precision.HIGHEST, preferred_element_type=F32) + carry
            carry = back[:1, :]
            glogit = jnp.where(real, back * (1.0 / (1.0 + jnp.exp(logit))), 0.0)
            bias = bias + jnp.sum(glogit, axis=0, keepdims=True)

            def grad(part, k):
                return grad_ref[at, part * width + k * PAIR : part * width + (k + 1) * PAIR]

            for k in range(3):
                gnear_ref[at, k * PAIR : (k + 1) * PAIR] = grad(k, 0).astype(BF16)
                gfar_ref[at, k * PAIR : (k + 1) * PAIR] = grad(k, 1).astype(BF16)
            q_last, k_last, v_last = grad(0, 2), grad(1, 2), grad(2, 2)
            k_roll = pltpu.roll(k_last, HEAD, 1)
            gnear_ref[at, 3 * PAIR : 4 * PAIR] = jnp.where(low_lanes, q_last, k_roll).astype(BF16)
            gnear_ref[at, 4 * PAIR :] = jnp.where(low_lanes, v_last, pltpu.roll(glogit, HEAD, 1)).astype(BF16)
            gfar_ref[at, 3 * PAIR : 4 * PAIR] = jnp.where(low_lanes, pltpu.roll(q_last, HEAD, 1), k_last).astype(BF16)
            gfar_ref[at, 4 * PAIR :] = jnp.where(low_lanes, pltpu.roll(v_last, HEAD, 1), glogit).astype(BF16)
        gbias_ref[...] = bias


def full_spec(shape):
    return pl.BlockSpec(shape, lambda *_: (0,) * len(shape))


NO_COST = pl.CostEstimate(flops=0, bytes_accessed=0, transcendentals=0)


def params():
    return pltpu.CompilerParams(vmem_limit_bytes=56 * 2**20, dimension_semantics=("arbitrary",))


def pack_one(core, query, keys, values, forget, gain, bias):
    share = gain.shape[1]
    out = jax.ShapeDtypeStruct((share, 5 * PAIR), BF16)
    return pl.pallas_call(
        pack_kernel,
        grid=(1,),
        out_shape=(out, out),
        in_specs=[
            pl.BlockSpec(memory_space=pltpu.SMEM),
            *(full_spec(w.shape) for w in (query, keys, values, forget, gain, bias)),
        ],
        out_specs=(full_spec(out.shape), full_spec(out.shape)),
        compiler_params=params(),
        cost_estimate=NO_COST,
    )(core, query, keys, values, forget, gain, bias)


def attend(pos, blocks, wa, wb, bias, seg_row, seg_col):
    quarter, wide = blocks[0].shape
    length = 4 * quarter
    width = 3 * PAIR
    small = jax.ShapeDtypeStruct((length, PAIR), F32)
    outs = (
        jax.ShapeDtypeStruct((length, width), BF16),
        jax.ShapeDtypeStruct((length, wide), BF16),
        jax.ShapeDtypeStruct((length, 3 * width), BF16),
        small,
        small,
        small,
    )
    operands = (*blocks, wa, wb, bias, seg_row, seg_col)
    return pl.pallas_call(
        functools.partial(forward_kernel, quarter),
        grid=(3,),
        out_shape=outs,
        in_specs=[pl.BlockSpec(memory_space=pltpu.SMEM), *(full_spec(o.shape) for o in operands)],
        out_specs=tuple(full_spec(o.shape) for o in outs),
        scratch_shapes=[pltpu.VMEM((PAIR, length), F32), pltpu.VMEM((length, PAIR), F32)],
        compiler_params=params(),
        cost_estimate=NO_COST,
    )(pos, *operands)


def feed_kernel(s0_ref, s1_ref, c0_ref, c1_ref, ga_ref, gb_ref, da_ref, db_ref, *refs):
    hidden_ref, grada_ref, gradb_ref, second_ref, cot_ref, back_ref, gain_ref = refs[-7:]
    cut = da_ref.shape[1]
    block = s0_ref.shape[0]
    gain = None
    for i, (s_ref, c_ref) in enumerate(((s0_ref, c0_ref), (s1_ref, c1_ref))):
        at = slice(i * block, (i + 1) * block)
        second_ref[at, :] = s_ref[...]
        cot_ref[at, :] = c_ref[...]
        back = None
        for k, (w_ref, d_ref, grad_ref) in enumerate(((ga_ref, da_ref, grada_ref), (gb_ref, db_ref, gradb_ref))):
            both = nn(s_ref[...], w_ref[...])
            grad_hidden = nn(c_ref[...], d_ref[...]).astype(BF16).astype(F32)
            gate, upper = both[:, :cut], both[:, cut:]
            sigma = 1.0 / (1.0 + jnp.exp(-gate))
            swish = gate * sigma
            hidden_ref[at, k * cut : (k + 1) * cut] = (swish * upper).astype(BF16)
            grad_gate = (grad_hidden * upper * sigma * (1.0 + gate * (1.0 - sigma))).astype(BF16)
            grad_up = (grad_hidden * swish).astype(BF16)
            grad_ref[at, :cut] = grad_gate
            grad_ref[at, cut:] = grad_up
            part = nt(grad_gate, w_ref[:, :cut]) + nt(grad_up, w_ref[:, cut:])
            back = part if back is None else back + part
        back_ref[at, :] = back
        part = jnp.sum(s_ref[...].astype(F32) * back, axis=0, keepdims=True)
        gain = part if gain is None else gain + part
    gain_ref[...] = gain


def feed_tokens(second, cot, weights, which, before=()):
    block, wide = second[0].shape
    cut = weights[2].shape[1]
    operands = (*second, *cot, *weights)
    widths = (2 * cut, 2 * cut, 2 * cut, wide, wide)
    outs = tuple(jax.ShapeDtypeStruct((4 * block, w), BF16) for w in widths)
    outs += (jax.ShapeDtypeStruct((2 * block, wide), F32), jax.ShapeDtypeStruct((1, wide), F32))
    return pl.pallas_call(
        feed_kernel,
        grid=(1,),
        out_shape=outs,
        in_specs=[*(full_spec(o.shape) for o in operands)] + [pl.BlockSpec(memory_space=pl.ANY)] * len(before),
        out_specs=(
            *(pl.BlockSpec((2 * block, w), lambda i: (which, 0)) for w in widths),
            full_spec((2 * block, wide)),
            full_spec((1, wide)),
        ),
        input_output_aliases={len(operands) + k: k for k in range(len(before))},
        compiler_params=params(),
        cost_estimate=NO_COST,
    )(*operands, *before)


def feed_grads_kernel(
    chip_ref, second_ref, cot_ref, hidden_ref, ga_ref, gb_ref, da_ref, db_ref, outb_ref, outd_ref, outa_ref, part_ref,
):
    cut = da_ref.shape[1]
    second, cot = second_ref[...], cot_ref[...]
    outb_ref[...] = tn(second, gb_ref[...]).astype(BF16)
    outd_ref[...] = tn(cot, hidden_ref[:, cut:]).astype(BF16)
    outa_ref[:, : 2 * cut] = tn(second, ga_ref[...]).astype(BF16)
    outa_ref[:, 2 * cut :] = tn(cot, hidden_ref[:, :cut]).astype(BF16)
    part = nt(hidden_ref[:, :cut], da_ref[...]) + nt(hidden_ref[:, cut:], db_ref[...])
    part_ref[...] = part.astype(BF16)


def pairs_apart(rows, chips):
    block = rows.shape[0] // chips
    return rows_of([rows[r * block : (r + 1) * block] for r in (*range(0, chips, 2), *range(1, chips, 2))])


def feed_grads(chip, second, cot, hidden, ga, gb, da, db, chips):
    length, wide = second.shape
    block = wide // chips
    cut = da.shape[1]
    half_of = chips // 2
    if block % PAIR:
        down = tn(cot, hidden).astype(BF16)
        part = nt(hidden[:, :cut], da) + nt(hidden[:, cut:], db)
        own = jnp.concatenate([tn(second, ga).astype(BF16), down[:, :cut]], axis=1)
        own = [lax.dynamic_slice_in_dim(own, (chip[0] ^ r) * block, block, 0) for r in range(chips)]
        return tn(second, gb).astype(BF16), pairs_apart(down[:, cut:], chips), rows_of(own), part.astype(BF16)
    cols = pl.BlockSpec((length, block), lambda r, chip: (0, r))
    rows = pl.BlockSpec((block, cut), lambda r, chip: (r, 0))
    return pl.pallas_call(
        feed_grads_kernel,
        out_shape=(
            jax.ShapeDtypeStruct((wide, 2 * cut), BF16),
            jax.ShapeDtypeStruct((wide, cut), BF16),
            jax.ShapeDtypeStruct((wide, 3 * cut), BF16),
            jax.ShapeDtypeStruct((length, wide), BF16),
        ),
        grid_spec=pltpu.PrefetchScalarGridSpec(
            num_scalar_prefetch=1,
            grid=(chips,),
            in_specs=[cols, cols, *(full_spec(o.shape) for o in (hidden, ga, gb)), rows, rows],
            out_specs=(
                pl.BlockSpec((block, 2 * cut), lambda r, chip: (r, 0)),
                pl.BlockSpec((block, cut), lambda r, chip: ((r % 2) * half_of + r // 2, 0)),
                pl.BlockSpec((block, 3 * cut), lambda r, chip: (r ^ chip[0], 0)),
                pl.BlockSpec((length, block), lambda r, chip: (0, r)),
            ),
        ),
        compiler_params=params(),
        cost_estimate=NO_COST,
    )(chip, second, cot, hidden, ga, gb, da, db)


def first_grads_kernel(x_ref, near_ref, far_ref, outn_ref, outf_ref, gate_ref):
    x = x_ref[...]
    near, far = tn(x, near_ref[...]), tn(x, far_ref[...])
    outn_ref[...] = near.astype(BF16)
    outf_ref[...] = far.astype(BF16)
    gate_ref[:, :PAIR] = near[:, 4 * PAIR :]
    gate_ref[:, PAIR:] = far[:, 4 * PAIR :]


def first_grads(x_hat, near, far, chips):
    length, wide = x_hat.shape
    block = wide // chips
    cols = near.shape[1]
    half_of = chips // 2
    if block % PAIR:
        near, far = tn(x_hat, near), tn(x_hat, far)
        gate = jnp.concatenate([near[:, 4 * PAIR :], far[:, 4 * PAIR :]], axis=1)
        return near.astype(BF16), pairs_apart(far.astype(BF16), chips), gate
    return pl.pallas_call(
        first_grads_kernel,
        grid=(chips,),
        out_shape=(
            jax.ShapeDtypeStruct((wide, cols), BF16),
            jax.ShapeDtypeStruct((wide, cols), BF16),
            jax.ShapeDtypeStruct((wide, 2 * PAIR), F32),
        ),
        in_specs=[pl.BlockSpec((length, block), lambda r: (0, r)), full_spec(near.shape), full_spec(far.shape)],
        out_specs=(
            pl.BlockSpec((block, cols), lambda r: (r, 0)),
            pl.BlockSpec((block, cols), lambda r: ((r % 2) * half_of + r // 2, 0)),
            pl.BlockSpec((block, 2 * PAIR), lambda r: (r, 0)),
        ),
        compiler_params=params(),
        cost_estimate=NO_COST,
    )(x_hat, near, far)


def attend_back(pos, qkv, logit, seg_row, seg_col, lse, cum, grad_mixed, cols, quarter):
    length = qkv.shape[0]
    grads = jax.ShapeDtypeStruct((length, cols), BF16)
    return pl.pallas_call(
        functools.partial(backward_kernel, quarter),
        grid=(3,),
        out_shape=(grads, grads, jax.ShapeDtypeStruct((1, PAIR), F32)),
        in_specs=[
            pl.BlockSpec(memory_space=pltpu.SMEM),
            full_spec(qkv.shape),
            full_spec(logit.shape),
            full_spec(seg_row.shape),
            full_spec(seg_col.shape),
            full_spec(lse.shape),
            full_spec(cum.shape),
            full_spec(grad_mixed.shape),
        ],
        out_specs=(full_spec((length, cols)), full_spec((length, cols)), full_spec((1, PAIR))),
        scratch_shapes=[
            pltpu.VMEM((PAIR, length), F32),
            pltpu.VMEM((length, PAIR), F32),
            pltpu.VMEM((PAIR, length), F32),
            pltpu.VMEM((length, 9 * PAIR), F32),
            pltpu.VMEM((length, PAIR), F32),
            pltpu.VMEM((length, PAIR), F32),
        ],
        compiler_params=params(),
        cost_estimate=NO_COST,
    )(pos, qkv, logit, seg_row, seg_col, lse, cum, grad_mixed)


def unit_rows(value):
    scale = lax.rsqrt(jnp.mean(value * value, axis=-1, keepdims=True) + EPS)
    return value * scale, scale


def unit_back(value, scale, weighted):
    inner = jnp.mean(weighted * value, axis=-1, keepdims=True)
    return scale * weighted - value * (scale * scale * scale) * inner


def per_device(
    block_input, attn_gain, w_query, w_key, w_value, w_forget, forget_bias, w_output,
    mlp_gain, w_gate, w_up, w_down, segment_ids, cotangent,
):
    width = block_input.shape[1]
    quarter = block_input.shape[0]
    heads = w_forget.shape[1]
    share = w_query.shape[0]
    inner = w_output.shape[0]
    hidden_width = w_gate.shape[1]
    chips = lax.axis_size("dp") // 2
    bits = chips.bit_length() - 1
    d = lax.axis_index("dp")
    t = lax.axis_index("tensor")
    core, chip = d & 1, d >> 1
    first = core == 0
    at_home = core == t >> 1
    wide = width // chips
    half_heads = heads // 2

    def pick(one, two):
        return jnp.where(first, val(one), val(two))

    def pick_home(one, two):
        return jnp.where(at_home, val(one), val(two))

    def by_parity(mine, other):
        return pick(rows_of([mine, other]), rows_of([other, mine]))

    def reorder(rows):
        return jnp.concatenate(
            [lax.dynamic_slice_in_dim(rows, (chip ^ r) * wide, wide, 1) for r in range(chips)], axis=1
        )

    def reorder_rows(rows):
        return rows_of([lax.dynamic_slice_in_dim(rows, (chip ^ r) * wide, wide, 0) for r in range(chips)])

    planes = [[2 * k + c for k in range(chips)] for c in (0, 1)]
    up_order, down_order = list(range(bits)), list(reversed(range(bits)))

    class Pack:
        def __init__(self, mine, other):
            self.mine, self.other = mine, other

        def near(self, *others):
            self.near_other = send(hold(self.other, *others) if others else self.other, over_core)
            return self.near_other

        def cross(self, *others):
            mine, other = hold((self.mine, self.other), *others) if others else (self.mine, self.other)
            self.crossed = (send(mine, over_half), send(other, over_core_half))
            return self.crossed

        def near_rows(self):
            return by_parity(self.mine, self.near_other)

        def far_rows(self):
            return by_parity(*self.crossed)

    class Spread:
        def __init__(self, rows, order):
            self.pieces, self.order = {0: rows}, order

        def early(self):
            for bit in self.order:
                self.pieces[1 << bit] = send(self.pieces[0], over_chip(bit))
            return [self.pieces[1 << bit] for bit in self.order]

        def late(self):
            before = set(self.pieces)
            for i, bit in enumerate(self.order):
                passed = sum(1 << b for b in self.order[:i])
                for at in range(1, 1 << bits):
                    if not at & ~passed:
                        self.pieces[at | (1 << bit)] = send(self.pieces[at], over_chip(bit))
            return [v for k, v in self.pieces.items() if k not in before]

        def direct(self):
            for at in range(1, chips):
                self.pieces[at] = send(self.pieces[0], lambda d, t, at=at: (d ^ (2 * at), t))
            return [self.pieces[at] for at in range(1, chips)]

        def whole(self):
            return rows_of([self.pieces[r] for r in range(chips)])

    class Sum:
        def __init__(self, rows, order):
            cut = rows.shape[0] // 2
            self.order = order
            self.keep, self.give = Box(rows[:cut]), Box(rows[cut:])

        def made(self):
            return self.keep, self.give

        def out(self):
            self.got = send(self.give, over_chip(self.order[0]))
            return self.got

        def rest(self):
            rows = self.keep.v.astype(F32) + self.got.v.astype(F32)
            for bit in self.order[1:]:
                if self.order == down_order:
                    cut = rows.shape[0] // 2
                    self.keep, give = Box(rows[:cut]), rows[cut:]
                else:
                    blocks = [rows[k : k + wide] for k in range(0, rows.shape[0], wide)]
                    self.keep, give = Box(rows_of(blocks[0::2])), rows_of(blocks[1::2])
                self.last = send(give.astype(BF16), over_chip(bit))
                if bit != self.order[-1]:
                    rows = self.keep.v + self.last.v.astype(F32)
            return self.last

        def own(self):
            return (self.keep.v + self.last.v.astype(F32)).astype(BF16)

    class Finish:
        def near(self, rows):
            self.mine_near, other = pick(rows[:share], rows[share:]), pick(rows[share:], rows[:share])
            self.here = send(other, over_core)
            return self.here

        def far_one(self, rows):
            mine, other = pick(rows[:share], rows[share:]), pick(rows[share:], rows[:share])
            self.other = Box(other)
            self.same = send(mine, over_half)
            return self.same

        def far_two(self):
            self.cross = send(self.other, over_core_half)
            return self.cross

        def land(self):
            mine = self.mine_near.astype(F32) + self.same.v.astype(F32)
            rest = self.here.v.astype(F32) + self.cross.v.astype(F32)
            return pick(mine, rest), pick(rest, mine)

    gain_one = attn_gain.astype(F32)[:, None]
    gain_two = mlp_gain.astype(F32)[:, None]
    part, fpart = inner // 2, half_heads
    fcut = hidden_width // 2
    lanes = ((0, 0), (0, PAIR - heads))
    forget_own = jnp.pad(lax.dynamic_slice_in_dim(w_forget, d * share, share, 0), lanes)
    one = Pack(
        *pack_one(
            core.astype(jnp.int32)[None], w_query, w_key, w_value, forget_own, attn_gain[None, :],
            jnp.pad(forget_bias[None, :], lanes),
        )
    )
    out_t, down_t = w_output.T, w_down.T
    gate_scaled, up_scaled = ((w.astype(F32) * gain_two).astype(BF16) for w in (w_gate, w_up))

    def halves_of(arrays, size):
        halves = [jnp.concatenate([w[:, h * size : (h + 1) * size] for w in arrays], axis=1) for h in (0, 1)]
        return pick(*halves), pick(*halves[::-1])

    def stay(d, t):
        return (d, t ^ 1) if (d & 1) == (t >> 1) else None

    def move(d, t):
        return (d, t ^ 1) if (d & 1) != (t >> 1) else None

    one_far = one.cross()
    one.near()
    near_one = Spread(one.near_rows(), up_order)
    near_early = near_one.early()
    x_own, cot_own = Box(reorder(block_input)), Box(reorder(cotangent))

    hold(x_own, one_far, near_early)
    x_home = send(x_own, to_home)
    x_stay = send(x_own, stay)
    far_one = Spread(one.far_rows(), down_order)
    far_early = far_one.early()
    near_late = near_one.late()
    wo = Pack(*halves_of([out_t], part))
    feed_pack = Pack(*halves_of([gate_scaled, up_scaled, down_t], fcut))
    gate_pack, down_pack = Pack(*halves_of([gate_scaled, up_scaled], fcut)), Pack(*halves_of([down_t], fcut))

    hold(x_home, x_stay, far_early, near_late)
    x_move = send(x_home, move)
    x_core = send(x_home, over_core)
    far_late = far_one.late()
    wo_far = wo.cross(x_home)
    wo.near(x_home)
    seg_other = send(hold(segment_ids, x_home), over_core)
    feed_pack.near(x_home)
    near_all = Box(
        lax.all_gather(feed_pack.near_rows(), "dp", axis=0, tiled=True, axis_index_groups=planes)
    )
    seg_row = Box(pick_home(segment_ids, seg_other))
    far_bias = far_one.pieces[0][0, 4 * PAIR + HEAD + fpart + 1 :].astype(F32)
    bias_far = far_bias[:fpart] + far_bias[fpart : 2 * fpart] + far_bias[2 * fpart : 3 * fpart]
    spare = jnp.zeros((HEAD - fpart,), F32)
    bias = Box(jnp.concatenate([pick(forget_bias[:fpart], forget_bias[fpart:]), spare, bias_far, spare])[None, :])
    place = (t & 1) + 2 * core
    pos = jnp.stack([((a ^ place) >> 1) | (((a ^ place) & 1) << 1) for a in range(4)]).astype(jnp.int32)
    wa = Box(near_one.whole())

    hold(x_move, wa, bias, seg_row)
    hold(x_move, far_late)
    x_z = Box(pick_home(x_stay, x_move))
    x_both = send(x_z, over_core)
    wb = Box(far_one.whole())
    hold(x_both, wb, x_core)
    hold(x_both, wo_far)
    wo_a, wo_b = wo.near_rows(), wo.far_rows()
    wo_rows = jnp.concatenate([wo_a[:, :PAIR], wo_b[:, :PAIR], wo_a[:, PAIR:], wo_b[:, PAIR:]], axis=1)
    wo_spread = Spread(wo_rows, up_order)
    wo_sent = wo_spread.direct()
    gate_far = gate_pack.cross(x_both)
    qcols = wa.v.shape[1]

    resid = x_home.v.astype(F32)
    first_scale = unit_rows(resid)[1]
    seg_col = seg_row.v.reshape(-1, 1)
    mixed, x_hat, qkv, logit, lse, cum = attend(
        pos, [x_home.v, x_core.v, x_z.v, x_both.v], wa.v, wb.v, bias.v, seg_row.v, seg_col
    )
    mixed = hold(mixed, wo_sent, gate_far)
    wo_t = wo_spread.whole()

    def half(array, which):
        rows = array.shape[0] // 2
        return array[which * rows : (which + 1) * rows]

    order = {}

    def scatter_group(far, near, at_far=lambda far_sum: None, at_near=lambda near_sum: None, late_core=False):
        rows = far()
        far_in = send(rows[quarter:].astype(BF16), over_core)
        far_sum = Box((rows[:quarter].astype(F32) + far_in.v.astype(F32)).astype(BF16))
        at_far(far_sum)
        far_got = send(far_sum, over_z)
        rows = Box(near())
        if late_core:
            hold(rows, far_got)
        near_in = send(rows.v[quarter:].astype(BF16), over_core)
        near_sum = Box(rows.v[:quarter].astype(F32) + near_in.v.astype(F32))
        at_near(near_sum)
        hold(far_got, near_sum)
        return near_sum.v + far_got.v.astype(F32)

    sent = {}

    def weights_on(near_sum):
        sent["gate"] = Spread(gate_pack.far_rows(), up_order)
        sent["gate_sent"] = sent["gate"].direct()

    mixed = Box(mixed)
    hidden_res = Box(
        resid
        + scatter_group(
            lambda: nt(half(mixed.v, 1), wo_t),
            lambda: nt(half(mixed.v, 0), wo_t),
            lambda far_sum: hold(far_sum, mixed),
            weights_on,
        )
    )
    far_gate = sent["gate"]
    second, second_scale = unit_rows(hidden_res.v)
    second_low = Box(second.astype(BF16))
    second_z = send(second_low, over_z)
    down_far = down_pack.cross(second_low)
    second_core = send(second_low, over_core)
    hold(second_core, sent["gate_sent"])
    cot_stay = send(hold(cot_own, second_core), stay)
    hold(second_core, down_far)
    far_down = Spread(down_pack.far_rows(), down_order)
    down_sent = far_down.direct()
    cot_home = send(hold(cot_own, second_core), to_home)
    hold(near_all, second_core)
    gates_a = Box(reorder_rows(near_all.v[:, : 2 * fcut]))
    downs_a = Box(reorder_rows(near_all.v[:, 2 * fcut :]))
    hold(second_z, gates_a, downs_a)
    hold(second_z, cot_home, down_sent, cot_stay)
    second_both = send(second_z, over_core)
    cot_move = send(cot_home, move)
    cot_core = send(cot_home, over_core)
    gates_b, downs_b = Box(far_gate.whole()), Box(far_down.whole())
    hold(cot_move, second_both, gates_b, downs_b)
    cot_z = Box(pick_home(cot_stay, cot_move))
    cot_both = send(cot_z, over_core)
    hold(cot_both, cot_core)

    feed_weights = (gates_a.v, gates_b.v, downs_a.v, downs_b.v)
    made = {}

    def feed_far():
        made["far"] = feed_tokens((second_z.v, second_both.v), (cot_z.v, cot_both.v), feed_weights, 1)
        return made["far"][5]

    def feed_near():
        made["near"] = feed_tokens(
            (second_low.v, second_core.v), (cot_home.v, cot_core.v), feed_weights, 0, made["far"][:5]
        )
        return made["near"][5]

    grad_second = scatter_group(feed_far, feed_near, lambda far_sum: hold(far_sum, second_low, second_core), late_core=True)
    gain_two_part = made["far"][6] + made["near"][6]
    grad_res = Box(cot_home.v.astype(F32) + unit_back(hidden_res.v, second_scale, grad_second))
    branch = Box(grad_res.v.astype(BF16))
    laid = [Box(m) for m in made["near"][:5]]
    hold(branch, laid)
    branch_z = send(branch, over_z)
    hidden, grads_a, grads_b, second_all, cot_all = (m.v for m in laid)
    gb_rows, db_rows, a_rows, mlp_rows = feed_grads(
        chip.astype(jnp.int32)[None], second_all, cot_all, hidden, grads_a, grads_b, downs_a.v, downs_b.v, chips
    )
    gb_rows, db_rows, a_part, mlp_rows = (Box(m) for m in (gb_rows, db_rows, a_rows, mlp_rows))
    hold(branch_z, gb_rows, db_rows, a_part, mlp_rows)
    hold(branch, branch_z)
    branch_both = send(branch_z, over_core)
    branch_core = send(branch, over_core)
    gb, db = Sum(gb_rows.v, down_order), Sum(db_rows.v, up_order)
    b_out = [gb.out(), db.out()]
    branch_all = Box(rows_of([branch, branch_core, branch_z, branch_both]))

    grad_mixed = Box(nn(branch_all.v, wo_t).astype(BF16))
    mlp_out = Box(scatter_group(lambda: half(mlp_rows.v, 1), lambda: half(mlp_rows.v, 0)))
    hold(branch_all, grad_mixed)
    o_sum = Sum(tn(branch_all.v, mixed.v).astype(BF16), down_order)
    o_out = o_sum.out()
    hold(grad_mixed, o_sum.keep)
    grad_near, grad_far, grad_bias = attend_back(
        pos, qkv, logit, seg_row.v, seg_col, lse, cum, grad_mixed.v, qcols, quarter
    )
    grad_near, grad_far = Box(grad_near), Box(grad_far)
    hold(grad_near, grad_far, b_out, mlp_out)
    out_home = (hidden_res.v + mlp_out.v).astype(BF16)
    out_sent = send(out_home, to_home)
    b_late = [gb.rest(), db.rest()]
    hold(a_part, mlp_out)
    a_own = Box(
        lax.psum_scatter(a_part.v, "dp", scatter_dimension=0, tiled=True, axis_index_groups=planes)
    )
    first_parts = {}

    def first_part(which):
        first_parts[which] = nt(half(grad_near.v, which), wa.v) + nt(half(grad_far.v, which), wb.v)
        return first_parts[which]

    x_hat = Box(x_hat)

    def first_rest(near_sum):
        hold(near_sum, x_hat)
        grads = [Box(g) for g in first_grads(x_hat.v, grad_near.v, grad_far.v, chips)]
        made["qa"], made["qb"] = Sum(grads[0].v, down_order), Sum(grads[1].v, up_order)
        made["q_out"] = [made["qa"].out(), made["qb"].out()]
        made["gate"] = grads[2]
        hold(near_sum, grads[2])

    grad_first = scatter_group(
        lambda: first_part(1), lambda: first_part(0), lambda far_sum: hold(far_sum, grad_near, grad_far, x_hat), first_rest
    )
    qa, qb, gate_cols = made["qa"], made["qb"], made["gate"]
    back_home = Box((grad_res.v + unit_back(resid, first_scale, grad_first)).astype(BF16))
    hold(back_home, b_late, out_sent)
    back_sent = send(back_home, to_home)
    feed_end = Finish()
    b_same = feed_end.far_one(jnp.concatenate([gb.own(), db.own()], axis=1))
    hold(gate_cols, back_home)
    forget = jnp.concatenate([gate_cols.v[:, k * PAIR + HEAD : k * PAIR + HEAD + fpart] for k in (0, 1)], axis=1).T
    gain_part = functools.reduce(
        jnp.add, [jnp.sum(half(x_hat.v, w).astype(F32) * first_parts[w], axis=0) for w in (0, 1)]
    )
    gain_row = wa.v[:, 3 * part + fpart].astype(F32)
    small = reorder(jnp.concatenate([forget * gain_row[None, :], gain_part[None], gain_two_part], axis=0))
    small = Box(jnp.concatenate([small, jnp.pad(grad_bias, ((0, 0), (0, width - PAIR)))], axis=0))
    small_there = send(small, over_chip(0))
    hold(small, made["q_out"], small_there, o_out)
    q_late = [qa.rest(), qb.rest()]
    o_late = o_sum.rest()
    hold(feed_end.other, small)
    b_cross = feed_end.far_two()
    small = Box(small.v + small_there.v)
    hold(small, q_late, o_late)
    for bit in range(1, bits):
        small = Box(small.v + send(small, over_chip(bit)).v)
    near, far = small.v[:fpart], small.v[fpart:heads]
    gains, bias_sum = small.v[heads : heads + 2], small.v[heads + 2 :]
    spread_out = ((0, 0), (0, width - fpart))
    bias_near, bias_far = (jnp.pad(bias_sum[:, k * HEAD : k * HEAD + fpart], spread_out) for k in (0, 1))
    got = send(jnp.concatenate([far, bias_far, gains], axis=0), over_half)
    hold(a_own, q_late)
    feed_end.near(a_own.v)

    own_out = o_sum.own()
    out_halves = [
        jnp.concatenate(
            [own_out[:, h * PAIR : (h + 1) * PAIR], own_out[:, 2 * PAIR + h * HEAD : 2 * PAIR + (h + 1) * HEAD]], axis=1
        )
        for h in (0, 1)
    ]
    q_end = Finish()
    q_same = q_end.far_one(jnp.concatenate([qb.own(), out_halves[1]], axis=1))
    q_cross = q_end.far_two()
    q_here = q_end.near(jnp.concatenate([qa.own(), out_halves[0]], axis=1))
    hold(got, q_here, back_sent, b_same, b_cross)
    mine = jnp.concatenate(
        [near + got.v[:fpart], bias_near + got.v[fpart : fpart + 1], gains + got.v[fpart + 1 :]], axis=0
    )
    rest = send(mine, over_core).v
    grad_forget = pick(rows_of([mine[:fpart], rest[:fpart]]), rows_of([rest[:fpart], mine[:fpart]])).T
    bias_mine, bias_rest = mine[fpart, :fpart], rest[fpart, :fpart]
    grad_bias_out = pick(jnp.concatenate([bias_mine, bias_rest]), jnp.concatenate([bias_rest, bias_mine]))
    gains = mine[fpart + 1 :] + rest[fpart + 1 :]
    gains = lax.dynamic_slice_in_dim(gains, d * share, share, 1)
    gains = Box(gains + send(gains, over_z).v)
    hold(gains, q_same, q_cross)
    gains = gains.v
    grad_gain_one = gains[0] / attn_gain.astype(F32)
    grad_gain_two = gains[1] / mlp_gain.astype(F32)
    f_zero, f_one = feed_end.land()
    gate_sum, up_sum, down_sum = (
        jnp.concatenate([f[:, k * fcut : (k + 1) * fcut] for f in (f_zero, f_one)], axis=1) for k in range(3)
    )
    input_grad = reorder(back_sent.v).astype(F32)
    output = reorder(out_sent.v)
    q_zero, q_one = q_end.land()

    def joined(k):
        if k == 3:
            return jnp.concatenate([q_zero[:, qcols:], q_one[:, qcols:]], axis=1)
        lone = slice(3 * PAIR + k * HEAD, 3 * PAIR + (k + 1) * HEAD)
        pair = slice(k * PAIR, (k + 1) * PAIR)
        return jnp.concatenate([q_zero[:, pair], q_zero[:, lone], q_one[:, pair], q_one[:, lone]], axis=1)

    q_sums = [joined(k) for k in range(4)]

    return (
        output,
        input_grad,
        grad_gain_one,
        q_sums[0] * gain_one,
        q_sums[1] * gain_one,
        q_sums[2] * gain_one,
        grad_forget,
        grad_bias_out,
        q_sums[3].T,
        grad_gain_two,
        gate_sum * gain_two,
        up_sum * gain_two,
        down_sum.T,
    )


def solution(mesh):
    return jax.shard_map(
        per_device,
        mesh=mesh,
        in_specs=(
            P(("dp", "tensor"), None),
            P("dp"),
            P("dp", "tensor"),
            P("dp", "tensor"),
            P("dp", "tensor"),
            P(None, "tensor"),
            P("tensor"),
            P("tensor", "dp"),
            P("dp"),
            P("dp", "tensor"),
            P("dp", "tensor"),
            P("tensor", "dp"),
            P("dp", None),
            P(("dp", "tensor"), None),
        ),
        out_specs=(
            P(("dp", "tensor"), None),
            P(("dp", "tensor"), None),
            P("dp"),
            P("dp", "tensor"),
            P("dp", "tensor"),
            P("dp", "tensor"),
            P(None, "tensor"),
            P("tensor"),
            P("tensor", "dp"),
            P("dp"),
            P("dp", "tensor"),
            P("dp", "tensor"),
            P("tensor", "dp"),
        ),
        check_vma=False,
    )
```

```python
import functools

import jax
import jax.numpy as jnp
from jax import lax
from jax.experimental import pallas as pl
from jax.experimental.pallas import tpu as pltpu
from jax.sharding import PartitionSpec as P

HEAD = 64
PAIR = 2 * HEAD
EPS = 1e-06
F32 = jnp.float32
BF16 = jnp.bfloat16
NT = (((1,), (1,)), ((), ()))
TN = (((0,), (0,)), ((), ()))
AXES = ("dp", "tensor")


def nn(a, b):
    return jnp.dot(a, b, preferred_element_type=F32)


def nt(a, b):
    return lax.dot_general(a, b, NT, preferred_element_type=F32)


def tn(a, b):
    return lax.dot_general(a, b, TN, preferred_element_type=F32)


class Box:
    def __init__(self, v):
        self.v = v


def val(value):
    return value.v if isinstance(value, Box) else value


def boxes(tree):
    if isinstance(tree, Box):
        return [tree]
    assert isinstance(tree, (list, tuple)), type(tree)
    return [b for item in tree for b in boxes(item)]


def send(value, move):
    tensor = lax.axis_size("tensor")
    pairs = []
    for d in range(lax.axis_size("dp")):
        for t in range(tensor):
            to = move(d, t)
            if to is not None:
                pairs.append((d * tensor + t, to[0] * tensor + to[1]))
    return Box(lax.ppermute(val(value), AXES, pairs))


def to_home(d, t):
    return (d ^ 1, t ^ 2) if (d & 1) != (t >> 1) else (d, t)


def swap_home(d, t):
    return (d ^ 1, t ^ 2) if (d & 1) != (t >> 1) else None


def over_core(d, t):
    return (d ^ 1, t)


def over_z(d, t):
    return (d, t ^ 1)


def over_chip(bit):
    return lambda d, t: (d ^ (2 << bit), t)


def over_half(d, t):
    return (d, t ^ 2)


def over_core_half(d, t):
    return (d ^ 1, t ^ 2)


def hold(value, *others):
    held = boxes(others)
    result, new = lax.optimization_barrier((jax.tree.map(val, value, is_leaf=lambda x: isinstance(x, Box)), [b.v for b in held]))
    for b, v in zip(held, new):
        b.v = v
    if isinstance(value, Box):
        value.v = result
        return value
    return result


def meet(critical, *others):
    return hold(hold(critical), *others)


def rows_of(pieces):
    return jnp.concatenate([val(p) for p in pieces], axis=0)


def block_of(pos_ref, at, size):
    return pl.ds(pl.multiple_of(pos_ref[at] * size, size), size)


def lane_of(pair, h):
    return jnp.where(pair == 2, 2 + HEAD * h, HEAD * pair + h)


def pack_kernel(core_ref, query_ref, key_ref, value_ref, forget_ref, gain_ref, bias_ref, mine_ref, other_ref):
    share = gain_ref.shape[1]
    diagonal = lax.broadcasted_iota(jnp.int32, (share, share), 0) == lax.broadcasted_iota(jnp.int32, (share, share), 1)
    gain = jnp.sum(jnp.where(diagonal, gain_ref[...].astype(F32), 0.0), axis=1, keepdims=True)
    lane = lax.broadcasted_iota(jnp.int32, (share, PAIR), 1)
    low_lanes = lane < HEAD
    first = core_ref[0] == 0
    parts = [ref[...].astype(F32) * gain for ref in (query_ref, key_ref, value_ref)]
    forget = forget_ref[...].astype(F32) * gain
    bias = bias_ref[...]
    pieces = []
    for _ in range(3):
        piece = bias.astype(BF16).astype(F32)
        pieces.append(piece)
        bias = bias - piece
    halves = []
    for h in range(2):
        three = [p if h == 0 else pltpu.roll(p, p.shape[1] // 2, 1) for p in parts]
        tiles = [p[:, :PAIR] for p in three]
        lone = [p[:, PAIR : 2 * PAIR] for p in three]
        tiles.append(jnp.where(low_lanes, lone[0], pltpu.roll(lone[1], HEAD, 1)))
        rest = jnp.where(lane < HEAD + 3, pltpu.roll(forget, HEAD - 3 * h, 1), gain)
        for k, piece in enumerate(pieces):
            at = HEAD + 4 + 3 * k
            moved = jnp.broadcast_to(pltpu.roll(piece, at - 3 * h, 1), (share, PAIR))
            rest = jnp.where((lane >= at) & (lane < at + 3), moved, rest)
        rest = jnp.where(lane < HEAD + 13, rest, 0.0)
        tiles.append(jnp.where(low_lanes, lone[2], rest))
        halves.append(tiles)
    for k in range(5):
        at = slice(k * PAIR, (k + 1) * PAIR)
        mine_ref[:, at] = jnp.where(first, halves[0][k], halves[1][k]).astype(BF16)
        other_ref[:, at] = jnp.where(first, halves[1][k], halves[0][k]).astype(BF16)


def forward_kernel(
    quarter, pos_ref, x0_ref, x1_ref, x2_ref, x3_ref, wa_ref, wb_ref, bias_ref, segr_ref, segc_ref,
    mixed_ref, xhat_ref, qkv_ref, logit_ref, lse_ref, cum_ref, cumr_ref, rel_ref,
):
    pair = pl.program_id(0)
    width = 3 * PAIR
    lane = lax.broadcasted_iota(jnp.int32, (quarter, PAIR), 1)
    low_lanes = lane < HEAD
    count = segr_ref.shape[1] // quarter

    @pl.when(pair == 0)
    def _():
        for r, x_ref in enumerate((x0_ref, x1_ref, x2_ref, x3_ref)):
            at = slice(r * quarter, (r + 1) * quarter)
            x = x_ref[...].astype(F32)
            low = (x * lax.rsqrt(jnp.mean(x * x, axis=1, keepdims=True) + EPS)).astype(BF16)
            xhat_ref[at, :] = low
            near_all = nn(low, wa_ref[...])
            far_all = nn(low, wb_ref[...])

            def near(k):
                return near_all[:, k * PAIR : (k + 1) * PAIR]

            def far(k):
                return far_all[:, k * PAIR : (k + 1) * PAIR]

            for k in range(3):
                qkv_ref[at, k * width : k * width + PAIR] = near(k).astype(BF16)
                qkv_ref[at, k * width + PAIR : k * width + 2 * PAIR] = far(k).astype(BF16)

            def both(one, two):
                return jnp.where(low_lanes, one, two).astype(BF16)

            qkv_ref[at, 2 * PAIR : 3 * PAIR] = both(near(3), pltpu.roll(far(3), HEAD, 1))
            qkv_ref[at, width + 2 * PAIR : width + 3 * PAIR] = both(pltpu.roll(near(3), HEAD, 1), far(3))
            qkv_ref[at, 2 * width + 2 * PAIR : 2 * width + 3 * PAIR] = both(near(4), pltpu.roll(far(4), HEAD, 1))
            rel_ref[at, :] = jnp.where(low_lanes, pltpu.roll(near(4), HEAD, 1), far(4)) + bias_ref[...]
        rows = lax.broadcasted_iota(jnp.int32, (quarter, quarter), 0)
        cols = lax.broadcasted_iota(jnp.int32, (quarter, quarter), 1)
        lower = (cols <= rows).astype(F32)
        carry = jnp.zeros((1, PAIR), F32)
        for a in range(count):
            logit = rel_ref[block_of(pos_ref, a, quarter), :]
            here = slice(a * quarter, (a + 1) * quarter)
            logit_ref[here, :] = logit
            logsig = jnp.minimum(logit, 0.0) - jnp.log1p(jnp.exp(-jnp.abs(logit)))
            cum = jnp.dot(lower, logsig, precision=lax.Precision.HIGHEST, preferred_element_type=F32) + carry
            carry = cum[quarter - 1 :, :]
            cum_ref[here, :] = cum
            cumr_ref[:, here] = cum.T
        lse_ref[...] = jnp.zeros(lse_ref.shape, F32)

    def columns(part):
        return pl.ds(pl.multiple_of(part * width + pair * PAIR, PAIR), PAIR)

    diag_rows = lax.broadcasted_iota(jnp.int32, (quarter, quarter), 0)
    diag_cols = lax.broadcasted_iota(jnp.int32, (quarter, quarter), 1)
    for a in range(count):
        query = (qkv_ref[block_of(pos_ref, a, quarter), columns(0)] * 0.125).astype(BF16)
        seg_q = segc_ref[a * quarter : (a + 1) * quarter, :]
        spans = range(max(0, a - 512 // quarter), a + 1)
        outs = []
        for h in range(2):
            head = lane_of(pair, h)
            mine = (lane >= HEAD) if h else low_lanes
            query_h = jnp.where(mine, query, jnp.zeros_like(query))
            scores = []
            for b in spans:
                keys = qkv_ref[block_of(pos_ref, b, quarter), columns(1)]
                s = nt(query_h, keys) - cumr_ref[pl.ds(head, 1), b * quarter : (b + 1) * quarter]
                allowed = seg_q == segr_ref[:, b * quarter : (b + 1) * quarter]
                if a == b:
                    allowed &= diag_cols <= diag_rows
                scores.append(jnp.where(allowed, s, -jnp.inf))
            top = functools.reduce(jnp.maximum, [jnp.max(s, axis=1, keepdims=True) for s in scores])
            expd = [jnp.exp(s - top) for s in scores]
            total = functools.reduce(jnp.add, [jnp.sum(e, axis=1, keepdims=True) for e in expd])
            scale = 1.0 / total
            out = None
            for e, b in zip(expd, spans):
                values = qkv_ref[block_of(pos_ref, b, quarter), columns(2)]
                part = nn((e * scale).astype(BF16), values)
                out = part if out is None else out + part
            outs.append(out)
            lse = top + jnp.log(total)
            at = pl.ds(a * quarter, quarter)
            lse_ref[at, :] = jnp.where(lane == head, lse, lse_ref[at, :])
        mixed_ref[block_of(pos_ref, a, quarter), columns(0)] = jnp.where(low_lanes, outs[0], outs[1]).astype(BF16)


def backward_kernel(
    quarter, pos_ref, qkv_ref, logit_ref, segr_ref, segc_ref, lse_ref, cum_ref, gmix_ref,
    gnear_ref, gfar_ref, gbias_ref, lser_ref, gcol_ref, grow_ref, grad_ref, gk_ref, gv_ref,
):
    pair = pl.program_id(0)
    pairs = pl.num_programs(0)
    width = 3 * PAIR
    lane = lax.broadcasted_iota(jnp.int32, (quarter, PAIR), 1)
    low_lanes = lane < HEAD
    count = segr_ref.shape[1] // quarter

    @pl.when(pair == 0)
    def _():
        for a in range(count):
            at = slice(a * quarter, (a + 1) * quarter)
            lser_ref[:, at] = lse_ref[at, :].T
        gcol_ref[...] = jnp.zeros(gcol_ref.shape, F32)
        grow_ref[...] = jnp.zeros(grow_ref.shape, F32)

    def columns(part):
        return pl.ds(pl.multiple_of(part * width + pair * PAIR, PAIR), PAIR)

    diag_rows = lax.broadcasted_iota(jnp.int32, (quarter, quarter), 0)
    diag_cols = lax.broadcasted_iota(jnp.int32, (quarter, quarter), 1)
    gk_ref[...] = jnp.zeros(gk_ref.shape, F32)
    gv_ref[...] = jnp.zeros(gv_ref.shape, F32)
    for a in range(count):
        here = slice(a * quarter, (a + 1) * quarter)
        query = (qkv_ref[block_of(pos_ref, a, quarter), columns(0)] * 0.125).astype(BF16)
        gout = gmix_ref[block_of(pos_ref, a, quarter), columns(0)]
        seg_q = segr_ref[:, here]
        spans = range(max(0, a - 512 // quarter), a + 1)
        grad_query = None
        for h in range(2):
            head = lane_of(pair, h)
            mine = (lane >= HEAD) if h else low_lanes
            query_h = jnp.where(mine, query, jnp.zeros_like(query))
            gout_h = jnp.where(mine, gout, jnp.zeros_like(gout))
            lse = lser_ref[pl.ds(head, 1), here]
            probs, gprobs = [], []
            inner = None
            for b in spans:
                there = slice(b * quarter, (b + 1) * quarter)
                keys = qkv_ref[block_of(pos_ref, b, quarter), columns(1)]
                values = qkv_ref[block_of(pos_ref, b, quarter), columns(2)]
                cum_k = jnp.sum(jnp.where(lane == head, cum_ref[there, :], 0.0), axis=1, keepdims=True)
                s = nt(keys, query_h) - cum_k
                allowed = segc_ref[there, :] == seg_q
                if a == b:
                    allowed &= diag_rows <= diag_cols
                p = jnp.where(allowed, jnp.exp(s - lse), 0.0)
                g = nt(values, gout_h)
                probs.append(p)
                gprobs.append(g)
                part = jnp.sum(p * g, axis=0, keepdims=True)
                inner = part if inner is None else inner + part
            row_sum = None
            for p, g, b in zip(probs, gprobs, spans):
                there = slice(b * quarter, (b + 1) * quarter)
                keys = (qkv_ref[block_of(pos_ref, b, quarter), columns(1)] * 0.125).astype(BF16)
                keys_h = jnp.where(mine, keys, jnp.zeros_like(keys))
                gs = p * (g - inner)
                part = jnp.sum(gs, axis=0, keepdims=True)
                row_sum = part if row_sum is None else row_sum + part
                col_sum = jnp.sum(gs, axis=1, keepdims=True)
                gcol_ref[there, :] += jnp.where(lane == head, col_sum, 0.0)
                low = gs.astype(BF16)
                gk_ref[there, :] += nn(low, query_h)
                gv_ref[there, :] += nn(p.astype(BF16), gout_h)
                part = tn(low, keys_h)
                grad_query = part if grad_query is None else grad_query + part
            grow_ref[pl.ds(head, 1), here] = row_sum
        grad_ref[block_of(pos_ref, a, quarter), columns(0)] = grad_query
    for a in range(count):
        here = slice(a * quarter, (a + 1) * quarter)
        grad_ref[block_of(pos_ref, a, quarter), columns(1)] = gk_ref[here, :]
        grad_ref[block_of(pos_ref, a, quarter), columns(2)] = gv_ref[here, :]

    @pl.when(pair == pairs - 1)
    def _():
        upper = (diag_cols >= diag_rows).astype(F32)
        carry = jnp.zeros((1, PAIR), F32)
        bias = jnp.zeros((1, PAIR), F32)
        real = (lane % HEAD) < pairs
        for a in reversed(range(count)):
            here = slice(a * quarter, (a + 1) * quarter)
            at = block_of(pos_ref, a, quarter)
            logit = logit_ref[here, :]
            gcum = jnp.where(real, grow_ref[:, here].T - gcol_ref[here, :], 0.0)
            back = jnp.dot(upper, gcum, precision=lax.Precision.HIGHEST, preferred_element_type=F32) + carry
            carry = back[:1, :]
            glogit = jnp.where(real, back * (1.0 / (1.0 + jnp.exp(logit))), 0.0)
            bias = bias + jnp.sum(glogit, axis=0, keepdims=True)

            def grad(part, k):
                return grad_ref[at, part * width + k * PAIR : part * width + (k + 1) * PAIR]

            for k in range(3):
                gnear_ref[at, k * PAIR : (k + 1) * PAIR] = grad(k, 0).astype(BF16)
                gfar_ref[at, k * PAIR : (k + 1) * PAIR] = grad(k, 1).astype(BF16)
            q_last, k_last, v_last = grad(0, 2), grad(1, 2), grad(2, 2)
            k_roll = pltpu.roll(k_last, HEAD, 1)
            gnear_ref[at, 3 * PAIR : 4 * PAIR] = jnp.where(low_lanes, q_last, k_roll).astype(BF16)
            gnear_ref[at, 4 * PAIR :] = jnp.where(low_lanes, v_last, pltpu.roll(glogit, HEAD, 1)).astype(BF16)
            gfar_ref[at, 3 * PAIR : 4 * PAIR] = jnp.where(low_lanes, pltpu.roll(q_last, HEAD, 1), k_last).astype(BF16)
            gfar_ref[at, 4 * PAIR :] = jnp.where(low_lanes, pltpu.roll(v_last, HEAD, 1), glogit).astype(BF16)
        gbias_ref[...] = bias


def full_spec(shape):
    return pl.BlockSpec(shape, lambda *_: (0,) * len(shape))


NO_COST = pl.CostEstimate(flops=0, bytes_accessed=0, transcendentals=0)


def params():
    return pltpu.CompilerParams(vmem_limit_bytes=56 * 2**20, dimension_semantics=("arbitrary",))


def pack_one(core, query, keys, values, forget, gain, bias):
    share = gain.shape[1]
    out = jax.ShapeDtypeStruct((share, 5 * PAIR), BF16)
    return pl.pallas_call(
        pack_kernel,
        grid=(1,),
        out_shape=(out, out),
        in_specs=[
            pl.BlockSpec(memory_space=pltpu.SMEM),
            *(full_spec(w.shape) for w in (query, keys, values, forget, gain, bias)),
        ],
        out_specs=(full_spec(out.shape), full_spec(out.shape)),
        compiler_params=params(),
        cost_estimate=NO_COST,
    )(core, query, keys, values, forget, gain, bias)


def attend(pos, blocks, wa, wb, bias, seg_row, seg_col):
    quarter, wide = blocks[0].shape
    length = 4 * quarter
    width = 3 * PAIR
    small = jax.ShapeDtypeStruct((length, PAIR), F32)
    outs = (
        jax.ShapeDtypeStruct((length, width), BF16),
        jax.ShapeDtypeStruct((length, wide), BF16),
        jax.ShapeDtypeStruct((length, 3 * width), BF16),
        small,
        small,
        small,
    )
    operands = (*blocks, wa, wb, bias, seg_row, seg_col)
    return pl.pallas_call(
        functools.partial(forward_kernel, quarter),
        grid=(3,),
        out_shape=outs,
        in_specs=[pl.BlockSpec(memory_space=pltpu.SMEM), *(full_spec(o.shape) for o in operands)],
        out_specs=tuple(full_spec(o.shape) for o in outs),
        scratch_shapes=[pltpu.VMEM((PAIR, length), F32), pltpu.VMEM((length, PAIR), F32)],
        compiler_params=params(),
        cost_estimate=NO_COST,
    )(pos, *operands)


def feed_kernel(s0_ref, s1_ref, c0_ref, c1_ref, ga_ref, gb_ref, da_ref, db_ref, *refs):
    hidden_ref, grada_ref, gradb_ref, second_ref, cot_ref, back_ref, gain_ref = refs[-7:]
    cut = da_ref.shape[1]
    block = s0_ref.shape[0]
    gain = None
    for i, (s_ref, c_ref) in enumerate(((s0_ref, c0_ref), (s1_ref, c1_ref))):
        at = slice(i * block, (i + 1) * block)
        second_ref[at, :] = s_ref[...]
        cot_ref[at, :] = c_ref[...]
        back = None
        for k, (w_ref, d_ref, grad_ref) in enumerate(((ga_ref, da_ref, grada_ref), (gb_ref, db_ref, gradb_ref))):
            both = nn(s_ref[...], w_ref[...])
            grad_hidden = nn(c_ref[...], d_ref[...]).astype(BF16).astype(F32)
            gate, upper = both[:, :cut], both[:, cut:]
            sigma = 1.0 / (1.0 + jnp.exp(-gate))
            swish = gate * sigma
            hidden_ref[at, k * cut : (k + 1) * cut] = (swish * upper).astype(BF16)
            grad_gate = (grad_hidden * upper * sigma * (1.0 + gate * (1.0 - sigma))).astype(BF16)
            grad_up = (grad_hidden * swish).astype(BF16)
            grad_ref[at, :cut] = grad_gate
            grad_ref[at, cut:] = grad_up
            part = nt(grad_gate, w_ref[:, :cut]) + nt(grad_up, w_ref[:, cut:])
            back = part if back is None else back + part
        back_ref[at, :] = back
        part = jnp.sum(s_ref[...].astype(F32) * back, axis=0, keepdims=True)
        gain = part if gain is None else gain + part
    gain_ref[...] = gain


def feed_tokens(second, cot, weights, which, before=()):
    block, wide = second[0].shape
    cut = weights[2].shape[1]
    operands = (*second, *cot, *weights)
    widths = (2 * cut, 2 * cut, 2 * cut, wide, wide)
    outs = tuple(jax.ShapeDtypeStruct((4 * block, w), BF16) for w in widths)
    outs += (jax.ShapeDtypeStruct((2 * block, wide), F32), jax.ShapeDtypeStruct((1, wide), F32))
    return pl.pallas_call(
        feed_kernel,
        grid=(1,),
        out_shape=outs,
        in_specs=[*(full_spec(o.shape) for o in operands)] + [pl.BlockSpec(memory_space=pl.ANY)] * len(before),
        out_specs=(
            *(pl.BlockSpec((2 * block, w), lambda i: (which, 0)) for w in widths),
            full_spec((2 * block, wide)),
            full_spec((1, wide)),
        ),
        input_output_aliases={len(operands) + k: k for k in range(len(before))},
        compiler_params=params(),
        cost_estimate=NO_COST,
    )(*operands, *before)


def put_half(rows, keep_ref, give_ref):
    first = pl.program_id(0) < pl.num_programs(0) // 2

    @pl.when(first)
    def _():
        keep_ref[...] = rows.astype(BF16)

    @pl.when(jnp.logical_not(first))
    def _():
        give_ref[...] = rows.astype(BF16)


def put_pair(rows, keep_ref, give_ref):
    even = pl.program_id(0) % 2 == 0

    @pl.when(even)
    def _():
        keep_ref[...] = rows.astype(BF16)

    @pl.when(jnp.logical_not(even))
    def _():
        give_ref[...] = rows.astype(BF16)


def half_specs(block, cols, half_of):
    return (
        pl.BlockSpec((block, cols), lambda r, *_: (jnp.minimum(r, half_of - 1), 0)),
        pl.BlockSpec((block, cols), lambda r, *_: (jnp.maximum(r - half_of, 0), 0)),
    )


def pair_specs(block, cols):
    return (pl.BlockSpec((block, cols), lambda r, *_: (r // 2, 0)),) * 2


def feed_grads_kernel(
    chip_ref, second_ref, cot_ref, hidden_ref, ga_ref, gb_ref, da_ref, db_ref,
    keepb_ref, giveb_ref, keepd_ref, gived_ref, outa_ref, part_ref,
):
    cut = da_ref.shape[1]
    second, cot = second_ref[...], cot_ref[...]
    put_half(tn(second, gb_ref[...]), keepb_ref, giveb_ref)
    put_pair(tn(cot, hidden_ref[:, cut:]), keepd_ref, gived_ref)
    outa_ref[:, : 2 * cut] = tn(second, ga_ref[...]).astype(BF16)
    outa_ref[:, 2 * cut :] = tn(cot, hidden_ref[:, :cut]).astype(BF16)
    part = nt(hidden_ref[:, :cut], da_ref[...]) + nt(hidden_ref[:, cut:], db_ref[...])
    part_ref[...] = part.astype(BF16)


def pairs_apart(rows, chips):
    block = rows.shape[0] // chips
    return rows_of([rows[r * block : (r + 1) * block] for r in (*range(0, chips, 2), *range(1, chips, 2))])


def halves_apart(rows):
    cut = rows.shape[0] // 2
    return rows[:cut], rows[cut:]


def feed_grads(chip, second, cot, hidden, ga, gb, da, db, chips):
    length, wide = second.shape
    block = wide // chips
    cut = da.shape[1]
    half_of = chips // 2
    if block % PAIR:
        down = tn(cot, hidden).astype(BF16)
        part = nt(hidden[:, :cut], da) + nt(hidden[:, cut:], db)
        own = jnp.concatenate([tn(second, ga).astype(BF16), down[:, :cut]], axis=1)
        own = [lax.dynamic_slice_in_dim(own, (chip[0] ^ r) * block, block, 0) for r in range(chips)]
        halves = halves_apart(tn(second, gb).astype(BF16)) + halves_apart(pairs_apart(down[:, cut:], chips))
        return *halves, rows_of(own), part.astype(BF16)
    cols = pl.BlockSpec((length, block), lambda r, chip: (0, r))
    rows = pl.BlockSpec((block, cut), lambda r, chip: (r, 0))
    return pl.pallas_call(
        feed_grads_kernel,
        out_shape=(
            *(jax.ShapeDtypeStruct((wide // 2, 2 * cut), BF16),) * 2,
            *(jax.ShapeDtypeStruct((wide // 2, cut), BF16),) * 2,
            jax.ShapeDtypeStruct((wide, 3 * cut), BF16),
            jax.ShapeDtypeStruct((length, wide), BF16),
        ),
        grid_spec=pltpu.PrefetchScalarGridSpec(
            num_scalar_prefetch=1,
            grid=(chips,),
            in_specs=[cols, cols, *(full_spec(o.shape) for o in (hidden, ga, gb)), rows, rows],
            out_specs=(
                *half_specs(block, 2 * cut, half_of),
                *pair_specs(block, cut),
                pl.BlockSpec((block, 3 * cut), lambda r, chip: (r ^ chip[0], 0)),
                pl.BlockSpec((length, block), lambda r, chip: (0, r)),
            ),
        ),
        compiler_params=params(),
        cost_estimate=NO_COST,
    )(chip, second, cot, hidden, ga, gb, da, db)


def first_grads_kernel(x_ref, near_ref, far_ref, keepn_ref, given_ref, keepf_ref, givef_ref, gate_ref):
    x = x_ref[...]
    near, far = tn(x, near_ref[...]), tn(x, far_ref[...])
    put_half(near, keepn_ref, given_ref)
    put_pair(far, keepf_ref, givef_ref)
    gate_ref[:, :PAIR] = near[:, 4 * PAIR :]
    gate_ref[:, PAIR:] = far[:, 4 * PAIR :]


def first_grads(x_hat, near, far, chips):
    length, wide = x_hat.shape
    block = wide // chips
    cols = near.shape[1]
    half_of = chips // 2
    if block % PAIR:
        near, far = tn(x_hat, near), tn(x_hat, far)
        gate = jnp.concatenate([near[:, 4 * PAIR :], far[:, 4 * PAIR :]], axis=1)
        return *halves_apart(near.astype(BF16)), *halves_apart(pairs_apart(far.astype(BF16), chips)), gate
    return pl.pallas_call(
        first_grads_kernel,
        grid=(chips,),
        out_shape=(
            *(jax.ShapeDtypeStruct((wide // 2, cols), BF16),) * 4,
            jax.ShapeDtypeStruct((wide, 2 * PAIR), F32),
        ),
        in_specs=[pl.BlockSpec((length, block), lambda r: (0, r)), full_spec(near.shape), full_spec(far.shape)],
        out_specs=(
            *half_specs(block, cols, half_of),
            *pair_specs(block, cols),
            pl.BlockSpec((block, 2 * PAIR), lambda r: (r, 0)),
        ),
        compiler_params=params(),
        cost_estimate=NO_COST,
    )(x_hat, near, far)


def attend_back(pos, qkv, logit, seg_row, seg_col, lse, cum, grad_mixed, cols, quarter):
    length = qkv.shape[0]
    grads = jax.ShapeDtypeStruct((length, cols), BF16)
    return pl.pallas_call(
        functools.partial(backward_kernel, quarter),
        grid=(3,),
        out_shape=(grads, grads, jax.ShapeDtypeStruct((1, PAIR), F32)),
        in_specs=[
            pl.BlockSpec(memory_space=pltpu.SMEM),
            full_spec(qkv.shape),
            full_spec(logit.shape),
            full_spec(seg_row.shape),
            full_spec(seg_col.shape),
            full_spec(lse.shape),
            full_spec(cum.shape),
            full_spec(grad_mixed.shape),
        ],
        out_specs=(full_spec((length, cols)), full_spec((length, cols)), full_spec((1, PAIR))),
        scratch_shapes=[
            pltpu.VMEM((PAIR, length), F32),
            pltpu.VMEM((length, PAIR), F32),
            pltpu.VMEM((PAIR, length), F32),
            pltpu.VMEM((length, 9 * PAIR), F32),
            pltpu.VMEM((length, PAIR), F32),
            pltpu.VMEM((length, PAIR), F32),
        ],
        compiler_params=params(),
        cost_estimate=NO_COST,
    )(pos, qkv, logit, seg_row, seg_col, lse, cum, grad_mixed)


def unit_rows(value):
    scale = lax.rsqrt(jnp.mean(value * value, axis=-1, keepdims=True) + EPS)
    return value * scale, scale


def unit_back(value, scale, weighted):
    inner = jnp.mean(weighted * value, axis=-1, keepdims=True)
    return scale * weighted - value * (scale * scale * scale) * inner


def per_device(
    block_input, attn_gain, w_query, w_key, w_value, w_forget, forget_bias, w_output,
    mlp_gain, w_gate, w_up, w_down, segment_ids, cotangent,
):
    width = block_input.shape[1]
    quarter = block_input.shape[0]
    heads = w_forget.shape[1]
    share = w_query.shape[0]
    inner = w_output.shape[0]
    hidden_width = w_gate.shape[1]
    chips = lax.axis_size("dp") // 2
    bits = chips.bit_length() - 1
    d = lax.axis_index("dp")
    t = lax.axis_index("tensor")
    core, chip = d & 1, d >> 1
    first = core == 0
    at_home = core == t >> 1
    wide = width // chips
    half_heads = heads // 2

    def pick(one, two):
        return jnp.where(first, val(one), val(two))

    def pick_home(one, two):
        return jnp.where(at_home, val(one), val(two))

    def by_parity(mine, other):
        return pick(rows_of([mine, other]), rows_of([other, mine]))

    def reorder(rows):
        return jnp.concatenate(
            [lax.dynamic_slice_in_dim(rows, (chip ^ r) * wide, wide, 1) for r in range(chips)], axis=1
        )

    def reorder_rows(rows):
        return rows_of([lax.dynamic_slice_in_dim(rows, (chip ^ r) * wide, wide, 0) for r in range(chips)])

    planes = [[2 * k + c for k in range(chips)] for c in (0, 1)]
    up_order, down_order = list(range(bits)), list(reversed(range(bits)))

    class Pack:
        def __init__(self, mine, other):
            self.mine, self.other = mine, other

        def near(self, *others):
            self.near_other = send(hold(self.other, *others) if others else self.other, over_core)
            return self.near_other

        def cross(self, *others):
            mine, other = hold((self.mine, self.other), *others) if others else (self.mine, self.other)
            self.crossed = (send(mine, over_half), send(other, over_core_half))
            return self.crossed

        def near_rows(self):
            return by_parity(self.mine, self.near_other)

        def far_rows(self):
            return by_parity(*self.crossed)

    class Spread:
        def __init__(self, rows, order):
            self.pieces, self.order = {0: rows}, order

        def early(self):
            for bit in self.order:
                self.pieces[1 << bit] = send(self.pieces[0], over_chip(bit))
            return [self.pieces[1 << bit] for bit in self.order]

        def late(self):
            before = set(self.pieces)
            for i, bit in enumerate(self.order):
                passed = sum(1 << b for b in self.order[:i])
                for at in range(1, 1 << bits):
                    if not at & ~passed:
                        self.pieces[at | (1 << bit)] = send(self.pieces[at], over_chip(bit))
            return [v for k, v in self.pieces.items() if k not in before]

        def direct(self):
            for at in range(1, chips):
                self.pieces[at] = send(self.pieces[0], lambda d, t, at=at: (d ^ (2 * at), t))
            return [self.pieces[at] for at in range(1, chips)]

        def whole(self):
            return rows_of([self.pieces[r] for r in range(chips)])

    class Sum:
        def __init__(self, keep, give, order):
            self.order = order
            self.keep, self.give = Box(val(keep)), Box(val(give))

        def made(self):
            return self.keep, self.give

        def out(self):
            self.got = send(self.give, over_chip(self.order[0]))
            return self.got

        def rest(self):
            rows = self.keep.v.astype(F32) + self.got.v.astype(F32)
            for bit in self.order[1:]:
                if self.order == down_order:
                    cut = rows.shape[0] // 2
                    self.keep, give = Box(rows[:cut]), rows[cut:]
                else:
                    blocks = [rows[k : k + wide] for k in range(0, rows.shape[0], wide)]
                    self.keep, give = Box(rows_of(blocks[0::2])), rows_of(blocks[1::2])
                self.last = send(give.astype(BF16), over_chip(bit))
                if bit != self.order[-1]:
                    rows = self.keep.v + self.last.v.astype(F32)
            return self.last

        def own(self):
            return (self.keep.v + self.last.v.astype(F32)).astype(BF16)

    class Finish:
        def near(self, rows):
            self.mine_near, other = pick(rows[:share], rows[share:]), pick(rows[share:], rows[:share])
            self.here = send(other, over_core)
            return self.here

        def far_one(self, rows):
            mine, other = pick(rows[:share], rows[share:]), pick(rows[share:], rows[:share])
            self.other = Box(other)
            self.same = send(mine, over_half)
            return self.same

        def far_two(self):
            self.cross = send(self.other, over_core_half)
            return self.cross

        def land(self):
            mine = self.mine_near.astype(F32) + self.same.v.astype(F32)
            rest = self.here.v.astype(F32) + self.cross.v.astype(F32)
            return pick(mine, rest), pick(rest, mine)

    gain_one = attn_gain.astype(F32)[:, None]
    gain_two = mlp_gain.astype(F32)[:, None]
    part, fpart = inner // 2, half_heads
    fcut = hidden_width // 2
    lanes = ((0, 0), (0, PAIR - heads))
    forget_own = jnp.pad(lax.dynamic_slice_in_dim(w_forget, d * share, share, 0), lanes)
    one = Pack(
        *pack_one(
            core.astype(jnp.int32)[None], w_query, w_key, w_value, forget_own, attn_gain[None, :],
            jnp.pad(forget_bias[None, :], lanes),
        )
    )
    out_t, down_t = w_output.T, w_down.T
    gate_scaled, up_scaled = ((w.astype(F32) * gain_two).astype(BF16) for w in (w_gate, w_up))

    def halves_of(arrays, size):
        halves = [jnp.concatenate([w[:, h * size : (h + 1) * size] for w in arrays], axis=1) for h in (0, 1)]
        return pick(*halves), pick(*halves[::-1])

    def stay(d, t):
        return (d, t ^ 1) if (d & 1) == (t >> 1) else None

    def move(d, t):
        return (d, t ^ 1) if (d & 1) != (t >> 1) else None

    one_far = one.cross()
    one.near()
    near_one = Spread(one.near_rows(), up_order)
    near_early = near_one.early()
    x_own, cot_own = Box(reorder(block_input)), Box(reorder(cotangent))

    x_stay = send(x_own, stay)

    hold(x_own, one_far, near_early, x_stay)
    x_home = send(x_own, to_home)
    cot_stay = send(hold(cot_own, x_own), stay)
    far_one = Spread(one.far_rows(), down_order)
    far_early = far_one.early()
    near_late = near_one.late()
    wo = Pack(*halves_of([out_t], part))
    feed_pack = Pack(*halves_of([gate_scaled, up_scaled, down_t], fcut))
    gate_pack, down_pack = Pack(*halves_of([gate_scaled, up_scaled], fcut)), Pack(*halves_of([down_t], fcut))

    hold(x_home, far_early, near_late, cot_stay)
    x_move = send(x_home, move)
    x_core = send(x_home, over_core)
    far_late = far_one.late()
    wo_far = wo.cross(x_home)
    wo.near(x_home)
    seg_other = send(hold(segment_ids, x_home), over_core)
    feed_pack.near(x_home)
    near_all = Box(
        lax.all_gather(feed_pack.near_rows(), "dp", axis=0, tiled=True, axis_index_groups=planes)
    )
    seg_row = Box(pick_home(segment_ids, seg_other))
    far_bias = far_one.pieces[0][0, 4 * PAIR + HEAD + fpart + 1 :].astype(F32)
    bias_far = far_bias[:fpart] + far_bias[fpart : 2 * fpart] + far_bias[2 * fpart : 3 * fpart]
    spare = jnp.zeros((HEAD - fpart,), F32)
    bias = Box(jnp.concatenate([pick(forget_bias[:fpart], forget_bias[fpart:]), spare, bias_far, spare])[None, :])
    place = (t & 1) + 2 * core
    pos = jnp.stack([((a ^ place) >> 1) | (((a ^ place) & 1) << 1) for a in range(4)]).astype(jnp.int32)
    wa = Box(near_one.whole())

    hold(x_move, wa, bias, seg_row)
    hold(x_move, far_late, wo_far)
    x_z = Box(pick_home(x_stay, x_move))
    x_both = send(x_z, over_core)
    wb = Box(far_one.whole())
    hold(x_both, wb, x_core)
    wo_a, wo_b = wo.near_rows(), wo.far_rows()
    wo_rows = jnp.concatenate([wo_a[:, :PAIR], wo_b[:, :PAIR], wo_a[:, PAIR:], wo_b[:, PAIR:]], axis=1)
    wo_spread = Spread(wo_rows, up_order)
    wo_sent = wo_spread.direct()
    gate_far = gate_pack.cross(x_both)
    qcols = wa.v.shape[1]

    resid = x_home.v.astype(F32)
    first_scale = unit_rows(resid)[1]
    seg_col = seg_row.v.reshape(-1, 1)
    mixed, x_hat, qkv, logit, lse, cum = attend(
        pos, [x_home.v, x_core.v, x_z.v, x_both.v], wa.v, wb.v, bias.v, seg_row.v, seg_col
    )
    mixed = hold(mixed, wo_sent, gate_far)
    wo_t = wo_spread.whole()

    def half(array, which):
        rows = array.shape[0] // 2
        return array[which * rows : (which + 1) * rows]

    order = {}

    def scatter_group(far, near, at_far=lambda far_sum: None, at_near=lambda near_sum: None, at_end=lambda: (), after_far=None, late_core=False):
        rows = far()
        far_in = send(rows[quarter:].astype(BF16), over_core)
        far_sum = Box((rows[:quarter].astype(F32) + far_in.v.astype(F32)).astype(BF16))
        at_far(far_sum)
        far_got = send(far_sum, over_z)
        rows = Box(near())
        if late_core:
            hold(far_got, rows)
            if after_far:
                after_far(far_got)
            hold(rows, far_got)
        near_in = send(rows.v[quarter:].astype(BF16), over_core)
        near_sum = Box(rows.v[:quarter].astype(F32) + near_in.v.astype(F32))
        at_near(near_sum)
        hold(far_got, near_sum)
        if at_end():
            hold(far_got, at_end())
        return near_sum.v + far_got.v.astype(F32)

    sent = {}

    def weights_on(near_sum):
        sent["gate"] = Spread(gate_pack.far_rows(), up_order)
        sent["early"] = sent["gate"].early()
        sent["down"] = down_pack.cross(near_sum)

    mixed = Box(mixed)
    hidden_res = Box(
        resid
        + scatter_group(
            lambda: nt(half(mixed.v, 1), wo_t),
            lambda: nt(half(mixed.v, 0), wo_t),
            lambda far_sum: hold(far_sum, mixed),
            weights_on,
            lambda: (sent["early"], sent["down"]),
        )
    )
    far_gate = sent["gate"]
    second, second_scale = unit_rows(hidden_res.v)
    second_low = Box(second.astype(BF16))
    second_z = send(second_low, over_z)
    second_core = send(second_low, over_core)
    gate_late = far_gate.late()
    far_down = Spread(down_pack.far_rows(), down_order)
    down_early = far_down.early()
    cot_home = send(hold(cot_own, second_core), to_home)
    hold(near_all, second_core)
    gates_a = Box(reorder_rows(near_all.v[:, : 2 * fcut]))
    downs_a = Box(reorder_rows(near_all.v[:, 2 * fcut :]))
    hold(second_z, gates_a, downs_a)
    hold(second_z, cot_home, gate_late, down_early)
    second_both = send(second_z, over_core)
    cot_move = send(cot_home, move)
    down_late = far_down.late()
    cot_core = send(cot_home, over_core)
    gates_b = Box(far_gate.whole())
    hold(cot_move, second_both, gates_b)
    hold(cot_move, down_late)
    downs_b = Box(far_down.whole())
    cot_z = Box(pick_home(cot_stay, cot_move))
    cot_both = send(cot_z, over_core)
    hold(cot_both, cot_core)

    feed_weights = (gates_a.v, gates_b.v, downs_a.v, downs_b.v)
    made = {}

    def feed_far():
        made["far"] = feed_tokens((second_z.v, second_both.v), (cot_z.v, cot_both.v), feed_weights, 1)
        return made["far"][5]

    def feed_near():
        made["near"] = feed_tokens(
            (second_low.v, second_core.v), (cot_home.v, cot_core.v), feed_weights, 0, made["far"][:5]
        )
        return made["near"][5]

    grad_second = scatter_group(feed_far, feed_near, lambda far_sum: hold(far_sum, second_low, second_core), late_core=True)
    gain_two_part = made["far"][6] + made["near"][6]
    grad_res = Box(cot_home.v.astype(F32) + unit_back(hidden_res.v, second_scale, grad_second))
    branch = Box(grad_res.v.astype(BF16))
    laid = [Box(m) for m in made["near"][:5]]
    hold(branch, laid)
    branch_z = send(branch, over_z)
    hidden, grads_a, grads_b, second_all, cot_all = (m.v for m in laid)
    *b_rows, a_part, mlp_rows = (
        Box(m)
        for m in feed_grads(
            chip.astype(jnp.int32)[None], second_all, cot_all, hidden, grads_a, grads_b, downs_a.v, downs_b.v, chips
        )
    )
    hold(branch_z, b_rows, a_part, mlp_rows)
    hold(branch, branch_z)
    branch_both = send(branch_z, over_core)
    branch_core = send(branch, over_core)
    gb, db = Sum(*b_rows[:2], down_order), Sum(*b_rows[2:], up_order)
    b_out = [gb.out(), db.out()]
    branch_all = Box(rows_of([branch, branch_core, branch_z, branch_both]))

    grad_mixed = Box(nn(branch_all.v, wo_t).astype(BF16))
    mlp_out = Box(scatter_group(lambda: half(mlp_rows.v, 1), lambda: half(mlp_rows.v, 0)))
    hold(branch_all, grad_mixed)
    o_sum = Sum(*halves_apart(tn(branch_all.v, mixed.v).astype(BF16)), down_order)
    o_out = o_sum.out()
    hold(grad_mixed, o_sum.keep)
    grad_near, grad_far, grad_bias = attend_back(
        pos, qkv, logit, seg_row.v, seg_col, lse, cum, grad_mixed.v, qcols, quarter
    )
    grad_near, grad_far, x_hat = Box(grad_near), Box(grad_far), Box(x_hat)
    hold(grad_near, grad_far, b_out, mlp_out)
    out_home = (hidden_res.v + mlp_out.v).astype(BF16)
    out_sent = send(out_home, swap_home)
    b_late = [gb.rest(), db.rest()]
    hold(a_part, mlp_out)
    a_own = Box(
        lax.psum_scatter(a_part.v, "dp", scatter_dimension=0, tiled=True, axis_index_groups=planes)
    )
    first_parts = {}
    feed_end = Finish()

    def first_part(which):
        first_parts[which] = nt(half(grad_near.v, which), wa.v) + nt(half(grad_far.v, which), wb.v)
        return first_parts[which]

    def first_near():
        rows = Box(first_part(0))
        hold(x_hat, rows)
        made["grads"] = [Box(g) for g in first_grads(x_hat.v, grad_near.v, grad_far.v, chips)]
        return rows.v

    grad_first = Box(
        scatter_group(
            lambda: first_part(1),
            first_near,
            lambda far_sum: hold(far_sum, grad_near, grad_far, x_hat),
            after_far=lambda far_got: hold(far_got, b_late, out_sent, made["grads"]),
            late_core=True,
        )
    )
    grads = made["grads"]
    qa, qb, gate_cols = Sum(*grads[:2], down_order), Sum(*grads[2:4], up_order), grads[4]
    b_same = feed_end.far_one(jnp.concatenate([gb.own(), db.own()], axis=1))
    q_out = [qa.out(), qb.out()]
    back_home = Box((grad_res.v + unit_back(resid, first_scale, grad_first.v)).astype(BF16))
    back_sent = send(back_home, swap_home)

    hold(gate_cols, back_home)
    forget = jnp.concatenate([gate_cols.v[:, k * PAIR + HEAD : k * PAIR + HEAD + fpart] for k in (0, 1)], axis=1).T
    gain_part = functools.reduce(
        jnp.add, [jnp.sum(half(x_hat.v, w).astype(F32) * first_parts[w], axis=0) for w in (0, 1)]
    )
    gain_row = wa.v[:, 3 * part + fpart].astype(F32)
    small = reorder(jnp.concatenate([forget * gain_row[None, :], gain_part[None], gain_two_part], axis=0))
    small = Box(jnp.concatenate([small, jnp.pad(grad_bias, ((0, 0), (0, width - PAIR)))], axis=0))
    small_there = send(small, over_chip(0))

    hold(small, q_out, small_there, o_out, b_same)
    q_late = [qa.rest(), qb.rest()]
    o_late = o_sum.rest()
    hold(feed_end.other, small)
    b_cross = feed_end.far_two()
    small = Box(small.v + small_there.v)
    hold(small, q_late, o_late, back_sent)
    for bit in range(1, bits):
        small = Box(small.v + send(small, over_chip(bit)).v)
    near, far = small.v[:fpart], small.v[fpart:heads]
    gains, bias_sum = small.v[heads : heads + 2], small.v[heads + 2 :]
    spread_out = ((0, 0), (0, width - fpart))
    bias_near, bias_far = (jnp.pad(bias_sum[:, k * HEAD : k * HEAD + fpart], spread_out) for k in (0, 1))
    far_small = Box(jnp.concatenate([far, bias_far, gains], axis=0))
    hold(far_small, q_late, o_late)
    got = send(far_small, over_half)
    hold(a_own, o_late)
    feed_end.near(a_own.v)

    own_out = o_sum.own()
    out_halves = [
        jnp.concatenate(
            [own_out[:, h * PAIR : (h + 1) * PAIR], own_out[:, 2 * PAIR + h * HEAD : 2 * PAIR + (h + 1) * HEAD]], axis=1
        )
        for h in (0, 1)
    ]
    q_end = Finish()
    q_same = q_end.far_one(jnp.concatenate([qb.own(), out_halves[1]], axis=1))
    q_cross = q_end.far_two()
    q_here = q_end.near(jnp.concatenate([qa.own(), out_halves[0]], axis=1))
    hold(got, q_here, b_cross)
    mine = jnp.concatenate(
        [near + got.v[:fpart], bias_near + got.v[fpart : fpart + 1], gains + got.v[fpart + 1 :]], axis=0
    )
    rest = send(mine, over_core).v
    grad_forget = pick(rows_of([mine[:fpart], rest[:fpart]]), rows_of([rest[:fpart], mine[:fpart]])).T
    bias_mine, bias_rest = mine[fpart, :fpart], rest[fpart, :fpart]
    grad_bias_out = pick(jnp.concatenate([bias_mine, bias_rest]), jnp.concatenate([bias_rest, bias_mine]))
    gains = mine[fpart + 1 :] + rest[fpart + 1 :]
    gains = lax.dynamic_slice_in_dim(gains, d * share, share, 1)
    gains = Box(gains + send(gains, over_z).v)
    hold(gains, q_same, q_cross)
    gains = gains.v
    grad_gain_one = gains[0] / attn_gain.astype(F32)
    grad_gain_two = gains[1] / mlp_gain.astype(F32)
    f_zero, f_one = feed_end.land()
    gate_sum, up_sum, down_sum = (
        jnp.concatenate([f[:, k * fcut : (k + 1) * fcut] for f in (f_zero, f_one)], axis=1) for k in range(3)
    )
    input_grad = reorder(pick_home(back_home, back_sent)).astype(F32)
    output = reorder(pick_home(out_home, out_sent))
    q_zero, q_one = q_end.land()

    def joined(k):
        if k == 3:
            return jnp.concatenate([q_zero[:, qcols:], q_one[:, qcols:]], axis=1)
        lone = slice(3 * PAIR + k * HEAD, 3 * PAIR + (k + 1) * HEAD)
        pair = slice(k * PAIR, (k + 1) * PAIR)
        return jnp.concatenate([q_zero[:, pair], q_zero[:, lone], q_one[:, pair], q_one[:, lone]], axis=1)

    q_sums = [joined(k) for k in range(4)]

    return (
        output,
        input_grad,
        grad_gain_one,
        q_sums[0] * gain_one,
        q_sums[1] * gain_one,
        q_sums[2] * gain_one,
        grad_forget,
        grad_bias_out,
        q_sums[3].T,
        grad_gain_two,
        gate_sum * gain_two,
        up_sum * gain_two,
        down_sum.T,
    )


def solution(mesh):
    return jax.shard_map(
        per_device,
        mesh=mesh,
        in_specs=(
            P(("dp", "tensor"), None),
            P("dp"),
            P("dp", "tensor"),
            P("dp", "tensor"),
            P("dp", "tensor"),
            P(None, "tensor"),
            P("tensor"),
            P("tensor", "dp"),
            P("dp"),
            P("dp", "tensor"),
            P("dp", "tensor"),
            P("tensor", "dp"),
            P("dp", None),
            P(("dp", "tensor"), None),
        ),
        out_specs=(
            P(("dp", "tensor"), None),
            P(("dp", "tensor"), None),
            P("dp"),
            P("dp", "tensor"),
            P("dp", "tensor"),
            P("dp", "tensor"),
            P(None, "tensor"),
            P("tensor"),
            P("tensor", "dp"),
            P("dp"),
            P("dp", "tensor"),
            P("dp", "tensor"),
            P("tensor", "dp"),
        ),
        check_vma=False,
    )
```

```python
import functools

import jax
import jax.numpy as jnp
from jax import lax
from jax.experimental import pallas as pl
from jax.experimental.pallas import tpu as pltpu
from jax.sharding import PartitionSpec as P

HEAD = 64
PAIR = 2 * HEAD
EPS = 1e-06
F32 = jnp.float32
BF16 = jnp.bfloat16
NT = (((1,), (1,)), ((), ()))
TN = (((0,), (0,)), ((), ()))
AXES = ("dp", "tensor")


def nn(a, b):
    return jnp.dot(a, b, preferred_element_type=F32)


def nt(a, b):
    return lax.dot_general(a, b, NT, preferred_element_type=F32)


def tn(a, b):
    return lax.dot_general(a, b, TN, preferred_element_type=F32)


class Box:
    def __init__(self, v):
        self.v = v


def val(value):
    return value.v if isinstance(value, Box) else value


def boxes(tree):
    if isinstance(tree, Box):
        return [tree]
    assert isinstance(tree, (list, tuple)), type(tree)
    return [b for item in tree for b in boxes(item)]


def send(value, move):
    tensor = lax.axis_size("tensor")
    pairs = []
    for d in range(lax.axis_size("dp")):
        for t in range(tensor):
            to = move(d, t)
            if to is not None:
                pairs.append((d * tensor + t, to[0] * tensor + to[1]))
    return Box(lax.ppermute(val(value), AXES, pairs))


def to_home(d, t):
    return (d ^ 1, t ^ 2) if (d & 1) != (t >> 1) else (d, t)


def swap_home(d, t):
    return (d ^ 1, t ^ 2) if (d & 1) != (t >> 1) else None


def over_core(d, t):
    return (d ^ 1, t)


def over_z(d, t):
    return (d, t ^ 1)


def over_chip(bit):
    return lambda d, t: (d ^ (2 << bit), t)


def over_half(d, t):
    return (d, t ^ 2)


def over_core_half(d, t):
    return (d ^ 1, t ^ 2)


def hold(value, *others):
    held = boxes(others)
    result, new = lax.optimization_barrier((jax.tree.map(val, value, is_leaf=lambda x: isinstance(x, Box)), [b.v for b in held]))
    for b, v in zip(held, new):
        b.v = v
    if isinstance(value, Box):
        value.v = result
        return value
    return result


def meet(critical, *others):
    return hold(hold(critical), *others)


def rows_of(pieces):
    return jnp.concatenate([val(p) for p in pieces], axis=0)


def block_of(pos_ref, at, size):
    return pl.ds(pl.multiple_of(pos_ref[at] * size, size), size)


def lane_of(pair, h):
    return jnp.where(pair == 2, 2 + HEAD * h, HEAD * pair + h)


def pack_kernel(core_ref, query_ref, key_ref, value_ref, forget_ref, gain_ref, bias_ref, mine_ref, other_ref):
    share = gain_ref.shape[1]
    diagonal = lax.broadcasted_iota(jnp.int32, (share, share), 0) == lax.broadcasted_iota(jnp.int32, (share, share), 1)
    gain = jnp.sum(jnp.where(diagonal, gain_ref[...].astype(F32), 0.0), axis=1, keepdims=True)
    lane = lax.broadcasted_iota(jnp.int32, (share, PAIR), 1)
    low_lanes = lane < HEAD
    first = core_ref[0] == 0
    parts = [ref[...].astype(F32) * gain for ref in (query_ref, key_ref, value_ref)]
    forget = forget_ref[...].astype(F32) * gain
    bias = bias_ref[...]
    pieces = []
    for _ in range(3):
        piece = bias.astype(BF16).astype(F32)
        pieces.append(piece)
        bias = bias - piece
    halves = []
    for h in range(2):
        three = [p if h == 0 else pltpu.roll(p, p.shape[1] // 2, 1) for p in parts]
        tiles = [p[:, :PAIR] for p in three]
        lone = [p[:, PAIR : 2 * PAIR] for p in three]
        tiles.append(jnp.where(low_lanes, lone[0], pltpu.roll(lone[1], HEAD, 1)))
        rest = jnp.where(lane < HEAD + 3, pltpu.roll(forget, HEAD - 3 * h, 1), gain)
        for k, piece in enumerate(pieces):
            at = HEAD + 4 + 3 * k
            moved = jnp.broadcast_to(pltpu.roll(piece, at - 3 * h, 1), (share, PAIR))
            rest = jnp.where((lane >= at) & (lane < at + 3), moved, rest)
        rest = jnp.where(lane < HEAD + 13, rest, 0.0)
        tiles.append(jnp.where(low_lanes, lone[2], rest))
        halves.append(tiles)
    for k in range(5):
        at = slice(k * PAIR, (k + 1) * PAIR)
        mine_ref[:, at] = jnp.where(first, halves[0][k], halves[1][k]).astype(BF16)
        other_ref[:, at] = jnp.where(first, halves[1][k], halves[0][k]).astype(BF16)


def forward_kernel(
    quarter, pos_ref, x0_ref, x1_ref, x2_ref, x3_ref, wa_ref, wb_ref, bias_ref, segr_ref, segc_ref,
    mixed_ref, xhat_ref, qkv_ref, logit_ref, lse_ref, cum_ref, cumr_ref, rel_ref,
):
    pair = pl.program_id(0)
    width = 3 * PAIR
    lane = lax.broadcasted_iota(jnp.int32, (quarter, PAIR), 1)
    low_lanes = lane < HEAD
    count = segr_ref.shape[1] // quarter

    @pl.when(pair == 0)
    def _():
        for r, x_ref in enumerate((x0_ref, x1_ref, x2_ref, x3_ref)):
            at = slice(r * quarter, (r + 1) * quarter)
            x = x_ref[...].astype(F32)
            low = (x * lax.rsqrt(jnp.mean(x * x, axis=1, keepdims=True) + EPS)).astype(BF16)
            xhat_ref[at, :] = low
            near_all = nn(low, wa_ref[...])
            far_all = nn(low, wb_ref[...])

            def near(k):
                return near_all[:, k * PAIR : (k + 1) * PAIR]

            def far(k):
                return far_all[:, k * PAIR : (k + 1) * PAIR]

            for k in range(3):
                qkv_ref[at, k * width : k * width + PAIR] = near(k).astype(BF16)
                qkv_ref[at, k * width + PAIR : k * width + 2 * PAIR] = far(k).astype(BF16)

            def both(one, two):
                return jnp.where(low_lanes, one, two).astype(BF16)

            qkv_ref[at, 2 * PAIR : 3 * PAIR] = both(near(3), pltpu.roll(far(3), HEAD, 1))
            qkv_ref[at, width + 2 * PAIR : width + 3 * PAIR] = both(pltpu.roll(near(3), HEAD, 1), far(3))
            qkv_ref[at, 2 * width + 2 * PAIR : 2 * width + 3 * PAIR] = both(near(4), pltpu.roll(far(4), HEAD, 1))
            rel_ref[at, :] = jnp.where(low_lanes, pltpu.roll(near(4), HEAD, 1), far(4)) + bias_ref[...]
        rows = lax.broadcasted_iota(jnp.int32, (quarter, quarter), 0)
        cols = lax.broadcasted_iota(jnp.int32, (quarter, quarter), 1)
        lower = (cols <= rows).astype(F32)
        carry = jnp.zeros((1, PAIR), F32)
        for a in range(count):
            logit = rel_ref[block_of(pos_ref, a, quarter), :]
            here = slice(a * quarter, (a + 1) * quarter)
            logit_ref[here, :] = logit
            logsig = jnp.minimum(logit, 0.0) - jnp.log1p(jnp.exp(-jnp.abs(logit)))
            cum = jnp.dot(lower, logsig, precision=lax.Precision.HIGHEST, preferred_element_type=F32) + carry
            carry = cum[quarter - 1 :, :]
            cum_ref[here, :] = cum
            cumr_ref[:, here] = cum.T
        lse_ref[...] = jnp.zeros(lse_ref.shape, F32)

    def columns(part):
        return pl.ds(pl.multiple_of(part * width + pair * PAIR, PAIR), PAIR)

    diag_rows = lax.broadcasted_iota(jnp.int32, (quarter, quarter), 0)
    diag_cols = lax.broadcasted_iota(jnp.int32, (quarter, quarter), 1)
    for a in range(count):
        query = (qkv_ref[block_of(pos_ref, a, quarter), columns(0)] * 0.125).astype(BF16)
        seg_q = segc_ref[a * quarter : (a + 1) * quarter, :]
        spans = range(max(0, a - 512 // quarter), a + 1)
        outs = []
        for h in range(2):
            head = lane_of(pair, h)
            mine = (lane >= HEAD) if h else low_lanes
            query_h = jnp.where(mine, query, jnp.zeros_like(query))
            scores = []
            for b in spans:
                keys = qkv_ref[block_of(pos_ref, b, quarter), columns(1)]
                s = nt(query_h, keys) - cumr_ref[pl.ds(head, 1), b * quarter : (b + 1) * quarter]
                allowed = seg_q == segr_ref[:, b * quarter : (b + 1) * quarter]
                if a == b:
                    allowed &= diag_cols <= diag_rows
                scores.append(jnp.where(allowed, s, -jnp.inf))
            top = functools.reduce(jnp.maximum, [jnp.max(s, axis=1, keepdims=True) for s in scores])
            expd = [jnp.exp(s - top) for s in scores]
            total = functools.reduce(jnp.add, [jnp.sum(e, axis=1, keepdims=True) for e in expd])
            scale = 1.0 / total
            out = None
            for e, b in zip(expd, spans):
                values = qkv_ref[block_of(pos_ref, b, quarter), columns(2)]
                part = nn((e * scale).astype(BF16), values)
                out = part if out is None else out + part
            outs.append(out)
            lse = top + jnp.log(total)
            at = pl.ds(a * quarter, quarter)
            lse_ref[at, :] = jnp.where(lane == head, lse, lse_ref[at, :])
        mixed_ref[block_of(pos_ref, a, quarter), columns(0)] = jnp.where(low_lanes, outs[0], outs[1]).astype(BF16)


def backward_kernel(
    quarter, pos_ref, qkv_ref, logit_ref, segr_ref, segc_ref, lse_ref, cum_ref, gmix_ref,
    gnear_ref, gfar_ref, gbias_ref, lser_ref, gcol_ref, grow_ref, grad_ref, gk_ref, gv_ref,
):
    pair = pl.program_id(0)
    pairs = pl.num_programs(0)
    width = 3 * PAIR
    lane = lax.broadcasted_iota(jnp.int32, (quarter, PAIR), 1)
    low_lanes = lane < HEAD
    count = segr_ref.shape[1] // quarter

    @pl.when(pair == 0)
    def _():
        for a in range(count):
            at = slice(a * quarter, (a + 1) * quarter)
            lser_ref[:, at] = lse_ref[at, :].T
        gcol_ref[...] = jnp.zeros(gcol_ref.shape, F32)
        grow_ref[...] = jnp.zeros(grow_ref.shape, F32)

    def columns(part):
        return pl.ds(pl.multiple_of(part * width + pair * PAIR, PAIR), PAIR)

    diag_rows = lax.broadcasted_iota(jnp.int32, (quarter, quarter), 0)
    diag_cols = lax.broadcasted_iota(jnp.int32, (quarter, quarter), 1)
    gk_ref[...] = jnp.zeros(gk_ref.shape, F32)
    gv_ref[...] = jnp.zeros(gv_ref.shape, F32)
    for a in range(count):
        here = slice(a * quarter, (a + 1) * quarter)
        query = (qkv_ref[block_of(pos_ref, a, quarter), columns(0)] * 0.125).astype(BF16)
        gout = gmix_ref[block_of(pos_ref, a, quarter), columns(0)]
        seg_q = segr_ref[:, here]
        spans = range(max(0, a - 512 // quarter), a + 1)
        grad_query = None
        for h in range(2):
            head = lane_of(pair, h)
            mine = (lane >= HEAD) if h else low_lanes
            query_h = jnp.where(mine, query, jnp.zeros_like(query))
            gout_h = jnp.where(mine, gout, jnp.zeros_like(gout))
            lse = lser_ref[pl.ds(head, 1), here]
            probs, gprobs = [], []
            inner = None
            for b in spans:
                there = slice(b * quarter, (b + 1) * quarter)
                keys = qkv_ref[block_of(pos_ref, b, quarter), columns(1)]
                values = qkv_ref[block_of(pos_ref, b, quarter), columns(2)]
                cum_k = jnp.sum(jnp.where(lane == head, cum_ref[there, :], 0.0), axis=1, keepdims=True)
                s = nt(keys, query_h) - cum_k
                allowed = segc_ref[there, :] == seg_q
                if a == b:
                    allowed &= diag_rows <= diag_cols
                p = jnp.where(allowed, jnp.exp(s - lse), 0.0)
                g = nt(values, gout_h)
                probs.append(p)
                gprobs.append(g)
                part = jnp.sum(p * g, axis=0, keepdims=True)
                inner = part if inner is None else inner + part
            row_sum = None
            for p, g, b in zip(probs, gprobs, spans):
                there = slice(b * quarter, (b + 1) * quarter)
                keys = (qkv_ref[block_of(pos_ref, b, quarter), columns(1)] * 0.125).astype(BF16)
                keys_h = jnp.where(mine, keys, jnp.zeros_like(keys))
                gs = p * (g - inner)
                part = jnp.sum(gs, axis=0, keepdims=True)
                row_sum = part if row_sum is None else row_sum + part
                col_sum = jnp.sum(gs, axis=1, keepdims=True)
                gcol_ref[there, :] += jnp.where(lane == head, col_sum, 0.0)
                low = gs.astype(BF16)
                gk_ref[there, :] += nn(low, query_h)
                gv_ref[there, :] += nn(p.astype(BF16), gout_h)
                part = tn(low, keys_h)
                grad_query = part if grad_query is None else grad_query + part
            grow_ref[pl.ds(head, 1), here] = row_sum
        grad_ref[block_of(pos_ref, a, quarter), columns(0)] = grad_query
    for a in range(count):
        here = slice(a * quarter, (a + 1) * quarter)
        grad_ref[block_of(pos_ref, a, quarter), columns(1)] = gk_ref[here, :]
        grad_ref[block_of(pos_ref, a, quarter), columns(2)] = gv_ref[here, :]

    @pl.when(pair == pairs - 1)
    def _():
        upper = (diag_cols >= diag_rows).astype(F32)
        carry = jnp.zeros((1, PAIR), F32)
        bias = jnp.zeros((1, PAIR), F32)
        real = (lane % HEAD) < pairs
        for a in reversed(range(count)):
            here = slice(a * quarter, (a + 1) * quarter)
            at = block_of(pos_ref, a, quarter)
            logit = logit_ref[here, :]
            gcum = jnp.where(real, grow_ref[:, here].T - gcol_ref[here, :], 0.0)
            back = jnp.dot(upper, gcum, precision=lax.Precision.HIGHEST, preferred_element_type=F32) + carry
            carry = back[:1, :]
            glogit = jnp.where(real, back * (1.0 / (1.0 + jnp.exp(logit))), 0.0)
            bias = bias + jnp.sum(glogit, axis=0, keepdims=True)

            def grad(part, k):
                return grad_ref[at, part * width + k * PAIR : part * width + (k + 1) * PAIR]

            for k in range(3):
                gnear_ref[at, k * PAIR : (k + 1) * PAIR] = grad(k, 0).astype(BF16)
                gfar_ref[at, k * PAIR : (k + 1) * PAIR] = grad(k, 1).astype(BF16)
            q_last, k_last, v_last = grad(0, 2), grad(1, 2), grad(2, 2)
            k_roll = pltpu.roll(k_last, HEAD, 1)
            gnear_ref[at, 3 * PAIR : 4 * PAIR] = jnp.where(low_lanes, q_last, k_roll).astype(BF16)
            gnear_ref[at, 4 * PAIR :] = jnp.where(low_lanes, v_last, pltpu.roll(glogit, HEAD, 1)).astype(BF16)
            gfar_ref[at, 3 * PAIR : 4 * PAIR] = jnp.where(low_lanes, pltpu.roll(q_last, HEAD, 1), k_last).astype(BF16)
            gfar_ref[at, 4 * PAIR :] = jnp.where(low_lanes, pltpu.roll(v_last, HEAD, 1), glogit).astype(BF16)
        gbias_ref[...] = bias


def full_spec(shape):
    return pl.BlockSpec(shape, lambda *_: (0,) * len(shape))


NO_COST = pl.CostEstimate(flops=0, bytes_accessed=0, transcendentals=0)


def params():
    return pltpu.CompilerParams(vmem_limit_bytes=56 * 2**20, dimension_semantics=("arbitrary",))


def pack_one(core, query, keys, values, forget, gain, bias):
    share = gain.shape[1]
    out = jax.ShapeDtypeStruct((share, 5 * PAIR), BF16)
    return pl.pallas_call(
        pack_kernel,
        grid=(1,),
        out_shape=(out, out),
        in_specs=[
            pl.BlockSpec(memory_space=pltpu.SMEM),
            *(full_spec(w.shape) for w in (query, keys, values, forget, gain, bias)),
        ],
        out_specs=(full_spec(out.shape), full_spec(out.shape)),
        compiler_params=params(),
        cost_estimate=NO_COST,
    )(core, query, keys, values, forget, gain, bias)


def attend(pos, blocks, wa, wb, bias, seg_row, seg_col):
    quarter, wide = blocks[0].shape
    length = 4 * quarter
    width = 3 * PAIR
    small = jax.ShapeDtypeStruct((length, PAIR), F32)
    outs = (
        jax.ShapeDtypeStruct((length, width), BF16),
        jax.ShapeDtypeStruct((length, wide), BF16),
        jax.ShapeDtypeStruct((length, 3 * width), BF16),
        small,
        small,
        small,
    )
    operands = (*blocks, wa, wb, bias, seg_row, seg_col)
    return pl.pallas_call(
        functools.partial(forward_kernel, quarter),
        grid=(3,),
        out_shape=outs,
        in_specs=[pl.BlockSpec(memory_space=pltpu.SMEM), *(full_spec(o.shape) for o in operands)],
        out_specs=tuple(full_spec(o.shape) for o in outs),
        scratch_shapes=[pltpu.VMEM((PAIR, length), F32), pltpu.VMEM((length, PAIR), F32)],
        compiler_params=params(),
        cost_estimate=NO_COST,
    )(pos, *operands)


def feed_kernel(s0_ref, s1_ref, c0_ref, c1_ref, ga_ref, gb_ref, da_ref, db_ref, *refs):
    hidden_ref, grada_ref, gradb_ref, second_ref, cot_ref, back_ref, gain_ref = refs[-7:]
    cut = da_ref.shape[1]
    block = s0_ref.shape[0]
    gain = None
    for i, (s_ref, c_ref) in enumerate(((s0_ref, c0_ref), (s1_ref, c1_ref))):
        at = slice(i * block, (i + 1) * block)
        second_ref[at, :] = s_ref[...]
        cot_ref[at, :] = c_ref[...]
        back = None
        for k, (w_ref, d_ref, grad_ref) in enumerate(((ga_ref, da_ref, grada_ref), (gb_ref, db_ref, gradb_ref))):
            both = nn(s_ref[...], w_ref[...])
            grad_hidden = nn(c_ref[...], d_ref[...]).astype(BF16).astype(F32)
            gate, upper = both[:, :cut], both[:, cut:]
            sigma = 1.0 / (1.0 + jnp.exp(-gate))
            swish = gate * sigma
            hidden_ref[at, k * cut : (k + 1) * cut] = (swish * upper).astype(BF16)
            grad_gate = (grad_hidden * upper * sigma * (1.0 + gate * (1.0 - sigma))).astype(BF16)
            grad_up = (grad_hidden * swish).astype(BF16)
            grad_ref[at, :cut] = grad_gate
            grad_ref[at, cut:] = grad_up
            part = nt(grad_gate, w_ref[:, :cut]) + nt(grad_up, w_ref[:, cut:])
            back = part if back is None else back + part
        back_ref[at, :] = back
        part = jnp.sum(s_ref[...].astype(F32) * back, axis=0, keepdims=True)
        gain = part if gain is None else gain + part
    gain_ref[...] = gain


def feed_tokens(second, cot, weights, which, before=()):
    block, wide = second[0].shape
    cut = weights[2].shape[1]
    operands = (*second, *cot, *weights)
    widths = (2 * cut, 2 * cut, 2 * cut, wide, wide)
    outs = tuple(jax.ShapeDtypeStruct((4 * block, w), BF16) for w in widths)
    outs += (jax.ShapeDtypeStruct((2 * block, wide), F32), jax.ShapeDtypeStruct((1, wide), F32))
    return pl.pallas_call(
        feed_kernel,
        grid=(1,),
        out_shape=outs,
        in_specs=[*(full_spec(o.shape) for o in operands)] + [pl.BlockSpec(memory_space=pl.ANY)] * len(before),
        out_specs=(
            *(pl.BlockSpec((2 * block, w), lambda i: (which, 0)) for w in widths),
            full_spec((2 * block, wide)),
            full_spec((1, wide)),
        ),
        input_output_aliases={len(operands) + k: k for k in range(len(before))},
        compiler_params=params(),
        cost_estimate=NO_COST,
    )(*operands, *before)


def put_half(rows, keep_ref, give_ref):
    first = pl.program_id(0) < pl.num_programs(0) // 2

    @pl.when(first)
    def _():
        keep_ref[...] = rows.astype(BF16)

    @pl.when(jnp.logical_not(first))
    def _():
        give_ref[...] = rows.astype(BF16)


def put_pair(rows, keep_ref, give_ref):
    even = pl.program_id(0) % 2 == 0

    @pl.when(even)
    def _():
        keep_ref[...] = rows.astype(BF16)

    @pl.when(jnp.logical_not(even))
    def _():
        give_ref[...] = rows.astype(BF16)


def half_specs(block, cols, half_of):
    return (
        pl.BlockSpec((block, cols), lambda r, *_: (jnp.minimum(r, half_of - 1), 0)),
        pl.BlockSpec((block, cols), lambda r, *_: (jnp.maximum(r - half_of, 0), 0)),
    )


def pair_specs(block, cols):
    return (pl.BlockSpec((block, cols), lambda r, *_: (r // 2, 0)),) * 2


def feed_grads_kernel(
    chip_ref, second_ref, cot_ref, hidden_ref, ga_ref, gb_ref, da_ref, db_ref,
    keepb_ref, giveb_ref, keepd_ref, gived_ref, outa_ref, part_ref,
):
    cut = da_ref.shape[1]
    second, cot = second_ref[...], cot_ref[...]
    put_half(tn(second, gb_ref[...]), keepb_ref, giveb_ref)
    put_pair(tn(cot, hidden_ref[:, cut:]), keepd_ref, gived_ref)
    outa_ref[:, : 2 * cut] = tn(second, ga_ref[...]).astype(BF16)
    outa_ref[:, 2 * cut :] = tn(cot, hidden_ref[:, :cut]).astype(BF16)
    part = nt(hidden_ref[:, :cut], da_ref[...]) + nt(hidden_ref[:, cut:], db_ref[...])
    part_ref[...] = part.astype(BF16)


def pairs_apart(rows, chips):
    block = rows.shape[0] // chips
    return rows_of([rows[r * block : (r + 1) * block] for r in (*range(0, chips, 2), *range(1, chips, 2))])


def halves_apart(rows):
    cut = rows.shape[0] // 2
    return rows[:cut], rows[cut:]


def feed_grads(chip, second, cot, hidden, ga, gb, da, db, chips):
    length, wide = second.shape
    block = wide // chips
    cut = da.shape[1]
    half_of = chips // 2
    if block % PAIR:
        down = tn(cot, hidden).astype(BF16)
        part = nt(hidden[:, :cut], da) + nt(hidden[:, cut:], db)
        own = jnp.concatenate([tn(second, ga).astype(BF16), down[:, :cut]], axis=1)
        own = [lax.dynamic_slice_in_dim(own, (chip[0] ^ r) * block, block, 0) for r in range(chips)]
        halves = halves_apart(tn(second, gb).astype(BF16)) + halves_apart(pairs_apart(down[:, cut:], chips))
        return *halves, rows_of(own), part.astype(BF16)
    cols = pl.BlockSpec((length, block), lambda r, chip: (0, r))
    rows = pl.BlockSpec((block, cut), lambda r, chip: (r, 0))
    return pl.pallas_call(
        feed_grads_kernel,
        out_shape=(
            *(jax.ShapeDtypeStruct((wide // 2, 2 * cut), BF16),) * 2,
            *(jax.ShapeDtypeStruct((wide // 2, cut), BF16),) * 2,
            jax.ShapeDtypeStruct((wide, 3 * cut), BF16),
            jax.ShapeDtypeStruct((length, wide), BF16),
        ),
        grid_spec=pltpu.PrefetchScalarGridSpec(
            num_scalar_prefetch=1,
            grid=(chips,),
            in_specs=[cols, cols, *(full_spec(o.shape) for o in (hidden, ga, gb)), rows, rows],
            out_specs=(
                *half_specs(block, 2 * cut, half_of),
                *pair_specs(block, cut),
                pl.BlockSpec((block, 3 * cut), lambda r, chip: (r ^ chip[0], 0)),
                pl.BlockSpec((length, block), lambda r, chip: (0, r)),
            ),
        ),
        compiler_params=params(),
        cost_estimate=NO_COST,
    )(chip, second, cot, hidden, ga, gb, da, db)


def first_grads_kernel(x_ref, near_ref, far_ref, keepn_ref, given_ref, keepf_ref, givef_ref, gate_ref):
    x = x_ref[...]
    near, far = tn(x, near_ref[...]), tn(x, far_ref[...])
    put_half(near, keepn_ref, given_ref)
    put_pair(far, keepf_ref, givef_ref)
    gate_ref[:, :PAIR] = near[:, 4 * PAIR :]
    gate_ref[:, PAIR:] = far[:, 4 * PAIR :]


def first_grads(x_hat, near, far, chips):
    length, wide = x_hat.shape
    block = wide // chips
    cols = near.shape[1]
    half_of = chips // 2
    if block % PAIR:
        near, far = tn(x_hat, near), tn(x_hat, far)
        gate = jnp.concatenate([near[:, 4 * PAIR :], far[:, 4 * PAIR :]], axis=1)
        return *halves_apart(near.astype(BF16)), *halves_apart(pairs_apart(far.astype(BF16), chips)), gate
    return pl.pallas_call(
        first_grads_kernel,
        grid=(chips,),
        out_shape=(
            *(jax.ShapeDtypeStruct((wide // 2, cols), BF16),) * 4,
            jax.ShapeDtypeStruct((wide, 2 * PAIR), F32),
        ),
        in_specs=[pl.BlockSpec((length, block), lambda r: (0, r)), full_spec(near.shape), full_spec(far.shape)],
        out_specs=(
            *half_specs(block, cols, half_of),
            *pair_specs(block, cols),
            pl.BlockSpec((block, 2 * PAIR), lambda r: (r, 0)),
        ),
        compiler_params=params(),
        cost_estimate=NO_COST,
    )(x_hat, near, far)


def attend_back(pos, qkv, logit, seg_row, seg_col, lse, cum, grad_mixed, cols, quarter):
    length = qkv.shape[0]
    grads = jax.ShapeDtypeStruct((length, cols), BF16)
    return pl.pallas_call(
        functools.partial(backward_kernel, quarter),
        grid=(3,),
        out_shape=(grads, grads, jax.ShapeDtypeStruct((1, PAIR), F32)),
        in_specs=[
            pl.BlockSpec(memory_space=pltpu.SMEM),
            full_spec(qkv.shape),
            full_spec(logit.shape),
            full_spec(seg_row.shape),
            full_spec(seg_col.shape),
            full_spec(lse.shape),
            full_spec(cum.shape),
            full_spec(grad_mixed.shape),
        ],
        out_specs=(full_spec((length, cols)), full_spec((length, cols)), full_spec((1, PAIR))),
        scratch_shapes=[
            pltpu.VMEM((PAIR, length), F32),
            pltpu.VMEM((length, PAIR), F32),
            pltpu.VMEM((PAIR, length), F32),
            pltpu.VMEM((length, 9 * PAIR), F32),
            pltpu.VMEM((length, PAIR), F32),
            pltpu.VMEM((length, PAIR), F32),
        ],
        compiler_params=params(),
        cost_estimate=NO_COST,
    )(pos, qkv, logit, seg_row, seg_col, lse, cum, grad_mixed)


def unit_rows(value):
    scale = lax.rsqrt(jnp.mean(value * value, axis=-1, keepdims=True) + EPS)
    return value * scale, scale


def unit_back(value, scale, weighted):
    inner = jnp.mean(weighted * value, axis=-1, keepdims=True)
    return scale * weighted - value * (scale * scale * scale) * inner


def per_device(
    block_input, attn_gain, w_query, w_key, w_value, w_forget, forget_bias, w_output,
    mlp_gain, w_gate, w_up, w_down, segment_ids, cotangent,
):
    width = block_input.shape[1]
    quarter = block_input.shape[0]
    heads = w_forget.shape[1]
    share = w_query.shape[0]
    inner = w_output.shape[0]
    hidden_width = w_gate.shape[1]
    chips = lax.axis_size("dp") // 2
    bits = chips.bit_length() - 1
    d = lax.axis_index("dp")
    t = lax.axis_index("tensor")
    core, chip = d & 1, d >> 1
    first = core == 0
    at_home = core == t >> 1
    wide = width // chips
    half_heads = heads // 2

    def pick(one, two):
        return jnp.where(first, val(one), val(two))

    def pick_home(one, two):
        return jnp.where(at_home, val(one), val(two))

    def by_parity(mine, other):
        return pick(rows_of([mine, other]), rows_of([other, mine]))

    def reorder(rows):
        return jnp.concatenate(
            [lax.dynamic_slice_in_dim(rows, (chip ^ r) * wide, wide, 1) for r in range(chips)], axis=1
        )

    def reorder_rows(rows):
        return rows_of([lax.dynamic_slice_in_dim(rows, (chip ^ r) * wide, wide, 0) for r in range(chips)])

    planes = [[2 * k + c for k in range(chips)] for c in (0, 1)]
    up_order, down_order = list(range(bits)), list(reversed(range(bits)))

    class Pack:
        def __init__(self, mine, other):
            self.mine, self.other = mine, other

        def near(self, *others):
            self.near_other = send(hold(self.other, *others) if others else self.other, over_core)
            return self.near_other

        def cross(self, *others):
            mine, other = hold((self.mine, self.other), *others) if others else (self.mine, self.other)
            self.crossed = (send(mine, over_half), send(other, over_core_half))
            return self.crossed

        def near_rows(self):
            return by_parity(self.mine, self.near_other)

        def far_rows(self):
            return by_parity(*self.crossed)

    class Spread:
        def __init__(self, rows, order):
            self.pieces, self.order = {0: rows}, order

        def early(self):
            for bit in self.order:
                self.pieces[1 << bit] = send(self.pieces[0], over_chip(bit))
            return [self.pieces[1 << bit] for bit in self.order]

        def late(self):
            before = set(self.pieces)
            for i, bit in enumerate(self.order):
                passed = sum(1 << b for b in self.order[:i])
                for at in range(1, 1 << bits):
                    if not at & ~passed:
                        self.pieces[at | (1 << bit)] = send(self.pieces[at], over_chip(bit))
            return [v for k, v in self.pieces.items() if k not in before]

        def direct(self):
            for at in range(1, chips):
                self.pieces[at] = send(self.pieces[0], lambda d, t, at=at: (d ^ (2 * at), t))
            return [self.pieces[at] for at in range(1, chips)]

        def whole(self):
            return rows_of([self.pieces[r] for r in range(chips)])

    class Sum:
        def __init__(self, keep, give, order):
            self.order = order
            self.keep, self.give = Box(val(keep)), Box(val(give))

        def made(self):
            return self.keep, self.give

        def out(self):
            self.got = send(self.give, over_chip(self.order[0]))
            return self.got

        def rest(self):
            rows = self.keep.v.astype(F32) + self.got.v.astype(F32)
            for bit in self.order[1:]:
                if self.order == down_order:
                    cut = rows.shape[0] // 2
                    self.keep, give = Box(rows[:cut]), rows[cut:]
                else:
                    blocks = [rows[k : k + wide] for k in range(0, rows.shape[0], wide)]
                    self.keep, give = Box(rows_of(blocks[0::2])), rows_of(blocks[1::2])
                self.last = send(give.astype(BF16), over_chip(bit))
                if bit != self.order[-1]:
                    rows = self.keep.v + self.last.v.astype(F32)
            return self.last

        def own(self):
            return (self.keep.v + self.last.v.astype(F32)).astype(BF16)

    class Finish:
        def near(self, rows):
            self.mine_near, other = pick(rows[:share], rows[share:]), pick(rows[share:], rows[:share])
            self.here = send(other, over_core)
            return self.here

        def far_one(self, rows):
            mine, other = pick(rows[:share], rows[share:]), pick(rows[share:], rows[:share])
            self.other = Box(other)
            self.same = send(mine, over_half)
            return self.same

        def far_two(self):
            self.cross = send(self.other, over_core_half)
            return self.cross

        def land(self):
            mine = self.mine_near.astype(F32) + self.same.v.astype(F32)
            rest = self.here.v.astype(F32) + self.cross.v.astype(F32)
            return pick(mine, rest), pick(rest, mine)

    gain_one = attn_gain.astype(F32)[:, None]
    gain_two = mlp_gain.astype(F32)[:, None]
    part, fpart = inner // 2, half_heads
    fcut = hidden_width // 2
    lanes = ((0, 0), (0, PAIR - heads))
    forget_own = jnp.pad(lax.dynamic_slice_in_dim(w_forget, d * share, share, 0), lanes)
    one = Pack(
        *pack_one(
            core.astype(jnp.int32)[None], w_query, w_key, w_value, forget_own, attn_gain[None, :],
            jnp.pad(forget_bias[None, :], lanes),
        )
    )
    out_t, down_t = w_output.T, w_down.T
    gate_scaled, up_scaled = ((w.astype(F32) * gain_two).astype(BF16) for w in (w_gate, w_up))

    def halves_of(arrays, size):
        halves = [jnp.concatenate([w[:, h * size : (h + 1) * size] for w in arrays], axis=1) for h in (0, 1)]
        return pick(*halves), pick(*halves[::-1])

    def stay(d, t):
        return (d, t ^ 1) if (d & 1) == (t >> 1) else None

    def move(d, t):
        return (d, t ^ 1) if (d & 1) != (t >> 1) else None

    one_far = one.cross()
    one.near()
    near_one = Spread(one.near_rows(), up_order)
    near_early = near_one.early()
    x_own, cot_own = Box(reorder(block_input)), Box(reorder(cotangent))

    x_stay = send(x_own, stay)

    hold(x_own, one_far, near_early, x_stay)
    x_home = send(x_own, to_home)
    cot_stay = send(hold(cot_own, x_own), stay)
    far_one = Spread(one.far_rows(), down_order)
    far_early = far_one.early()
    near_late = near_one.late()
    wo = Pack(*halves_of([out_t], part))
    feed_pack = Pack(*halves_of([gate_scaled, up_scaled, down_t], fcut))
    gate_pack, down_pack = Pack(*halves_of([gate_scaled, up_scaled], fcut)), Pack(*halves_of([down_t], fcut))

    hold(x_home, far_early, cot_stay)
    x_move = send(x_home, move)
    x_core = send(x_home, over_core)
    far_late = far_one.late()
    wo_far = wo.cross(x_home)
    wo.near(x_home)
    seg_other = send(hold(segment_ids, x_home), over_core)
    feed_pack.near(x_home)
    near_all = Box(
        lax.all_gather(feed_pack.near_rows(), "dp", axis=0, tiled=True, axis_index_groups=planes)
    )
    seg_row = Box(pick_home(segment_ids, seg_other))
    far_bias = far_one.pieces[0][0, 4 * PAIR + HEAD + fpart + 1 :].astype(F32)
    bias_far = far_bias[:fpart] + far_bias[fpart : 2 * fpart] + far_bias[2 * fpart : 3 * fpart]
    spare = jnp.zeros((HEAD - fpart,), F32)
    bias = Box(jnp.concatenate([pick(forget_bias[:fpart], forget_bias[fpart:]), spare, bias_far, spare])[None, :])
    place = (t & 1) + 2 * core
    pos = jnp.stack([((a ^ place) >> 1) | (((a ^ place) & 1) << 1) for a in range(4)]).astype(jnp.int32)
    wa = Box(near_one.whole())

    hold(x_move, wa, bias, seg_row)
    hold(x_move, far_late, wo_far)
    x_z = Box(pick_home(x_stay, x_move))
    x_both = send(x_z, over_core)
    wb = Box(far_one.whole())
    hold(x_both, wb, x_core)
    wo_a, wo_b = wo.near_rows(), wo.far_rows()
    wo_rows = jnp.concatenate([wo_a[:, :PAIR], wo_b[:, :PAIR], wo_a[:, PAIR:], wo_b[:, PAIR:]], axis=1)
    wo_spread = Spread(wo_rows, up_order)
    wo_sent = wo_spread.direct()
    gate_far = gate_pack.cross(x_both)
    qcols = wa.v.shape[1]

    resid = x_home.v.astype(F32)
    first_scale = unit_rows(resid)[1]
    seg_col = seg_row.v.reshape(-1, 1)
    mixed, x_hat, qkv, logit, lse, cum = attend(
        pos, [x_home.v, x_core.v, x_z.v, x_both.v], wa.v, wb.v, bias.v, seg_row.v, seg_col
    )
    mixed = hold(mixed, wo_sent, gate_far)
    wo_t = wo_spread.whole()

    def half(array, which):
        rows = array.shape[0] // 2
        return array[which * rows : (which + 1) * rows]

    order = {}

    def scatter_group(far, near, at_far=lambda far_sum: None, at_near=lambda near_sum: None, at_end=lambda: (), after_far=None, late_core=False):
        rows = far()
        far_in = send(rows[quarter:].astype(BF16), over_core)
        far_sum = Box((rows[:quarter].astype(F32) + far_in.v.astype(F32)).astype(BF16))
        at_far(far_sum)
        far_got = send(far_sum, over_z)
        rows = Box(near())
        if late_core:
            hold(far_got, rows)
            if after_far:
                after_far(far_got)
            hold(rows, far_got)
        near_in = send(rows.v[quarter:].astype(BF16), over_core)
        near_sum = Box(rows.v[:quarter].astype(F32) + near_in.v.astype(F32))
        at_near(near_sum)
        hold(far_got, near_sum)
        if at_end():
            hold(far_got, at_end())
        return near_sum.v + far_got.v.astype(F32)

    sent = {}

    def weights_on(near_sum):
        sent["gate"] = Spread(gate_pack.far_rows(), up_order)
        sent["early"] = sent["gate"].early()
        sent["down"] = down_pack.cross(near_sum)

    mixed = Box(mixed)
    hidden_res = Box(
        resid
        + scatter_group(
            lambda: nt(half(mixed.v, 1), wo_t),
            lambda: nt(half(mixed.v, 0), wo_t),
            lambda far_sum: hold(far_sum, mixed),
            weights_on,
            lambda: (sent["early"], sent["down"]),
        )
    )
    far_gate = sent["gate"]
    second, second_scale = unit_rows(hidden_res.v)
    second_low = Box(second.astype(BF16))
    second_z = send(second_low, over_z)
    second_core = send(second_low, over_core)
    gate_late = far_gate.late()
    far_down = Spread(down_pack.far_rows(), down_order)
    down_early = far_down.early()
    cot_home = send(hold(cot_own, second_core), to_home)
    hold(near_all, second_core)
    gates_a = Box(reorder_rows(near_all.v[:, : 2 * fcut]))
    downs_a = Box(reorder_rows(near_all.v[:, 2 * fcut :]))
    hold(second_z, gates_a, downs_a)
    hold(second_z, cot_home, gate_late, down_early)
    second_both = send(second_z, over_core)
    cot_move = send(cot_home, move)
    down_late = far_down.late()
    cot_core = send(cot_home, over_core)
    gates_b = Box(far_gate.whole())
    hold(cot_move, second_both, gates_b)
    hold(cot_move, down_late)
    downs_b = Box(far_down.whole())
    cot_z = Box(pick_home(cot_stay, cot_move))
    cot_both = send(cot_z, over_core)
    hold(cot_both, cot_core)

    feed_weights = (gates_a.v, gates_b.v, downs_a.v, downs_b.v)
    made = {}

    def feed_far():
        made["far"] = feed_tokens((second_z.v, second_both.v), (cot_z.v, cot_both.v), feed_weights, 1)
        return made["far"][5]

    def feed_near():
        made["near"] = feed_tokens(
            (second_low.v, second_core.v), (cot_home.v, cot_core.v), feed_weights, 0, made["far"][:5]
        )
        return made["near"][5]

    grad_second = scatter_group(feed_far, feed_near, lambda far_sum: hold(far_sum, second_low, second_core), late_core=True)
    gain_two_part = made["far"][6] + made["near"][6]
    grad_res = Box(cot_home.v.astype(F32) + unit_back(hidden_res.v, second_scale, grad_second))
    branch = Box(grad_res.v.astype(BF16))
    laid = [Box(m) for m in made["near"][:5]]
    hold(branch, laid)
    branch_z = send(branch, over_z)
    hidden, grads_a, grads_b, second_all, cot_all = (m.v for m in laid)
    *b_rows, a_part, mlp_rows = (
        Box(m)
        for m in feed_grads(
            chip.astype(jnp.int32)[None], second_all, cot_all, hidden, grads_a, grads_b, downs_a.v, downs_b.v, chips
        )
    )
    hold(branch_z, b_rows, a_part, mlp_rows)
    hold(branch, branch_z)
    branch_both = send(branch_z, over_core)
    branch_core = send(branch, over_core)
    gb, db = Sum(*b_rows[:2], down_order), Sum(*b_rows[2:], up_order)
    b_out = [gb.out(), db.out()]
    branch_all = Box(rows_of([branch, branch_core, branch_z, branch_both]))

    grad_mixed = Box(nn(branch_all.v, wo_t).astype(BF16))
    mlp_out = Box(scatter_group(lambda: half(mlp_rows.v, 1), lambda: half(mlp_rows.v, 0)))
    hold(branch_all, grad_mixed)
    o_sum = Sum(*halves_apart(tn(branch_all.v, mixed.v).astype(BF16)), down_order)
    o_out = o_sum.out()
    hold(grad_mixed, o_sum.keep)
    grad_near, grad_far, grad_bias = attend_back(
        pos, qkv, logit, seg_row.v, seg_col, lse, cum, grad_mixed.v, qcols, quarter
    )
    grad_near, grad_far, x_hat = Box(grad_near), Box(grad_far), Box(x_hat)
    hold(grad_near, grad_far, b_out, mlp_out)
    out_home = (hidden_res.v + mlp_out.v).astype(BF16)
    out_sent = send(out_home, swap_home)
    b_late = [gb.rest(), db.rest()]
    first_parts = {}
    feed_end = Finish()

    def first_part(which):
        first_parts[which] = nt(half(grad_near.v, which), wa.v) + nt(half(grad_far.v, which), wb.v)
        return first_parts[which]

    def first_near():
        rows = Box(first_part(0))
        hold(x_hat, rows)
        made["grads"] = [Box(g) for g in first_grads(x_hat.v, grad_near.v, grad_far.v, chips)]
        return rows.v

    grad_first = Box(
        scatter_group(
            lambda: first_part(1),
            first_near,
            lambda far_sum: hold(far_sum, grad_near, grad_far, x_hat),
            after_far=lambda far_got: hold(far_got, b_late, out_sent, made["grads"]),
            late_core=True,
        )
    )
    grads = made["grads"]
    qa, qb, gate_cols = Sum(*grads[:2], down_order), Sum(*grads[2:4], up_order), grads[4]
    hold(a_part, grad_first)
    a_own = Box(
        lax.psum_scatter(a_part.v, "dp", scatter_dimension=0, tiled=True, axis_index_groups=planes)
    )
    b_same = feed_end.far_one(jnp.concatenate([gb.own(), db.own()], axis=1))
    q_out = [qa.out(), qb.out()]
    back_home = Box((grad_res.v + unit_back(resid, first_scale, grad_first.v)).astype(BF16))
    back_sent = send(back_home, swap_home)

    hold(gate_cols, back_home)
    forget = jnp.concatenate([gate_cols.v[:, k * PAIR + HEAD : k * PAIR + HEAD + fpart] for k in (0, 1)], axis=1).T
    gain_part = functools.reduce(
        jnp.add, [jnp.sum(half(x_hat.v, w).astype(F32) * first_parts[w], axis=0) for w in (0, 1)]
    )
    gain_row = wa.v[:, 3 * part + fpart].astype(F32)
    small = reorder(jnp.concatenate([forget * gain_row[None, :], gain_part[None], gain_two_part], axis=0))
    small = Box(jnp.concatenate([small, jnp.pad(grad_bias, ((0, 0), (0, width - PAIR)))], axis=0))
    small_there = send(small, over_chip(0))

    hold(small, q_out, small_there, o_out, b_same)
    q_late = [qa.rest(), qb.rest()]
    o_late = o_sum.rest()
    hold(feed_end.other, small)
    b_cross = feed_end.far_two()
    small = Box(small.v + small_there.v)
    hold(small, q_late, o_late, back_sent)
    for bit in range(1, bits):
        small = Box(small.v + send(small, over_chip(bit)).v)
    near, far = small.v[:fpart], small.v[fpart:heads]
    gains, bias_sum = small.v[heads : heads + 2], small.v[heads + 2 :]
    spread_out = ((0, 0), (0, width - fpart))
    bias_near, bias_far = (jnp.pad(bias_sum[:, k * HEAD : k * HEAD + fpart], spread_out) for k in (0, 1))
    far_small = Box(jnp.concatenate([far, bias_far, gains], axis=0))
    hold(far_small, q_late, o_late)
    got = send(far_small, over_half)

    own_out = o_sum.own()
    out_halves = [
        jnp.concatenate(
            [own_out[:, h * PAIR : (h + 1) * PAIR], own_out[:, 2 * PAIR + h * HEAD : 2 * PAIR + (h + 1) * HEAD]], axis=1
        )
        for h in (0, 1)
    ]
    q_end = Finish()
    q_same = q_end.far_one(jnp.concatenate([qb.own(), out_halves[1]], axis=1))
    q_cross = q_end.far_two()
    q_here = q_end.near(jnp.concatenate([qa.own(), out_halves[0]], axis=1))
    hold(a_own, q_same)
    feed_end.near(a_own.v)
    hold(got, q_here, b_cross)
    mine = jnp.concatenate(
        [near + got.v[:fpart], bias_near + got.v[fpart : fpart + 1], gains + got.v[fpart + 1 :]], axis=0
    )
    rest = send(mine, over_core).v
    grad_forget = pick(rows_of([mine[:fpart], rest[:fpart]]), rows_of([rest[:fpart], mine[:fpart]])).T
    bias_mine, bias_rest = mine[fpart, :fpart], rest[fpart, :fpart]
    grad_bias_out = pick(jnp.concatenate([bias_mine, bias_rest]), jnp.concatenate([bias_rest, bias_mine]))
    gains = mine[fpart + 1 :] + rest[fpart + 1 :]
    gains = lax.dynamic_slice_in_dim(gains, d * share, share, 1)
    gains = gains + send(gains, over_z).v
    grad_gain_one = gains[0] / attn_gain.astype(F32)
    grad_gain_two = gains[1] / mlp_gain.astype(F32)
    f_zero, f_one = feed_end.land()
    gate_sum, up_sum, down_sum = (
        jnp.concatenate([f[:, k * fcut : (k + 1) * fcut] for f in (f_zero, f_one)], axis=1) for k in range(3)
    )
    done = [Box(v) for v in (gate_sum * gain_two, up_sum * gain_two, down_sum.T, grad_gain_one, grad_gain_two)]
    hold(q_same, done)
    hold(q_cross, q_same)
    gate_out, up_out, down_out, grad_gain_one, grad_gain_two = (b.v for b in done)
    input_grad = reorder(pick_home(back_home, back_sent)).astype(F32)
    output = reorder(pick_home(out_home, out_sent))
    q_zero, q_one = q_end.land()

    def joined(k):
        if k == 3:
            return jnp.concatenate([q_zero[:, qcols:], q_one[:, qcols:]], axis=1)
        lone = slice(3 * PAIR + k * HEAD, 3 * PAIR + (k + 1) * HEAD)
        pair = slice(k * PAIR, (k + 1) * PAIR)
        return jnp.concatenate([q_zero[:, pair], q_zero[:, lone], q_one[:, pair], q_one[:, lone]], axis=1)

    q_sums = [joined(k) for k in range(4)]

    return (
        output,
        input_grad,
        grad_gain_one,
        q_sums[0] * gain_one,
        q_sums[1] * gain_one,
        q_sums[2] * gain_one,
        grad_forget,
        grad_bias_out,
        q_sums[3].T,
        grad_gain_two,
        gate_out,
        up_out,
        down_out,
    )


def solution(mesh):
    return jax.shard_map(
        per_device,
        mesh=mesh,
        in_specs=(
            P(("dp", "tensor"), None),
            P("dp"),
            P("dp", "tensor"),
            P("dp", "tensor"),
            P("dp", "tensor"),
            P(None, "tensor"),
            P("tensor"),
            P("tensor", "dp"),
            P("dp"),
            P("dp", "tensor"),
            P("dp", "tensor"),
            P("tensor", "dp"),
            P("dp", None),
            P(("dp", "tensor"), None),
        ),
        out_specs=(
            P(("dp", "tensor"), None),
            P(("dp", "tensor"), None),
            P("dp"),
            P("dp", "tensor"),
            P("dp", "tensor"),
            P("dp", "tensor"),
            P(None, "tensor"),
            P("tensor"),
            P("tensor", "dp"),
            P("dp"),
            P("dp", "tensor"),
            P("dp", "tensor"),
            P("tensor", "dp"),
        ),
        check_vma=False,
    )
```

```python
import functools

import jax
import jax.numpy as jnp
from jax import lax
from jax.experimental import pallas as pl
from jax.experimental.pallas import tpu as pltpu
from jax.sharding import PartitionSpec as P

HEAD = 64
PAIR = 2 * HEAD
EPS = 1e-06
F32 = jnp.float32
BF16 = jnp.bfloat16
NT = (((1,), (1,)), ((), ()))
TN = (((0,), (0,)), ((), ()))
AXES = ("dp", "tensor")


def nn(a, b):
    return jnp.dot(a, b, preferred_element_type=F32)


def nt(a, b):
    return lax.dot_general(a, b, NT, preferred_element_type=F32)


def tn(a, b):
    return lax.dot_general(a, b, TN, preferred_element_type=F32)


class Box:
    def __init__(self, v):
        self.v = v


def val(value):
    return value.v if isinstance(value, Box) else value


def boxes(tree):
    if isinstance(tree, Box):
        return [tree]
    assert isinstance(tree, (list, tuple)), type(tree)
    return [b for item in tree for b in boxes(item)]


def send(value, move):
    tensor = lax.axis_size("tensor")
    pairs = []
    for d in range(lax.axis_size("dp")):
        for t in range(tensor):
            to = move(d, t)
            if to is not None:
                pairs.append((d * tensor + t, to[0] * tensor + to[1]))
    return Box(lax.ppermute(val(value), AXES, pairs))


def to_home(d, t):
    return (d ^ 1, t ^ 2) if (d & 1) != (t >> 1) else (d, t)


def swap_home(d, t):
    return (d ^ 1, t ^ 2) if (d & 1) != (t >> 1) else None


def over_core(d, t):
    return (d ^ 1, t)


def over_z(d, t):
    return (d, t ^ 1)


def over_chip(bit):
    return lambda d, t: (d ^ (2 << bit), t)


def over_half(d, t):
    return (d, t ^ 2)


def over_core_half(d, t):
    return (d ^ 1, t ^ 2)


def hold(value, *others):
    held = boxes(others)
    result, new = lax.optimization_barrier((jax.tree.map(val, value, is_leaf=lambda x: isinstance(x, Box)), [b.v for b in held]))
    for b, v in zip(held, new):
        b.v = v
    if isinstance(value, Box):
        value.v = result
        return value
    return result


def meet(critical, *others):
    return hold(hold(critical), *others)


def rows_of(pieces):
    return jnp.concatenate([val(p) for p in pieces], axis=0)


def block_of(pos_ref, at, size):
    return pl.ds(pl.multiple_of(pos_ref[at] * size, size), size)


def lane_of(pair, h):
    return jnp.where(pair == 2, 2 + HEAD * h, HEAD * pair + h)


def pack_kernel(core_ref, query_ref, key_ref, value_ref, forget_ref, gain_ref, bias_ref, mine_ref, other_ref):
    share = gain_ref.shape[1]
    diagonal = lax.broadcasted_iota(jnp.int32, (share, share), 0) == lax.broadcasted_iota(jnp.int32, (share, share), 1)
    gain = jnp.sum(jnp.where(diagonal, gain_ref[...].astype(F32), 0.0), axis=1, keepdims=True)
    lane = lax.broadcasted_iota(jnp.int32, (share, PAIR), 1)
    low_lanes = lane < HEAD
    first = core_ref[0] == 0
    parts = [ref[...].astype(F32) * gain for ref in (query_ref, key_ref, value_ref)]
    forget = forget_ref[...].astype(F32) * gain
    bias = bias_ref[...]
    pieces = []
    for _ in range(3):
        piece = bias.astype(BF16).astype(F32)
        pieces.append(piece)
        bias = bias - piece
    halves = []
    for h in range(2):
        three = [p if h == 0 else pltpu.roll(p, p.shape[1] // 2, 1) for p in parts]
        tiles = [p[:, :PAIR] for p in three]
        lone = [p[:, PAIR : 2 * PAIR] for p in three]
        tiles.append(jnp.where(low_lanes, lone[0], pltpu.roll(lone[1], HEAD, 1)))
        rest = jnp.where(lane < HEAD + 3, pltpu.roll(forget, HEAD - 3 * h, 1), gain)
        for k, piece in enumerate(pieces):
            at = HEAD + 4 + 3 * k
            moved = jnp.broadcast_to(pltpu.roll(piece, at - 3 * h, 1), (share, PAIR))
            rest = jnp.where((lane >= at) & (lane < at + 3), moved, rest)
        rest = jnp.where(lane < HEAD + 13, rest, 0.0)
        tiles.append(jnp.where(low_lanes, lone[2], rest))
        halves.append(tiles)
    for k in range(5):
        at = slice(k * PAIR, (k + 1) * PAIR)
        mine_ref[:, at] = jnp.where(first, halves[0][k], halves[1][k]).astype(BF16)
        other_ref[:, at] = jnp.where(first, halves[1][k], halves[0][k]).astype(BF16)


def forward_kernel(
    quarter, pos_ref, x0_ref, x1_ref, x2_ref, x3_ref, wa_ref, wb_ref, bias_ref, segr_ref, segc_ref,
    mixed_ref, xhat_ref, qkv_ref, logit_ref, lse_ref, cum_ref, cumr_ref, rel_ref,
):
    pair = pl.program_id(0)
    width = 3 * PAIR
    lane = lax.broadcasted_iota(jnp.int32, (quarter, PAIR), 1)
    low_lanes = lane < HEAD
    count = segr_ref.shape[1] // quarter

    @pl.when(pair == 0)
    def _():
        for r, x_ref in enumerate((x0_ref, x1_ref, x2_ref, x3_ref)):
            at = slice(r * quarter, (r + 1) * quarter)
            x = x_ref[...].astype(F32)
            low = (x * lax.rsqrt(jnp.mean(x * x, axis=1, keepdims=True) + EPS)).astype(BF16)
            xhat_ref[at, :] = low
            near_all = nn(low, wa_ref[...])
            far_all = nn(low, wb_ref[...])

            def near(k):
                return near_all[:, k * PAIR : (k + 1) * PAIR]

            def far(k):
                return far_all[:, k * PAIR : (k + 1) * PAIR]

            for k in range(3):
                qkv_ref[at, k * width : k * width + PAIR] = near(k).astype(BF16)
                qkv_ref[at, k * width + PAIR : k * width + 2 * PAIR] = far(k).astype(BF16)

            def both(one, two):
                return jnp.where(low_lanes, one, two).astype(BF16)

            qkv_ref[at, 2 * PAIR : 3 * PAIR] = both(near(3), pltpu.roll(far(3), HEAD, 1))
            qkv_ref[at, width + 2 * PAIR : width + 3 * PAIR] = both(pltpu.roll(near(3), HEAD, 1), far(3))
            qkv_ref[at, 2 * width + 2 * PAIR : 2 * width + 3 * PAIR] = both(near(4), pltpu.roll(far(4), HEAD, 1))
            rel_ref[at, :] = jnp.where(low_lanes, pltpu.roll(near(4), HEAD, 1), far(4)) + bias_ref[...]
        rows = lax.broadcasted_iota(jnp.int32, (quarter, quarter), 0)
        cols = lax.broadcasted_iota(jnp.int32, (quarter, quarter), 1)
        lower = (cols <= rows).astype(F32)
        carry = jnp.zeros((1, PAIR), F32)
        for a in range(count):
            logit = rel_ref[block_of(pos_ref, a, quarter), :]
            here = slice(a * quarter, (a + 1) * quarter)
            logit_ref[here, :] = logit
            logsig = jnp.minimum(logit, 0.0) - jnp.log1p(jnp.exp(-jnp.abs(logit)))
            cum = jnp.dot(lower, logsig, precision=lax.Precision.HIGHEST, preferred_element_type=F32) + carry
            carry = cum[quarter - 1 :, :]
            cum_ref[here, :] = cum
            cumr_ref[:, here] = cum.T
        lse_ref[...] = jnp.zeros(lse_ref.shape, F32)

    def columns(part):
        return pl.ds(pl.multiple_of(part * width + pair * PAIR, PAIR), PAIR)

    diag_rows = lax.broadcasted_iota(jnp.int32, (quarter, quarter), 0)
    diag_cols = lax.broadcasted_iota(jnp.int32, (quarter, quarter), 1)
    for a in range(count):
        query = (qkv_ref[block_of(pos_ref, a, quarter), columns(0)] * 0.125).astype(BF16)
        seg_q = segc_ref[a * quarter : (a + 1) * quarter, :]
        spans = range(max(0, a - 512 // quarter), a + 1)
        outs = []
        for h in range(2):
            head = lane_of(pair, h)
            mine = (lane >= HEAD) if h else low_lanes
            query_h = jnp.where(mine, query, jnp.zeros_like(query))
            scores = []
            for b in spans:
                keys = qkv_ref[block_of(pos_ref, b, quarter), columns(1)]
                s = nt(query_h, keys) - cumr_ref[pl.ds(head, 1), b * quarter : (b + 1) * quarter]
                allowed = seg_q == segr_ref[:, b * quarter : (b + 1) * quarter]
                if a == b:
                    allowed &= diag_cols <= diag_rows
                scores.append(jnp.where(allowed, s, -jnp.inf))
            top = functools.reduce(jnp.maximum, [jnp.max(s, axis=1, keepdims=True) for s in scores])
            expd = [jnp.exp(s - top) for s in scores]
            total = functools.reduce(jnp.add, [jnp.sum(e, axis=1, keepdims=True) for e in expd])
            scale = 1.0 / total
            out = None
            for e, b in zip(expd, spans):
                values = qkv_ref[block_of(pos_ref, b, quarter), columns(2)]
                part = nn((e * scale).astype(BF16), values)
                out = part if out is None else out + part
            outs.append(out)
            lse = top + jnp.log(total)
            at = pl.ds(a * quarter, quarter)
            lse_ref[at, :] = jnp.where(lane == head, lse, lse_ref[at, :])
        mixed_ref[block_of(pos_ref, a, quarter), columns(0)] = jnp.where(low_lanes, outs[0], outs[1]).astype(BF16)


def backward_kernel(
    quarter, pos_ref, qkv_ref, logit_ref, segr_ref, segc_ref, lse_ref, cum_ref, gmix_ref,
    gnear_ref, gfar_ref, gbias_ref, lser_ref, gcol_ref, grow_ref, grad_ref, gk_ref, gv_ref,
):
    pair = pl.program_id(0)
    pairs = pl.num_programs(0)
    width = 3 * PAIR
    lane = lax.broadcasted_iota(jnp.int32, (quarter, PAIR), 1)
    low_lanes = lane < HEAD
    count = segr_ref.shape[1] // quarter

    @pl.when(pair == 0)
    def _():
        for a in range(count):
            at = slice(a * quarter, (a + 1) * quarter)
            lser_ref[:, at] = lse_ref[at, :].T
        gcol_ref[...] = jnp.zeros(gcol_ref.shape, F32)
        grow_ref[...] = jnp.zeros(grow_ref.shape, F32)

    def columns(part):
        return pl.ds(pl.multiple_of(part * width + pair * PAIR, PAIR), PAIR)

    diag_rows = lax.broadcasted_iota(jnp.int32, (quarter, quarter), 0)
    diag_cols = lax.broadcasted_iota(jnp.int32, (quarter, quarter), 1)
    gk_ref[...] = jnp.zeros(gk_ref.shape, F32)
    gv_ref[...] = jnp.zeros(gv_ref.shape, F32)
    for a in range(count):
        here = slice(a * quarter, (a + 1) * quarter)
        query = (qkv_ref[block_of(pos_ref, a, quarter), columns(0)] * 0.125).astype(BF16)
        gout = gmix_ref[block_of(pos_ref, a, quarter), columns(0)]
        seg_q = segr_ref[:, here]
        spans = range(max(0, a - 512 // quarter), a + 1)
        grad_query = None
        for h in range(2):
            head = lane_of(pair, h)
            mine = (lane >= HEAD) if h else low_lanes
            query_h = jnp.where(mine, query, jnp.zeros_like(query))
            gout_h = jnp.where(mine, gout, jnp.zeros_like(gout))
            lse = lser_ref[pl.ds(head, 1), here]
            probs, gprobs = [], []
            inner = None
            for b in spans:
                there = slice(b * quarter, (b + 1) * quarter)
                keys = qkv_ref[block_of(pos_ref, b, quarter), columns(1)]
                values = qkv_ref[block_of(pos_ref, b, quarter), columns(2)]
                cum_k = jnp.sum(jnp.where(lane == head, cum_ref[there, :], 0.0), axis=1, keepdims=True)
                s = nt(keys, query_h) - cum_k
                allowed = segc_ref[there, :] == seg_q
                if a == b:
                    allowed &= diag_rows <= diag_cols
                p = jnp.where(allowed, jnp.exp(s - lse), 0.0)
                g = nt(values, gout_h)
                probs.append(p)
                gprobs.append(g)
                part = jnp.sum(p * g, axis=0, keepdims=True)
                inner = part if inner is None else inner + part
            row_sum = None
            for p, g, b in zip(probs, gprobs, spans):
                there = slice(b * quarter, (b + 1) * quarter)
                keys = (qkv_ref[block_of(pos_ref, b, quarter), columns(1)] * 0.125).astype(BF16)
                keys_h = jnp.where(mine, keys, jnp.zeros_like(keys))
                gs = p * (g - inner)
                part = jnp.sum(gs, axis=0, keepdims=True)
                row_sum = part if row_sum is None else row_sum + part
                col_sum = jnp.sum(gs, axis=1, keepdims=True)
                gcol_ref[there, :] += jnp.where(lane == head, col_sum, 0.0)
                low = gs.astype(BF16)
                gk_ref[there, :] += nn(low, query_h)
                gv_ref[there, :] += nn(p.astype(BF16), gout_h)
                part = tn(low, keys_h)
                grad_query = part if grad_query is None else grad_query + part
            grow_ref[pl.ds(head, 1), here] = row_sum
        grad_ref[block_of(pos_ref, a, quarter), columns(0)] = grad_query
    for a in range(count):
        here = slice(a * quarter, (a + 1) * quarter)
        grad_ref[block_of(pos_ref, a, quarter), columns(1)] = gk_ref[here, :]
        grad_ref[block_of(pos_ref, a, quarter), columns(2)] = gv_ref[here, :]

    @pl.when(pair == pairs - 1)
    def _():
        upper = (diag_cols >= diag_rows).astype(F32)
        carry = jnp.zeros((1, PAIR), F32)
        bias = jnp.zeros((1, PAIR), F32)
        real = (lane % HEAD) < pairs
        for a in reversed(range(count)):
            here = slice(a * quarter, (a + 1) * quarter)
            at = block_of(pos_ref, a, quarter)
            logit = logit_ref[here, :]
            gcum = jnp.where(real, grow_ref[:, here].T - gcol_ref[here, :], 0.0)
            back = jnp.dot(upper, gcum, precision=lax.Precision.HIGHEST, preferred_element_type=F32) + carry
            carry = back[:1, :]
            glogit = jnp.where(real, back * (1.0 / (1.0 + jnp.exp(logit))), 0.0)
            bias = bias + jnp.sum(glogit, axis=0, keepdims=True)

            def grad(part, k):
                return grad_ref[at, part * width + k * PAIR : part * width + (k + 1) * PAIR]

            for k in range(3):
                gnear_ref[at, k * PAIR : (k + 1) * PAIR] = grad(k, 0).astype(BF16)
                gfar_ref[at, k * PAIR : (k + 1) * PAIR] = grad(k, 1).astype(BF16)
            q_last, k_last, v_last = grad(0, 2), grad(1, 2), grad(2, 2)
            k_roll = pltpu.roll(k_last, HEAD, 1)
            gnear_ref[at, 3 * PAIR : 4 * PAIR] = jnp.where(low_lanes, q_last, k_roll).astype(BF16)
            gnear_ref[at, 4 * PAIR :] = jnp.where(low_lanes, v_last, pltpu.roll(glogit, HEAD, 1)).astype(BF16)
            gfar_ref[at, 3 * PAIR : 4 * PAIR] = jnp.where(low_lanes, pltpu.roll(q_last, HEAD, 1), k_last).astype(BF16)
            gfar_ref[at, 4 * PAIR :] = jnp.where(low_lanes, pltpu.roll(v_last, HEAD, 1), glogit).astype(BF16)
        gbias_ref[...] = bias


def full_spec(shape):
    return pl.BlockSpec(shape, lambda *_: (0,) * len(shape))


NO_COST = pl.CostEstimate(flops=0, bytes_accessed=0, transcendentals=0)


def params(mib):
    return pltpu.CompilerParams(vmem_limit_bytes=mib * 2**20, dimension_semantics=("arbitrary",))


def pack_one(core, query, keys, values, forget, gain, bias):
    share = gain.shape[1]
    out = jax.ShapeDtypeStruct((share, 5 * PAIR), BF16)
    return pl.pallas_call(
        pack_kernel,
        grid=(1,),
        out_shape=(out, out),
        in_specs=[
            pl.BlockSpec(memory_space=pltpu.SMEM),
            *(full_spec(w.shape) for w in (query, keys, values, forget, gain, bias)),
        ],
        out_specs=(full_spec(out.shape), full_spec(out.shape)),
        compiler_params=params(6),
        cost_estimate=NO_COST,
    )(core, query, keys, values, forget, gain, bias)


def attend(pos, blocks, wa, wb, bias, seg_row, seg_col):
    quarter, wide = blocks[0].shape
    length = 4 * quarter
    width = 3 * PAIR
    small = jax.ShapeDtypeStruct((length, PAIR), F32)
    outs = (
        jax.ShapeDtypeStruct((length, width), BF16),
        jax.ShapeDtypeStruct((length, wide), BF16),
        jax.ShapeDtypeStruct((length, 3 * width), BF16),
        small,
        small,
        small,
    )
    operands = (*blocks, wa, wb, bias, seg_row, seg_col)
    return pl.pallas_call(
        functools.partial(forward_kernel, quarter),
        grid=(3,),
        out_shape=outs,
        in_specs=[pl.BlockSpec(memory_space=pltpu.SMEM), *(full_spec(o.shape) for o in operands)],
        out_specs=tuple(full_spec(o.shape) for o in outs),
        scratch_shapes=[pltpu.VMEM((PAIR, length), F32), pltpu.VMEM((length, PAIR), F32)],
        compiler_params=params(27),
        cost_estimate=NO_COST,
    )(pos, *operands)


def feed_kernel(s0_ref, s1_ref, c0_ref, c1_ref, ga_ref, gb_ref, da_ref, db_ref, *refs):
    hidden_ref, grada_ref, gradb_ref, second_ref, cot_ref, back_ref, gain_ref = refs[-7:]
    cut = da_ref.shape[1]
    block = s0_ref.shape[0]
    gain = None
    for i, (s_ref, c_ref) in enumerate(((s0_ref, c0_ref), (s1_ref, c1_ref))):
        at = slice(i * block, (i + 1) * block)
        second_ref[at, :] = s_ref[...]
        cot_ref[at, :] = c_ref[...]
        back = None
        for k, (w_ref, d_ref, grad_ref) in enumerate(((ga_ref, da_ref, grada_ref), (gb_ref, db_ref, gradb_ref))):
            both = nn(s_ref[...], w_ref[...])
            grad_hidden = nn(c_ref[...], d_ref[...]).astype(BF16).astype(F32)
            gate, upper = both[:, :cut], both[:, cut:]
            sigma = 1.0 / (1.0 + jnp.exp(-gate))
            swish = gate * sigma
            hidden_ref[at, k * cut : (k + 1) * cut] = (swish * upper).astype(BF16)
            grad_gate = (grad_hidden * upper * sigma * (1.0 + gate * (1.0 - sigma))).astype(BF16)
            grad_up = (grad_hidden * swish).astype(BF16)
            grad_ref[at, :cut] = grad_gate
            grad_ref[at, cut:] = grad_up
            part = nt(grad_gate, w_ref[:, :cut]) + nt(grad_up, w_ref[:, cut:])
            back = part if back is None else back + part
        back_ref[at, :] = back
        part = jnp.sum(s_ref[...].astype(F32) * back, axis=0, keepdims=True)
        gain = part if gain is None else gain + part
    gain_ref[...] = gain


def feed_tokens(second, cot, weights, which, before=()):
    block, wide = second[0].shape
    cut = weights[2].shape[1]
    operands = (*second, *cot, *weights)
    widths = (2 * cut, 2 * cut, 2 * cut, wide, wide)
    outs = tuple(jax.ShapeDtypeStruct((4 * block, w), BF16) for w in widths)
    outs += (jax.ShapeDtypeStruct((2 * block, wide), F32), jax.ShapeDtypeStruct((1, wide), F32))
    return pl.pallas_call(
        feed_kernel,
        grid=(1,),
        out_shape=outs,
        in_specs=[*(full_spec(o.shape) for o in operands)] + [pl.BlockSpec(memory_space=pl.ANY)] * len(before),
        out_specs=(
            *(pl.BlockSpec((2 * block, w), lambda i: (which, 0)) for w in widths),
            full_spec((2 * block, wide)),
            full_spec((1, wide)),
        ),
        input_output_aliases={len(operands) + k: k for k in range(len(before))},
        compiler_params=params(28),
        cost_estimate=NO_COST,
    )(*operands, *before)


def put_half(rows, keep_ref, give_ref):
    first = pl.program_id(0) < pl.num_programs(0) // 2

    @pl.when(first)
    def _():
        keep_ref[...] = rows.astype(BF16)

    @pl.when(jnp.logical_not(first))
    def _():
        give_ref[...] = rows.astype(BF16)


def put_pair(rows, keep_ref, give_ref):
    even = pl.program_id(0) % 2 == 0

    @pl.when(even)
    def _():
        keep_ref[...] = rows.astype(BF16)

    @pl.when(jnp.logical_not(even))
    def _():
        give_ref[...] = rows.astype(BF16)


def half_specs(block, cols, half_of):
    return (
        pl.BlockSpec((block, cols), lambda r, *_: (jnp.minimum(r, half_of - 1), 0)),
        pl.BlockSpec((block, cols), lambda r, *_: (jnp.maximum(r - half_of, 0), 0)),
    )


def pair_specs(block, cols):
    return (pl.BlockSpec((block, cols), lambda r, *_: (r // 2, 0)),) * 2


def feed_grads_kernel(
    chip_ref, second_ref, cot_ref, hidden_ref, ga_ref, gb_ref, da_ref, db_ref,
    keepb_ref, giveb_ref, keepd_ref, gived_ref, outa_ref, part_ref,
):
    cut = da_ref.shape[1]
    second, cot = second_ref[...], cot_ref[...]
    put_half(tn(second, gb_ref[...]), keepb_ref, giveb_ref)
    put_pair(tn(cot, hidden_ref[:, cut:]), keepd_ref, gived_ref)
    outa_ref[:, : 2 * cut] = tn(second, ga_ref[...]).astype(BF16)
    outa_ref[:, 2 * cut :] = tn(cot, hidden_ref[:, :cut]).astype(BF16)
    part = nt(hidden_ref[:, :cut], da_ref[...]) + nt(hidden_ref[:, cut:], db_ref[...])
    part_ref[...] = part.astype(BF16)


def pairs_apart(rows, chips):
    block = rows.shape[0] // chips
    return rows_of([rows[r * block : (r + 1) * block] for r in (*range(0, chips, 2), *range(1, chips, 2))])


def halves_apart(rows):
    cut = rows.shape[0] // 2
    return rows[:cut], rows[cut:]


def feed_grads(chip, second, cot, hidden, ga, gb, da, db, chips):
    length, wide = second.shape
    block = wide // chips
    cut = da.shape[1]
    half_of = chips // 2
    if block % PAIR:
        down = tn(cot, hidden).astype(BF16)
        part = nt(hidden[:, :cut], da) + nt(hidden[:, cut:], db)
        own = jnp.concatenate([tn(second, ga).astype(BF16), down[:, :cut]], axis=1)
        own = [lax.dynamic_slice_in_dim(own, (chip[0] ^ r) * block, block, 0) for r in range(chips)]
        halves = halves_apart(tn(second, gb).astype(BF16)) + halves_apart(pairs_apart(down[:, cut:], chips))
        return *halves, rows_of(own), part.astype(BF16)
    cols = pl.BlockSpec((length, block), lambda r, chip: (0, r))
    rows = pl.BlockSpec((block, cut), lambda r, chip: (r, 0))
    return pl.pallas_call(
        feed_grads_kernel,
        out_shape=(
            *(jax.ShapeDtypeStruct((wide // 2, 2 * cut), BF16),) * 2,
            *(jax.ShapeDtypeStruct((wide // 2, cut), BF16),) * 2,
            jax.ShapeDtypeStruct((wide, 3 * cut), BF16),
            jax.ShapeDtypeStruct((length, wide), BF16),
        ),
        grid_spec=pltpu.PrefetchScalarGridSpec(
            num_scalar_prefetch=1,
            grid=(chips,),
            in_specs=[cols, cols, *(full_spec(o.shape) for o in (hidden, ga, gb)), rows, rows],
            out_specs=(
                *half_specs(block, 2 * cut, half_of),
                *pair_specs(block, cut),
                pl.BlockSpec((block, 3 * cut), lambda r, chip: (r ^ chip[0], 0)),
                pl.BlockSpec((length, block), lambda r, chip: (0, r)),
            ),
        ),
        compiler_params=params(26),
        cost_estimate=NO_COST,
    )(chip, second, cot, hidden, ga, gb, da, db)


def first_grads_kernel(x_ref, near_ref, far_ref, keepn_ref, given_ref, keepf_ref, givef_ref, gate_ref):
    x = x_ref[...]
    near, far = tn(x, near_ref[...]), tn(x, far_ref[...])
    put_half(near, keepn_ref, given_ref)
    put_pair(far, keepf_ref, givef_ref)
    gate_ref[:, :PAIR] = near[:, 4 * PAIR :]
    gate_ref[:, PAIR:] = far[:, 4 * PAIR :]


def first_grads(x_hat, near, far, chips):
    length, wide = x_hat.shape
    block = wide // chips
    cols = near.shape[1]
    half_of = chips // 2
    if block % PAIR:
        near, far = tn(x_hat, near), tn(x_hat, far)
        gate = jnp.concatenate([near[:, 4 * PAIR :], far[:, 4 * PAIR :]], axis=1)
        return *halves_apart(near.astype(BF16)), *halves_apart(pairs_apart(far.astype(BF16), chips)), gate
    return pl.pallas_call(
        first_grads_kernel,
        grid=(chips,),
        out_shape=(
            *(jax.ShapeDtypeStruct((wide // 2, cols), BF16),) * 4,
            jax.ShapeDtypeStruct((wide, 2 * PAIR), F32),
        ),
        in_specs=[pl.BlockSpec((length, block), lambda r: (0, r)), full_spec(near.shape), full_spec(far.shape)],
        out_specs=(
            *half_specs(block, cols, half_of),
            *pair_specs(block, cols),
            pl.BlockSpec((block, 2 * PAIR), lambda r: (r, 0)),
        ),
        compiler_params=params(14),
        cost_estimate=NO_COST,
    )(x_hat, near, far)


def attend_back(pos, qkv, logit, seg_row, seg_col, lse, cum, grad_mixed, cols, quarter):
    length = qkv.shape[0]
    grads = jax.ShapeDtypeStruct((length, cols), BF16)
    return pl.pallas_call(
        functools.partial(backward_kernel, quarter),
        grid=(3,),
        out_shape=(grads, grads, jax.ShapeDtypeStruct((1, PAIR), F32)),
        in_specs=[
            pl.BlockSpec(memory_space=pltpu.SMEM),
            full_spec(qkv.shape),
            full_spec(logit.shape),
            full_spec(seg_row.shape),
            full_spec(seg_col.shape),
            full_spec(lse.shape),
            full_spec(cum.shape),
            full_spec(grad_mixed.shape),
        ],
        out_specs=(full_spec((length, cols)), full_spec((length, cols)), full_spec((1, PAIR))),
        scratch_shapes=[
            pltpu.VMEM((PAIR, length), F32),
            pltpu.VMEM((length, PAIR), F32),
            pltpu.VMEM((PAIR, length), F32),
            pltpu.VMEM((length, 9 * PAIR), F32),
            pltpu.VMEM((length, PAIR), F32),
            pltpu.VMEM((length, PAIR), F32),
        ],
        compiler_params=params(28),
        cost_estimate=NO_COST,
    )(pos, qkv, logit, seg_row, seg_col, lse, cum, grad_mixed)


def unit_rows(value):
    scale = lax.rsqrt(jnp.mean(value * value, axis=-1, keepdims=True) + EPS)
    return value * scale, scale


def unit_back(value, scale, weighted):
    inner = jnp.mean(weighted * value, axis=-1, keepdims=True)
    return scale * weighted - value * (scale * scale * scale) * inner


def per_device(
    block_input, attn_gain, w_query, w_key, w_value, w_forget, forget_bias, w_output,
    mlp_gain, w_gate, w_up, w_down, segment_ids, cotangent,
):
    width = block_input.shape[1]
    quarter = block_input.shape[0]
    heads = w_forget.shape[1]
    share = w_query.shape[0]
    inner = w_output.shape[0]
    hidden_width = w_gate.shape[1]
    chips = lax.axis_size("dp") // 2
    bits = chips.bit_length() - 1
    d = lax.axis_index("dp")
    t = lax.axis_index("tensor")
    core, chip = d & 1, d >> 1
    first = core == 0
    at_home = core == t >> 1
    wide = width // chips
    half_heads = heads // 2

    def pick(one, two):
        return jnp.where(first, val(one), val(two))

    def pick_home(one, two):
        return jnp.where(at_home, val(one), val(two))

    def by_parity(mine, other):
        return pick(rows_of([mine, other]), rows_of([other, mine]))

    def reorder(rows):
        return jnp.concatenate(
            [lax.dynamic_slice_in_dim(rows, (chip ^ r) * wide, wide, 1) for r in range(chips)], axis=1
        )

    def reorder_rows(rows):
        return rows_of([lax.dynamic_slice_in_dim(rows, (chip ^ r) * wide, wide, 0) for r in range(chips)])

    planes = [[2 * k + c for k in range(chips)] for c in (0, 1)]
    up_order, down_order = list(range(bits)), list(reversed(range(bits)))

    class Pack:
        def __init__(self, mine, other):
            self.mine, self.other = mine, other

        def near(self, *others):
            self.near_other = send(hold(self.other, *others) if others else self.other, over_core)
            return self.near_other

        def cross(self, *others):
            mine, other = hold((self.mine, self.other), *others) if others else (self.mine, self.other)
            self.crossed = (send(mine, over_half), send(other, over_core_half))
            return self.crossed

        def near_rows(self):
            return by_parity(self.mine, self.near_other)

        def far_rows(self):
            return by_parity(*self.crossed)

    class Spread:
        def __init__(self, rows, order):
            self.pieces, self.order = {0: rows}, order

        def early(self):
            for bit in self.order:
                self.pieces[1 << bit] = send(self.pieces[0], over_chip(bit))
            return [self.pieces[1 << bit] for bit in self.order]

        def late(self):
            before = set(self.pieces)
            for i, bit in enumerate(self.order):
                passed = sum(1 << b for b in self.order[:i])
                for at in range(1, 1 << bits):
                    if not at & ~passed:
                        self.pieces[at | (1 << bit)] = send(self.pieces[at], over_chip(bit))
            return [v for k, v in self.pieces.items() if k not in before]

        def direct(self):
            for at in range(1, chips):
                self.pieces[at] = send(self.pieces[0], lambda d, t, at=at: (d ^ (2 * at), t))
            return [self.pieces[at] for at in range(1, chips)]

        def whole(self):
            return rows_of([self.pieces[r] for r in range(chips)])

    class Sum:
        def __init__(self, keep, give, order):
            self.order = order
            self.keep, self.give = Box(val(keep)), Box(val(give))

        def made(self):
            return self.keep, self.give

        def out(self):
            self.got = send(self.give, over_chip(self.order[0]))
            return self.got

        def rest(self):
            rows = self.keep.v.astype(F32) + self.got.v.astype(F32)
            for bit in self.order[1:]:
                if self.order == down_order:
                    cut = rows.shape[0] // 2
                    self.keep, give = Box(rows[:cut]), rows[cut:]
                else:
                    blocks = [rows[k : k + wide] for k in range(0, rows.shape[0], wide)]
                    self.keep, give = Box(rows_of(blocks[0::2])), rows_of(blocks[1::2])
                self.last = send(give.astype(BF16), over_chip(bit))
                if bit != self.order[-1]:
                    rows = self.keep.v + self.last.v.astype(F32)
            return self.last

        def own(self):
            return (self.keep.v + self.last.v.astype(F32)).astype(BF16)

    class Finish:
        def near(self, rows):
            self.mine_near, other = pick(rows[:share], rows[share:]), pick(rows[share:], rows[:share])
            self.here = send(other, over_core)
            return self.here

        def far_one(self, rows):
            mine, other = pick(rows[:share], rows[share:]), pick(rows[share:], rows[:share])
            self.other = Box(other)
            self.same = send(mine, over_half)
            return self.same

        def far_two(self):
            self.cross = send(self.other, over_core_half)
            return self.cross

        def land(self):
            mine = self.mine_near.astype(F32) + self.same.v.astype(F32)
            rest = self.here.v.astype(F32) + self.cross.v.astype(F32)
            return pick(mine, rest), pick(rest, mine)

    gain_one = attn_gain.astype(F32)[:, None]
    gain_two = mlp_gain.astype(F32)[:, None]
    part, fpart = inner // 2, half_heads
    fcut = hidden_width // 2
    lanes = ((0, 0), (0, PAIR - heads))
    forget_own = jnp.pad(lax.dynamic_slice_in_dim(w_forget, d * share, share, 0), lanes)
    one = Pack(
        *pack_one(
            core.astype(jnp.int32)[None], w_query, w_key, w_value, forget_own, attn_gain[None, :],
            jnp.pad(forget_bias[None, :], lanes),
        )
    )
    out_t, down_t = w_output.T, w_down.T
    gate_scaled, up_scaled = ((w.astype(F32) * gain_two).astype(BF16) for w in (w_gate, w_up))

    def halves_of(arrays, size):
        halves = [jnp.concatenate([w[:, h * size : (h + 1) * size] for w in arrays], axis=1) for h in (0, 1)]
        return pick(*halves), pick(*halves[::-1])

    def stay(d, t):
        return (d, t ^ 1) if (d & 1) == (t >> 1) else None

    def move(d, t):
        return (d, t ^ 1) if (d & 1) != (t >> 1) else None

    one_far = one.cross()
    one.near()
    near_one = Spread(one.near_rows(), up_order)
    near_early = near_one.early()
    x_own, cot_own = Box(reorder(block_input)), Box(reorder(cotangent))

    x_stay = send(x_own, stay)

    hold(x_own, one_far, near_early, x_stay)
    x_home = send(x_own, to_home)
    cot_stay = send(hold(cot_own, x_own), stay)
    far_one = Spread(one.far_rows(), down_order)
    far_early = far_one.early()
    near_late = near_one.late()
    wo = Pack(*halves_of([out_t], part))
    feed_pack = Pack(*halves_of([gate_scaled, up_scaled, down_t], fcut))
    gate_pack, down_pack = Pack(*halves_of([gate_scaled, up_scaled], fcut)), Pack(*halves_of([down_t], fcut))

    hold(x_home, far_early, cot_stay)
    x_move = send(x_home, move)
    x_core = send(x_home, over_core)
    far_late = far_one.late()
    wo_far = wo.cross(x_home)
    wo.near(x_home)
    seg_other = send(hold(segment_ids, x_home), over_core)
    feed_pack.near(x_home)
    near_all = Box(
        lax.all_gather(feed_pack.near_rows(), "dp", axis=0, tiled=True, axis_index_groups=planes)
    )
    seg_row = Box(pick_home(segment_ids, seg_other))
    far_bias = far_one.pieces[0][0, 4 * PAIR + HEAD + fpart + 1 :].astype(F32)
    bias_far = far_bias[:fpart] + far_bias[fpart : 2 * fpart] + far_bias[2 * fpart : 3 * fpart]
    spare = jnp.zeros((HEAD - fpart,), F32)
    bias = Box(jnp.concatenate([pick(forget_bias[:fpart], forget_bias[fpart:]), spare, bias_far, spare])[None, :])
    place = (t & 1) + 2 * core
    pos = jnp.stack([((a ^ place) >> 1) | (((a ^ place) & 1) << 1) for a in range(4)]).astype(jnp.int32)
    wa = Box(near_one.whole())

    hold(x_move, wa, bias, seg_row)
    hold(x_move, far_late, wo_far)
    x_z = Box(pick_home(x_stay, x_move))
    x_both = send(x_z, over_core)
    wb = Box(far_one.whole())
    hold(x_both, wb, x_core)
    wo_a, wo_b = wo.near_rows(), wo.far_rows()
    wo_rows = jnp.concatenate([wo_a[:, :PAIR], wo_b[:, :PAIR], wo_a[:, PAIR:], wo_b[:, PAIR:]], axis=1)
    wo_spread = Spread(wo_rows, up_order)
    wo_sent = wo_spread.direct()
    gate_far = gate_pack.cross(x_both)
    qcols = wa.v.shape[1]

    resid = x_home.v.astype(F32)
    first_scale = unit_rows(resid)[1]
    seg_col = seg_row.v.reshape(-1, 1)
    mixed, x_hat, qkv, logit, lse, cum = attend(
        pos, [x_home.v, x_core.v, x_z.v, x_both.v], wa.v, wb.v, bias.v, seg_row.v, seg_col
    )
    mixed = hold(mixed, wo_sent, gate_far)
    wo_t = wo_spread.whole()

    def half(array, which):
        rows = array.shape[0] // 2
        return array[which * rows : (which + 1) * rows]

    order = {}

    def scatter_group(far, near, at_far=lambda far_sum: None, at_near=lambda near_sum: None, at_end=lambda: (), after_far=None, late_core=False):
        rows = far()
        far_in = send(rows[quarter:].astype(BF16), over_core)
        far_sum = Box((rows[:quarter].astype(F32) + far_in.v.astype(F32)).astype(BF16))
        at_far(far_sum)
        far_got = send(far_sum, over_z)
        rows = Box(near())
        if late_core:
            hold(far_got, rows)
            if after_far:
                after_far(far_got)
            hold(rows, far_got)
        near_in = send(rows.v[quarter:].astype(BF16), over_core)
        near_sum = Box(rows.v[:quarter].astype(F32) + near_in.v.astype(F32))
        at_near(near_sum)
        hold(far_got, near_sum)
        if at_end():
            hold(far_got, at_end())
        return near_sum.v + far_got.v.astype(F32)

    sent = {}

    def weights_on(near_sum):
        sent["gate"] = Spread(gate_pack.far_rows(), up_order)
        sent["early"] = sent["gate"].early()
        sent["down"] = down_pack.cross(near_sum)

    mixed = Box(mixed)
    hidden_res = Box(
        resid
        + scatter_group(
            lambda: nt(half(mixed.v, 1), wo_t),
            lambda: nt(half(mixed.v, 0), wo_t),
            lambda far_sum: hold(far_sum, mixed),
            weights_on,
            lambda: (sent["early"], sent["down"]),
        )
    )
    far_gate = sent["gate"]
    second, second_scale = unit_rows(hidden_res.v)
    second_low = Box(second.astype(BF16))
    second_z = send(second_low, over_z)
    second_core = send(second_low, over_core)
    gate_late = far_gate.late()
    far_down = Spread(down_pack.far_rows(), down_order)
    down_early = far_down.early()
    cot_home = send(hold(cot_own, second_core), to_home)
    hold(near_all, second_core)
    gates_a = Box(reorder_rows(near_all.v[:, : 2 * fcut]))
    downs_a = Box(reorder_rows(near_all.v[:, 2 * fcut :]))
    hold(second_z, gates_a, downs_a)
    hold(second_z, cot_home, gate_late, down_early)
    second_both = send(second_z, over_core)
    cot_move = send(cot_home, move)
    down_late = far_down.late()
    cot_core = send(cot_home, over_core)
    gates_b = Box(far_gate.whole())
    hold(cot_move, second_both, gates_b)
    hold(cot_move, down_late)
    downs_b = Box(far_down.whole())
    cot_z = Box(pick_home(cot_stay, cot_move))
    cot_both = send(cot_z, over_core)
    hold(cot_both, cot_core)

    feed_weights = (gates_a.v, gates_b.v, downs_a.v, downs_b.v)
    made = {}

    def feed_far():
        made["far"] = feed_tokens((second_z.v, second_both.v), (cot_z.v, cot_both.v), feed_weights, 1)
        return made["far"][5]

    def feed_near():
        made["near"] = feed_tokens(
            (second_low.v, second_core.v), (cot_home.v, cot_core.v), feed_weights, 0, made["far"][:5]
        )
        return made["near"][5]

    grad_second = scatter_group(feed_far, feed_near, lambda far_sum: hold(far_sum, second_low, second_core), late_core=True)
    gain_two_part = made["far"][6] + made["near"][6]
    grad_res = Box(cot_home.v.astype(F32) + unit_back(hidden_res.v, second_scale, grad_second))
    branch = Box(grad_res.v.astype(BF16))
    laid = [Box(m) for m in made["near"][:5]]
    hold(branch, laid)
    branch_z = send(branch, over_z)
    hidden, grads_a, grads_b, second_all, cot_all = (m.v for m in laid)
    *b_rows, a_part, mlp_rows = (
        Box(m)
        for m in feed_grads(
            chip.astype(jnp.int32)[None], second_all, cot_all, hidden, grads_a, grads_b, downs_a.v, downs_b.v, chips
        )
    )
    hold(branch_z, b_rows, a_part, mlp_rows)
    hold(branch, branch_z)
    branch_both = send(branch_z, over_core)
    branch_core = send(branch, over_core)
    gb, db = Sum(*b_rows[:2], down_order), Sum(*b_rows[2:], up_order)
    b_out = [gb.out(), db.out()]
    branch_all = Box(rows_of([branch, branch_core, branch_z, branch_both]))

    grad_mixed = Box(nn(branch_all.v, wo_t).astype(BF16))
    mlp_out = Box(scatter_group(lambda: half(mlp_rows.v, 1), lambda: half(mlp_rows.v, 0)))
    hold(branch_all, grad_mixed)
    o_sum = Sum(*halves_apart(tn(branch_all.v, mixed.v).astype(BF16)), down_order)
    o_out = o_sum.out()
    hold(grad_mixed, o_sum.keep)
    grad_near, grad_far, grad_bias = attend_back(
        pos, qkv, logit, seg_row.v, seg_col, lse, cum, grad_mixed.v, qcols, quarter
    )
    grad_near, grad_far, x_hat = Box(grad_near), Box(grad_far), Box(x_hat)
    hold(grad_near, grad_far, b_out, mlp_out)
    out_home = (hidden_res.v + mlp_out.v).astype(BF16)
    out_sent = send(out_home, swap_home)
    b_late = [gb.rest(), db.rest()]
    first_parts = {}
    feed_end = Finish()

    def first_part(which):
        first_parts[which] = nt(half(grad_near.v, which), wa.v) + nt(half(grad_far.v, which), wb.v)
        return first_parts[which]

    def first_near():
        rows = Box(first_part(0))
        hold(x_hat, rows)
        made["grads"] = [Box(g) for g in first_grads(x_hat.v, grad_near.v, grad_far.v, chips)]
        return rows.v

    grad_first = Box(
        scatter_group(
            lambda: first_part(1),
            first_near,
            lambda far_sum: hold(far_sum, grad_near, grad_far, x_hat),
            after_far=lambda far_got: hold(far_got, b_late, out_sent, made["grads"]),
            late_core=True,
        )
    )
    grads = made["grads"]
    qa, qb, gate_cols = Sum(*grads[:2], down_order), Sum(*grads[2:4], up_order), grads[4]
    hold(a_part, grad_first)
    a_own = Box(
        lax.psum_scatter(a_part.v, "dp", scatter_dimension=0, tiled=True, axis_index_groups=planes)
    )
    b_same = feed_end.far_one(jnp.concatenate([gb.own(), db.own()], axis=1))
    q_out = [qa.out(), qb.out()]
    back_home = Box((grad_res.v + unit_back(resid, first_scale, grad_first.v)).astype(BF16))
    back_sent = send(back_home, swap_home)

    hold(gate_cols, back_home)
    forget = jnp.concatenate([gate_cols.v[:, k * PAIR + HEAD : k * PAIR + HEAD + fpart] for k in (0, 1)], axis=1).T
    gain_part = functools.reduce(
        jnp.add, [jnp.sum(half(x_hat.v, w).astype(F32) * first_parts[w], axis=0) for w in (0, 1)]
    )
    gain_row = wa.v[:, 3 * part + fpart].astype(F32)
    small = reorder(jnp.concatenate([forget * gain_row[None, :], gain_part[None], gain_two_part], axis=0))
    small = Box(jnp.concatenate([small, jnp.pad(grad_bias, ((0, 0), (0, width - PAIR)))], axis=0))
    small_there = send(small, over_chip(0))

    hold(small, q_out, small_there, o_out, b_same)
    q_late = [qa.rest(), qb.rest()]
    o_late = o_sum.rest()
    hold(feed_end.other, small)
    b_cross = feed_end.far_two()
    small = Box(small.v + small_there.v)
    hold(small, q_late, o_late, back_sent)
    for bit in range(1, bits):
        small = Box(small.v + send(small, over_chip(bit)).v)
    near, far = small.v[:fpart], small.v[fpart:heads]
    gains, bias_sum = small.v[heads : heads + 2], small.v[heads + 2 :]
    spread_out = ((0, 0), (0, width - fpart))
    bias_near, bias_far = (jnp.pad(bias_sum[:, k * HEAD : k * HEAD + fpart], spread_out) for k in (0, 1))
    far_small = Box(jnp.concatenate([far, bias_far, gains], axis=0))
    hold(far_small, q_late, o_late)
    got = send(far_small, over_half)

    own_out = o_sum.own()
    out_halves = [
        jnp.concatenate(
            [own_out[:, h * PAIR : (h + 1) * PAIR], own_out[:, 2 * PAIR + h * HEAD : 2 * PAIR + (h + 1) * HEAD]], axis=1
        )
        for h in (0, 1)
    ]
    q_end = Finish()
    q_same = q_end.far_one(jnp.concatenate([qb.own(), out_halves[1]], axis=1))
    q_cross = q_end.far_two()
    q_here = q_end.near(jnp.concatenate([qa.own(), out_halves[0]], axis=1))
    hold(a_own, q_same)
    feed_end.near(a_own.v)
    hold(got, q_here, b_cross)
    mine = jnp.concatenate(
        [near + got.v[:fpart], bias_near + got.v[fpart : fpart + 1], gains + got.v[fpart + 1 :]], axis=0
    )
    rest = send(mine, over_core).v
    grad_forget = pick(rows_of([mine[:fpart], rest[:fpart]]), rows_of([rest[:fpart], mine[:fpart]])).T
    bias_mine, bias_rest = mine[fpart, :fpart], rest[fpart, :fpart]
    grad_bias_out = pick(jnp.concatenate([bias_mine, bias_rest]), jnp.concatenate([bias_rest, bias_mine]))
    gains = mine[fpart + 1 :] + rest[fpart + 1 :]
    gains = lax.dynamic_slice_in_dim(gains, d * share, share, 1)
    gains = gains + send(gains, over_z).v
    grad_gain_one = gains[0] / attn_gain.astype(F32)
    grad_gain_two = gains[1] / mlp_gain.astype(F32)
    f_zero, f_one = feed_end.land()
    gate_sum, up_sum, down_sum = (
        jnp.concatenate([f[:, k * fcut : (k + 1) * fcut] for f in (f_zero, f_one)], axis=1) for k in range(3)
    )
    done = [Box(v) for v in (gate_sum * gain_two, up_sum * gain_two, down_sum.T, grad_gain_one, grad_gain_two)]
    hold(q_same, done)
    hold(q_cross, q_same)
    gate_out, up_out, down_out, grad_gain_one, grad_gain_two = (b.v for b in done)
    input_grad = reorder(pick_home(back_home, back_sent)).astype(F32)
    output = reorder(pick_home(out_home, out_sent))
    q_zero, q_one = q_end.land()

    def joined(k):
        if k == 3:
            return jnp.concatenate([q_zero[:, qcols:], q_one[:, qcols:]], axis=1)
        lone = slice(3 * PAIR + k * HEAD, 3 * PAIR + (k + 1) * HEAD)
        pair = slice(k * PAIR, (k + 1) * PAIR)
        return jnp.concatenate([q_zero[:, pair], q_zero[:, lone], q_one[:, pair], q_one[:, lone]], axis=1)

    q_sums = [joined(k) for k in range(4)]

    return (
        output,
        input_grad,
        grad_gain_one,
        q_sums[0] * gain_one,
        q_sums[1] * gain_one,
        q_sums[2] * gain_one,
        grad_forget,
        grad_bias_out,
        q_sums[3].T,
        grad_gain_two,
        gate_out,
        up_out,
        down_out,
    )


def solution(mesh):
    return jax.shard_map(
        per_device,
        mesh=mesh,
        in_specs=(
            P(("dp", "tensor"), None),
            P("dp"),
            P("dp", "tensor"),
            P("dp", "tensor"),
            P("dp", "tensor"),
            P(None, "tensor"),
            P("tensor"),
            P("tensor", "dp"),
            P("dp"),
            P("dp", "tensor"),
            P("dp", "tensor"),
            P("tensor", "dp"),
            P("dp", None),
            P(("dp", "tensor"), None),
        ),
        out_specs=(
            P(("dp", "tensor"), None),
            P(("dp", "tensor"), None),
            P("dp"),
            P("dp", "tensor"),
            P("dp", "tensor"),
            P("dp", "tensor"),
            P(None, "tensor"),
            P("tensor"),
            P("tensor", "dp"),
            P("dp"),
            P("dp", "tensor"),
            P("dp", "tensor"),
            P("tensor", "dp"),
        ),
        check_vma=False,
    )
```

```python
import functools

import jax
import jax.numpy as jnp
from jax import lax
from jax.experimental import pallas as pl
from jax.experimental.pallas import tpu as pltpu
from jax.sharding import PartitionSpec as P

HEAD = 64
PAIR = 2 * HEAD
EPS = 1e-06
F32 = jnp.float32
BF16 = jnp.bfloat16
NT = (((1,), (1,)), ((), ()))
TN = (((0,), (0,)), ((), ()))
AXES = ("dp", "tensor")


def nn(a, b):
    return jnp.dot(a, b, preferred_element_type=F32)


def nt(a, b):
    return lax.dot_general(a, b, NT, preferred_element_type=F32)


def tn(a, b):
    return lax.dot_general(a, b, TN, preferred_element_type=F32)


class Box:
    def __init__(self, v):
        self.v = v


def val(value):
    return value.v if isinstance(value, Box) else value


def boxes(tree):
    if isinstance(tree, Box):
        return [tree]
    assert isinstance(tree, (list, tuple)), type(tree)
    return [b for item in tree for b in boxes(item)]


def send(value, move):
    tensor = lax.axis_size("tensor")
    pairs = []
    for d in range(lax.axis_size("dp")):
        for t in range(tensor):
            to = move(d, t)
            if to is not None:
                pairs.append((d * tensor + t, to[0] * tensor + to[1]))
    return Box(lax.ppermute(val(value), AXES, pairs))


def to_home(d, t):
    return (d ^ 1, t ^ 2) if (d & 1) != (t >> 1) else (d, t)


def swap_home(d, t):
    return (d ^ 1, t ^ 2) if (d & 1) != (t >> 1) else None


def over_core(d, t):
    return (d ^ 1, t)


def over_z(d, t):
    return (d, t ^ 1)


def over_chip(bit):
    return lambda d, t: (d ^ (2 << bit), t)


def over_half(d, t):
    return (d, t ^ 2)


def over_core_half(d, t):
    return (d ^ 1, t ^ 2)


def hold(value, *others):
    held = boxes(others)
    result, new = lax.optimization_barrier((jax.tree.map(val, value, is_leaf=lambda x: isinstance(x, Box)), [b.v for b in held]))
    for b, v in zip(held, new):
        b.v = v
    if isinstance(value, Box):
        value.v = result
        return value
    return result


def meet(critical, *others):
    return hold(hold(critical), *others)


def rows_of(pieces):
    return jnp.concatenate([val(p) for p in pieces], axis=0)


def block_of(pos_ref, at, size):
    return pl.ds(pl.multiple_of(pos_ref[at] * size, size), size)


def lane_of(pair, h):
    return jnp.where(pair == 2, 2 + HEAD * h, HEAD * pair + h)


def pack_kernel(core_ref, query_ref, key_ref, value_ref, forget_ref, gain_ref, bias_ref, mine_ref, other_ref):
    share = gain_ref.shape[1]
    diagonal = lax.broadcasted_iota(jnp.int32, (share, share), 0) == lax.broadcasted_iota(jnp.int32, (share, share), 1)
    gain = jnp.sum(jnp.where(diagonal, gain_ref[...].astype(F32), 0.0), axis=1, keepdims=True)
    lane = lax.broadcasted_iota(jnp.int32, (share, PAIR), 1)
    low_lanes = lane < HEAD
    first = core_ref[0] == 0
    parts = [ref[...].astype(F32) * gain for ref in (query_ref, key_ref, value_ref)]
    forget = forget_ref[...].astype(F32) * gain
    bias = bias_ref[...]
    pieces = []
    for _ in range(3):
        piece = bias.astype(BF16).astype(F32)
        pieces.append(piece)
        bias = bias - piece
    halves = []
    for h in range(2):
        three = [p if h == 0 else pltpu.roll(p, p.shape[1] // 2, 1) for p in parts]
        tiles = [p[:, :PAIR] for p in three]
        lone = [p[:, PAIR : 2 * PAIR] for p in three]
        tiles.append(jnp.where(low_lanes, lone[0], pltpu.roll(lone[1], HEAD, 1)))
        rest = jnp.where(lane < HEAD + 3, pltpu.roll(forget, HEAD - 3 * h, 1), gain)
        for k, piece in enumerate(pieces):
            at = HEAD + 4 + 3 * k
            moved = jnp.broadcast_to(pltpu.roll(piece, at - 3 * h, 1), (share, PAIR))
            rest = jnp.where((lane >= at) & (lane < at + 3), moved, rest)
        rest = jnp.where(lane < HEAD + 13, rest, 0.0)
        tiles.append(jnp.where(low_lanes, lone[2], rest))
        halves.append(tiles)
    for k in range(5):
        at = slice(k * PAIR, (k + 1) * PAIR)
        mine_ref[:, at] = jnp.where(first, halves[0][k], halves[1][k]).astype(BF16)
        other_ref[:, at] = jnp.where(first, halves[1][k], halves[0][k]).astype(BF16)


def forward_kernel(
    quarter, pos_ref, x0_ref, x1_ref, x2_ref, x3_ref, wa_ref, wb_ref, bias_ref, segr_ref, segc_ref,
    mixed_ref, xhat_ref, qkv_ref, logit_ref, lse_ref, cum_ref, cumr_ref, rel_ref,
):
    pair = pl.program_id(0)
    width = 3 * PAIR
    lane = lax.broadcasted_iota(jnp.int32, (quarter, PAIR), 1)
    low_lanes = lane < HEAD
    count = segr_ref.shape[1] // quarter

    @pl.when(pair == 0)
    def _():
        for r, x_ref in enumerate((x0_ref, x1_ref, x2_ref, x3_ref)):
            at = slice(r * quarter, (r + 1) * quarter)
            x = x_ref[...].astype(F32)
            low = (x * lax.rsqrt(jnp.mean(x * x, axis=1, keepdims=True) + EPS)).astype(BF16)
            xhat_ref[at, :] = low
            near_all = nn(low, wa_ref[...])
            far_all = nn(low, wb_ref[...])

            def near(k):
                return near_all[:, k * PAIR : (k + 1) * PAIR]

            def far(k):
                return far_all[:, k * PAIR : (k + 1) * PAIR]

            for k in range(3):
                qkv_ref[at, k * width : k * width + PAIR] = near(k).astype(BF16)
                qkv_ref[at, k * width + PAIR : k * width + 2 * PAIR] = far(k).astype(BF16)

            def both(one, two):
                return jnp.where(low_lanes, one, two).astype(BF16)

            qkv_ref[at, 2 * PAIR : 3 * PAIR] = both(near(3), pltpu.roll(far(3), HEAD, 1))
            qkv_ref[at, width + 2 * PAIR : width + 3 * PAIR] = both(pltpu.roll(near(3), HEAD, 1), far(3))
            qkv_ref[at, 2 * width + 2 * PAIR : 2 * width + 3 * PAIR] = both(near(4), pltpu.roll(far(4), HEAD, 1))
            rel_ref[at, :] = jnp.where(low_lanes, pltpu.roll(near(4), HEAD, 1), far(4)) + bias_ref[...]
        rows = lax.broadcasted_iota(jnp.int32, (quarter, quarter), 0)
        cols = lax.broadcasted_iota(jnp.int32, (quarter, quarter), 1)
        lower = (cols <= rows).astype(F32)
        carry = jnp.zeros((1, PAIR), F32)
        for a in range(count):
            logit = rel_ref[block_of(pos_ref, a, quarter), :]
            here = slice(a * quarter, (a + 1) * quarter)
            logit_ref[here, :] = logit
            logsig = jnp.minimum(logit, 0.0) - jnp.log1p(jnp.exp(-jnp.abs(logit)))
            cum = jnp.dot(lower, logsig, precision=lax.Precision.HIGHEST, preferred_element_type=F32) + carry
            carry = cum[quarter - 1 :, :]
            cum_ref[here, :] = cum
            cumr_ref[:, here] = cum.T
        lse_ref[...] = jnp.zeros(lse_ref.shape, F32)

    def columns(part):
        return pl.ds(pl.multiple_of(part * width + pair * PAIR, PAIR), PAIR)

    diag_rows = lax.broadcasted_iota(jnp.int32, (quarter, quarter), 0)
    diag_cols = lax.broadcasted_iota(jnp.int32, (quarter, quarter), 1)
    for a in range(count):
        query = (qkv_ref[block_of(pos_ref, a, quarter), columns(0)] * 0.125).astype(BF16)
        seg_q = segc_ref[a * quarter : (a + 1) * quarter, :]
        spans = range(max(0, a - 512 // quarter), a + 1)
        outs = []
        for h in range(2):
            head = lane_of(pair, h)
            mine = (lane >= HEAD) if h else low_lanes
            query_h = jnp.where(mine, query, jnp.zeros_like(query))
            scores = []
            for b in spans:
                keys = qkv_ref[block_of(pos_ref, b, quarter), columns(1)]
                s = nt(query_h, keys) - cumr_ref[pl.ds(head, 1), b * quarter : (b + 1) * quarter]
                allowed = seg_q == segr_ref[:, b * quarter : (b + 1) * quarter]
                if a == b:
                    allowed &= diag_cols <= diag_rows
                scores.append(jnp.where(allowed, s, -jnp.inf))
            top = functools.reduce(jnp.maximum, [jnp.max(s, axis=1, keepdims=True) for s in scores])
            expd = [jnp.exp(s - top) for s in scores]
            total = functools.reduce(jnp.add, [jnp.sum(e, axis=1, keepdims=True) for e in expd])
            scale = 1.0 / total
            out = None
            for e, b in zip(expd, spans):
                values = qkv_ref[block_of(pos_ref, b, quarter), columns(2)]
                part = nn((e * scale).astype(BF16), values)
                out = part if out is None else out + part
            outs.append(out)
            lse = top + jnp.log(total)
            at = pl.ds(a * quarter, quarter)
            lse_ref[at, :] = jnp.where(lane == head, lse, lse_ref[at, :])
        mixed_ref[block_of(pos_ref, a, quarter), columns(0)] = jnp.where(low_lanes, outs[0], outs[1]).astype(BF16)


def backward_kernel(
    quarter, pos_ref, qkv_ref, logit_ref, segr_ref, segc_ref, lse_ref, cum_ref, gmix_ref,
    gnear_ref, gfar_ref, gbias_ref, lser_ref, gcol_ref, grow_ref, grad_ref, gk_ref, gv_ref,
):
    pair = pl.program_id(0)
    pairs = pl.num_programs(0)
    width = 3 * PAIR
    lane = lax.broadcasted_iota(jnp.int32, (quarter, PAIR), 1)
    low_lanes = lane < HEAD
    count = segr_ref.shape[1] // quarter

    @pl.when(pair == 0)
    def _():
        for a in range(count):
            at = slice(a * quarter, (a + 1) * quarter)
            lser_ref[:, at] = lse_ref[at, :].T
        gcol_ref[...] = jnp.zeros(gcol_ref.shape, F32)
        grow_ref[...] = jnp.zeros(grow_ref.shape, F32)

    def columns(part):
        return pl.ds(pl.multiple_of(part * width + pair * PAIR, PAIR), PAIR)

    diag_rows = lax.broadcasted_iota(jnp.int32, (quarter, quarter), 0)
    diag_cols = lax.broadcasted_iota(jnp.int32, (quarter, quarter), 1)
    gk_ref[...] = jnp.zeros(gk_ref.shape, F32)
    gv_ref[...] = jnp.zeros(gv_ref.shape, F32)
    for a in range(count):
        here = slice(a * quarter, (a + 1) * quarter)
        query = (qkv_ref[block_of(pos_ref, a, quarter), columns(0)] * 0.125).astype(BF16)
        gout = gmix_ref[block_of(pos_ref, a, quarter), columns(0)]
        seg_q = segr_ref[:, here]
        spans = range(max(0, a - 512 // quarter), a + 1)
        grad_query = None
        for h in range(2):
            head = lane_of(pair, h)
            mine = (lane >= HEAD) if h else low_lanes
            query_h = jnp.where(mine, query, jnp.zeros_like(query))
            gout_h = jnp.where(mine, gout, jnp.zeros_like(gout))
            lse = lser_ref[pl.ds(head, 1), here]
            probs, gprobs = [], []
            inner = None
            for b in spans:
                there = slice(b * quarter, (b + 1) * quarter)
                keys = qkv_ref[block_of(pos_ref, b, quarter), columns(1)]
                values = qkv_ref[block_of(pos_ref, b, quarter), columns(2)]
                cum_k = jnp.sum(jnp.where(lane == head, cum_ref[there, :], 0.0), axis=1, keepdims=True)
                s = nt(keys, query_h) - cum_k
                allowed = segc_ref[there, :] == seg_q
                if a == b:
                    allowed &= diag_rows <= diag_cols
                p = jnp.where(allowed, jnp.exp(s - lse), 0.0)
                g = nt(values, gout_h)
                probs.append(p)
                gprobs.append(g)
                part = jnp.sum(p * g, axis=0, keepdims=True)
                inner = part if inner is None else inner + part
            row_sum = None
            for p, g, b in zip(probs, gprobs, spans):
                there = slice(b * quarter, (b + 1) * quarter)
                keys = (qkv_ref[block_of(pos_ref, b, quarter), columns(1)] * 0.125).astype(BF16)
                keys_h = jnp.where(mine, keys, jnp.zeros_like(keys))
                gs = p * (g - inner)
                part = jnp.sum(gs, axis=0, keepdims=True)
                row_sum = part if row_sum is None else row_sum + part
                col_sum = jnp.sum(gs, axis=1, keepdims=True)
                gcol_ref[there, :] += jnp.where(lane == head, col_sum, 0.0)
                low = gs.astype(BF16)
                gk_ref[there, :] += nn(low, query_h)
                gv_ref[there, :] += nn(p.astype(BF16), gout_h)
                part = tn(low, keys_h)
                grad_query = part if grad_query is None else grad_query + part
            grow_ref[pl.ds(head, 1), here] = row_sum
        grad_ref[block_of(pos_ref, a, quarter), columns(0)] = grad_query
    for a in range(count):
        here = slice(a * quarter, (a + 1) * quarter)
        grad_ref[block_of(pos_ref, a, quarter), columns(1)] = gk_ref[here, :]
        grad_ref[block_of(pos_ref, a, quarter), columns(2)] = gv_ref[here, :]

    @pl.when(pair == pairs - 1)
    def _():
        upper = (diag_cols >= diag_rows).astype(F32)
        carry = jnp.zeros((1, PAIR), F32)
        bias = jnp.zeros((1, PAIR), F32)
        real = (lane % HEAD) < pairs
        for a in reversed(range(count)):
            here = slice(a * quarter, (a + 1) * quarter)
            at = block_of(pos_ref, a, quarter)
            logit = logit_ref[here, :]
            gcum = jnp.where(real, grow_ref[:, here].T - gcol_ref[here, :], 0.0)
            back = jnp.dot(upper, gcum, precision=lax.Precision.HIGHEST, preferred_element_type=F32) + carry
            carry = back[:1, :]
            glogit = jnp.where(real, back * (1.0 / (1.0 + jnp.exp(logit))), 0.0)
            bias = bias + jnp.sum(glogit, axis=0, keepdims=True)

            def grad(part, k):
                return grad_ref[at, part * width + k * PAIR : part * width + (k + 1) * PAIR]

            for k in range(3):
                gnear_ref[at, k * PAIR : (k + 1) * PAIR] = grad(k, 0).astype(BF16)
                gfar_ref[at, k * PAIR : (k + 1) * PAIR] = grad(k, 1).astype(BF16)
            q_last, k_last, v_last = grad(0, 2), grad(1, 2), grad(2, 2)
            k_roll = pltpu.roll(k_last, HEAD, 1)
            gnear_ref[at, 3 * PAIR : 4 * PAIR] = jnp.where(low_lanes, q_last, k_roll).astype(BF16)
            gnear_ref[at, 4 * PAIR :] = jnp.where(low_lanes, v_last, pltpu.roll(glogit, HEAD, 1)).astype(BF16)
            gfar_ref[at, 3 * PAIR : 4 * PAIR] = jnp.where(low_lanes, pltpu.roll(q_last, HEAD, 1), k_last).astype(BF16)
            gfar_ref[at, 4 * PAIR :] = jnp.where(low_lanes, pltpu.roll(v_last, HEAD, 1), glogit).astype(BF16)
        gbias_ref[...] = bias


def full_spec(shape):
    return pl.BlockSpec(shape, lambda *_: (0,) * len(shape))


NO_COST = pl.CostEstimate(flops=0, bytes_accessed=0, transcendentals=0)


def params(mib):
    return pltpu.CompilerParams(vmem_limit_bytes=mib * 2**20, dimension_semantics=("arbitrary",))


def pack_one(core, query, keys, values, forget, gain, bias):
    share = gain.shape[1]
    out = jax.ShapeDtypeStruct((share, 5 * PAIR), BF16)
    return pl.pallas_call(
        pack_kernel,
        grid=(1,),
        out_shape=(out, out),
        in_specs=[
            pl.BlockSpec(memory_space=pltpu.SMEM),
            *(full_spec(w.shape) for w in (query, keys, values, forget, gain, bias)),
        ],
        out_specs=(full_spec(out.shape), full_spec(out.shape)),
        compiler_params=params(4),
        cost_estimate=NO_COST,
    )(core, query, keys, values, forget, gain, bias)


def attend(pos, blocks, wa, wb, bias, seg_row, seg_col):
    quarter, wide = blocks[0].shape
    length = 4 * quarter
    width = 3 * PAIR
    small = jax.ShapeDtypeStruct((length, PAIR), F32)
    outs = (
        jax.ShapeDtypeStruct((length, width), BF16),
        jax.ShapeDtypeStruct((length, wide), BF16),
        jax.ShapeDtypeStruct((length, 3 * width), BF16),
        small,
        small,
        small,
    )
    operands = (*blocks, wa, wb, bias, seg_row, seg_col)
    return pl.pallas_call(
        functools.partial(forward_kernel, quarter),
        grid=(3,),
        out_shape=outs,
        in_specs=[pl.BlockSpec(memory_space=pltpu.SMEM), *(full_spec(o.shape) for o in operands)],
        out_specs=tuple(full_spec(o.shape) for o in outs),
        scratch_shapes=[pltpu.VMEM((PAIR, length), F32), pltpu.VMEM((length, PAIR), F32)],
        compiler_params=params(24),
        cost_estimate=NO_COST,
    )(pos, *operands)


def feed_kernel(s0_ref, s1_ref, c0_ref, c1_ref, ga_ref, gb_ref, da_ref, db_ref, *refs):
    hidden_ref, grada_ref, gradb_ref, second_ref, cot_ref, back_ref, gain_ref = refs[-7:]
    cut = da_ref.shape[1]
    block = s0_ref.shape[0]
    gain = None
    for i, (s_ref, c_ref) in enumerate(((s0_ref, c0_ref), (s1_ref, c1_ref))):
        at = slice(i * block, (i + 1) * block)
        second_ref[at, :] = s_ref[...]
        cot_ref[at, :] = c_ref[...]
        back = None
        for k, (w_ref, d_ref, grad_ref) in enumerate(((ga_ref, da_ref, grada_ref), (gb_ref, db_ref, gradb_ref))):
            both = nn(s_ref[...], w_ref[...])
            grad_hidden = nn(c_ref[...], d_ref[...]).astype(BF16).astype(F32)
            gate, upper = both[:, :cut], both[:, cut:]
            sigma = 1.0 / (1.0 + jnp.exp(-gate))
            swish = gate * sigma
            hidden_ref[at, k * cut : (k + 1) * cut] = (swish * upper).astype(BF16)
            grad_gate = (grad_hidden * upper * sigma * (1.0 + gate * (1.0 - sigma))).astype(BF16)
            grad_up = (grad_hidden * swish).astype(BF16)
            grad_ref[at, :cut] = grad_gate
            grad_ref[at, cut:] = grad_up
            part = nt(grad_gate, w_ref[:, :cut]) + nt(grad_up, w_ref[:, cut:])
            back = part if back is None else back + part
        back_ref[at, :] = back
        part = jnp.sum(s_ref[...].astype(F32) * back, axis=0, keepdims=True)
        gain = part if gain is None else gain + part
    gain_ref[...] = gain


def feed_tokens(second, cot, weights, which, before=()):
    block, wide = second[0].shape
    cut = weights[2].shape[1]
    operands = (*second, *cot, *weights)
    widths = (2 * cut, 2 * cut, 2 * cut, wide, wide)
    outs = tuple(jax.ShapeDtypeStruct((4 * block, w), BF16) for w in widths)
    outs += (jax.ShapeDtypeStruct((2 * block, wide), F32), jax.ShapeDtypeStruct((1, wide), F32))
    return pl.pallas_call(
        feed_kernel,
        grid=(1,),
        out_shape=outs,
        in_specs=[*(full_spec(o.shape) for o in operands)] + [pl.BlockSpec(memory_space=pl.ANY)] * len(before),
        out_specs=(
            *(pl.BlockSpec((2 * block, w), lambda i: (which, 0)) for w in widths),
            full_spec((2 * block, wide)),
            full_spec((1, wide)),
        ),
        input_output_aliases={len(operands) + k: k for k in range(len(before))},
        compiler_params=params(25),
        cost_estimate=NO_COST,
    )(*operands, *before)


def put_half(rows, keep_ref, give_ref):
    first = pl.program_id(0) < pl.num_programs(0) // 2

    @pl.when(first)
    def _():
        keep_ref[...] = rows.astype(BF16)

    @pl.when(jnp.logical_not(first))
    def _():
        give_ref[...] = rows.astype(BF16)


def put_pair(rows, keep_ref, give_ref):
    even = pl.program_id(0) % 2 == 0

    @pl.when(even)
    def _():
        keep_ref[...] = rows.astype(BF16)

    @pl.when(jnp.logical_not(even))
    def _():
        give_ref[...] = rows.astype(BF16)


def half_specs(block, cols, half_of):
    return (
        pl.BlockSpec((block, cols), lambda r, *_: (jnp.minimum(r, half_of - 1), 0)),
        pl.BlockSpec((block, cols), lambda r, *_: (jnp.maximum(r - half_of, 0), 0)),
    )


def pair_specs(block, cols):
    return (pl.BlockSpec((block, cols), lambda r, *_: (r // 2, 0)),) * 2


def feed_grads_kernel(
    chip_ref, second_ref, cot_ref, hidden_ref, ga_ref, gb_ref, da_ref, db_ref,
    keepb_ref, giveb_ref, keepd_ref, gived_ref, outa_ref, part_ref,
):
    cut = da_ref.shape[1]
    second, cot = second_ref[...], cot_ref[...]
    put_half(tn(second, gb_ref[...]), keepb_ref, giveb_ref)
    put_pair(tn(cot, hidden_ref[:, cut:]), keepd_ref, gived_ref)
    outa_ref[:, : 2 * cut] = tn(second, ga_ref[...]).astype(BF16)
    outa_ref[:, 2 * cut :] = tn(cot, hidden_ref[:, :cut]).astype(BF16)
    part = nt(hidden_ref[:, :cut], da_ref[...]) + nt(hidden_ref[:, cut:], db_ref[...])
    part_ref[...] = part.astype(BF16)


def pairs_apart(rows, chips):
    block = rows.shape[0] // chips
    return rows_of([rows[r * block : (r + 1) * block] for r in (*range(0, chips, 2), *range(1, chips, 2))])


def halves_apart(rows):
    cut = rows.shape[0] // 2
    return rows[:cut], rows[cut:]


def feed_grads(chip, second, cot, hidden, ga, gb, da, db, chips):
    length, wide = second.shape
    block = wide // chips
    cut = da.shape[1]
    half_of = chips // 2
    if block % PAIR:
        down = tn(cot, hidden).astype(BF16)
        part = nt(hidden[:, :cut], da) + nt(hidden[:, cut:], db)
        own = jnp.concatenate([tn(second, ga).astype(BF16), down[:, :cut]], axis=1)
        own = [lax.dynamic_slice_in_dim(own, (chip[0] ^ r) * block, block, 0) for r in range(chips)]
        halves = halves_apart(tn(second, gb).astype(BF16)) + halves_apart(pairs_apart(down[:, cut:], chips))
        return *halves, rows_of(own), part.astype(BF16)
    cols = pl.BlockSpec((length, block), lambda r, chip: (0, r))
    rows = pl.BlockSpec((block, cut), lambda r, chip: (r, 0))
    return pl.pallas_call(
        feed_grads_kernel,
        out_shape=(
            *(jax.ShapeDtypeStruct((wide // 2, 2 * cut), BF16),) * 2,
            *(jax.ShapeDtypeStruct((wide // 2, cut), BF16),) * 2,
            jax.ShapeDtypeStruct((wide, 3 * cut), BF16),
            jax.ShapeDtypeStruct((length, wide), BF16),
        ),
        grid_spec=pltpu.PrefetchScalarGridSpec(
            num_scalar_prefetch=1,
            grid=(chips,),
            in_specs=[cols, cols, *(full_spec(o.shape) for o in (hidden, ga, gb)), rows, rows],
            out_specs=(
                *half_specs(block, 2 * cut, half_of),
                *pair_specs(block, cut),
                pl.BlockSpec((block, 3 * cut), lambda r, chip: (r ^ chip[0], 0)),
                pl.BlockSpec((length, block), lambda r, chip: (0, r)),
            ),
        ),
        compiler_params=params(23),
        cost_estimate=NO_COST,
    )(chip, second, cot, hidden, ga, gb, da, db)


def first_grads_kernel(x_ref, near_ref, far_ref, keepn_ref, given_ref, keepf_ref, givef_ref, gate_ref):
    x = x_ref[...]
    near, far = tn(x, near_ref[...]), tn(x, far_ref[...])
    put_half(near, keepn_ref, given_ref)
    put_pair(far, keepf_ref, givef_ref)
    gate_ref[:, :PAIR] = near[:, 4 * PAIR :]
    gate_ref[:, PAIR:] = far[:, 4 * PAIR :]


def first_grads(x_hat, near, far, chips):
    length, wide = x_hat.shape
    block = wide // chips
    cols = near.shape[1]
    half_of = chips // 2
    if block % PAIR:
        near, far = tn(x_hat, near), tn(x_hat, far)
        gate = jnp.concatenate([near[:, 4 * PAIR :], far[:, 4 * PAIR :]], axis=1)
        return *halves_apart(near.astype(BF16)), *halves_apart(pairs_apart(far.astype(BF16), chips)), gate
    return pl.pallas_call(
        first_grads_kernel,
        grid=(chips,),
        out_shape=(
            *(jax.ShapeDtypeStruct((wide // 2, cols), BF16),) * 4,
            jax.ShapeDtypeStruct((wide, 2 * PAIR), F32),
        ),
        in_specs=[pl.BlockSpec((length, block), lambda r: (0, r)), full_spec(near.shape), full_spec(far.shape)],
        out_specs=(
            *half_specs(block, cols, half_of),
            *pair_specs(block, cols),
            pl.BlockSpec((block, 2 * PAIR), lambda r: (r, 0)),
        ),
        compiler_params=params(12),
        cost_estimate=NO_COST,
    )(x_hat, near, far)


def attend_back(pos, qkv, logit, seg_row, seg_col, lse, cum, grad_mixed, cols, quarter):
    length = qkv.shape[0]
    grads = jax.ShapeDtypeStruct((length, cols), BF16)
    return pl.pallas_call(
        functools.partial(backward_kernel, quarter),
        grid=(3,),
        out_shape=(grads, grads, jax.ShapeDtypeStruct((1, PAIR), F32)),
        in_specs=[
            pl.BlockSpec(memory_space=pltpu.SMEM),
            full_spec(qkv.shape),
            full_spec(logit.shape),
            full_spec(seg_row.shape),
            full_spec(seg_col.shape),
            full_spec(lse.shape),
            full_spec(cum.shape),
            full_spec(grad_mixed.shape),
        ],
        out_specs=(full_spec((length, cols)), full_spec((length, cols)), full_spec((1, PAIR))),
        scratch_shapes=[
            pltpu.VMEM((PAIR, length), F32),
            pltpu.VMEM((length, PAIR), F32),
            pltpu.VMEM((PAIR, length), F32),
            pltpu.VMEM((length, 9 * PAIR), F32),
            pltpu.VMEM((length, PAIR), F32),
            pltpu.VMEM((length, PAIR), F32),
        ],
        compiler_params=params(25),
        cost_estimate=NO_COST,
    )(pos, qkv, logit, seg_row, seg_col, lse, cum, grad_mixed)


def unit_rows(value):
    scale = lax.rsqrt(jnp.mean(value * value, axis=-1, keepdims=True) + EPS)
    return value * scale, scale


def unit_back(value, scale, weighted):
    inner = jnp.mean(weighted * value, axis=-1, keepdims=True)
    return scale * weighted - value * (scale * scale * scale) * inner


def per_device(
    block_input, attn_gain, w_query, w_key, w_value, w_forget, forget_bias, w_output,
    mlp_gain, w_gate, w_up, w_down, segment_ids, cotangent,
):
    width = block_input.shape[1]
    quarter = block_input.shape[0]
    heads = w_forget.shape[1]
    share = w_query.shape[0]
    inner = w_output.shape[0]
    hidden_width = w_gate.shape[1]
    chips = lax.axis_size("dp") // 2
    bits = chips.bit_length() - 1
    d = lax.axis_index("dp")
    t = lax.axis_index("tensor")
    core, chip = d & 1, d >> 1
    first = core == 0
    at_home = core == t >> 1
    wide = width // chips
    half_heads = heads // 2

    def pick(one, two):
        return jnp.where(first, val(one), val(two))

    def pick_home(one, two):
        return jnp.where(at_home, val(one), val(two))

    def by_parity(mine, other):
        return pick(rows_of([mine, other]), rows_of([other, mine]))

    def reorder(rows):
        return jnp.concatenate(
            [lax.dynamic_slice_in_dim(rows, (chip ^ r) * wide, wide, 1) for r in range(chips)], axis=1
        )

    def reorder_rows(rows):
        return rows_of([lax.dynamic_slice_in_dim(rows, (chip ^ r) * wide, wide, 0) for r in range(chips)])

    planes = [[2 * k + c for k in range(chips)] for c in (0, 1)]
    up_order, down_order = list(range(bits)), list(reversed(range(bits)))

    class Pack:
        def __init__(self, mine, other):
            self.mine, self.other = mine, other

        def near(self, *others):
            self.near_other = send(hold(self.other, *others) if others else self.other, over_core)
            return self.near_other

        def cross(self, *others):
            mine, other = hold((self.mine, self.other), *others) if others else (self.mine, self.other)
            self.crossed = (send(mine, over_half), send(other, over_core_half))
            return self.crossed

        def near_rows(self):
            return by_parity(self.mine, self.near_other)

        def far_rows(self):
            return by_parity(*self.crossed)

    class Spread:
        def __init__(self, rows, order):
            self.pieces, self.order = {0: rows}, order

        def early(self):
            for bit in self.order:
                self.pieces[1 << bit] = send(self.pieces[0], over_chip(bit))
            return [self.pieces[1 << bit] for bit in self.order]

        def late(self):
            before = set(self.pieces)
            for i, bit in enumerate(self.order):
                passed = sum(1 << b for b in self.order[:i])
                for at in range(1, 1 << bits):
                    if not at & ~passed:
                        self.pieces[at | (1 << bit)] = send(self.pieces[at], over_chip(bit))
            return [v for k, v in self.pieces.items() if k not in before]

        def direct(self):
            for at in range(1, chips):
                self.pieces[at] = send(self.pieces[0], lambda d, t, at=at: (d ^ (2 * at), t))
            return [self.pieces[at] for at in range(1, chips)]

        def whole(self):
            return rows_of([self.pieces[r] for r in range(chips)])

    class Sum:
        def __init__(self, keep, give, order):
            self.order = order
            self.keep, self.give = Box(val(keep)), Box(val(give))

        def made(self):
            return self.keep, self.give

        def out(self):
            self.got = send(self.give, over_chip(self.order[0]))
            return self.got

        def rest(self):
            rows = self.keep.v.astype(F32) + self.got.v.astype(F32)
            for bit in self.order[1:]:
                if self.order == down_order:
                    cut = rows.shape[0] // 2
                    self.keep, give = Box(rows[:cut]), rows[cut:]
                else:
                    blocks = [rows[k : k + wide] for k in range(0, rows.shape[0], wide)]
                    self.keep, give = Box(rows_of(blocks[0::2])), rows_of(blocks[1::2])
                self.last = send(give.astype(BF16), over_chip(bit))
                if bit != self.order[-1]:
                    rows = self.keep.v + self.last.v.astype(F32)
            return self.last

        def own(self):
            return (self.keep.v + self.last.v.astype(F32)).astype(BF16)

    class Finish:
        def near(self, rows):
            self.mine_near, other = pick(rows[:share], rows[share:]), pick(rows[share:], rows[:share])
            self.here = send(other, over_core)
            return self.here

        def far_one(self, rows):
            mine, other = pick(rows[:share], rows[share:]), pick(rows[share:], rows[:share])
            self.other = Box(other)
            self.same = send(mine, over_half)
            return self.same

        def far_two(self):
            self.cross = send(self.other, over_core_half)
            return self.cross

        def land(self):
            mine = self.mine_near.astype(F32) + self.same.v.astype(F32)
            rest = self.here.v.astype(F32) + self.cross.v.astype(F32)
            return pick(mine, rest), pick(rest, mine)

    gain_one = attn_gain.astype(F32)[:, None]
    gain_two = mlp_gain.astype(F32)[:, None]
    part, fpart = inner // 2, half_heads
    fcut = hidden_width // 2
    lanes = ((0, 0), (0, PAIR - heads))
    forget_own = jnp.pad(lax.dynamic_slice_in_dim(w_forget, d * share, share, 0), lanes)
    one = Pack(
        *pack_one(
            core.astype(jnp.int32)[None], w_query, w_key, w_value, forget_own, attn_gain[None, :],
            jnp.pad(forget_bias[None, :], lanes),
        )
    )
    out_t, down_t = w_output.T, w_down.T
    gate_scaled, up_scaled = ((w.astype(F32) * gain_two).astype(BF16) for w in (w_gate, w_up))

    def halves_of(arrays, size):
        halves = [jnp.concatenate([w[:, h * size : (h + 1) * size] for w in arrays], axis=1) for h in (0, 1)]
        return pick(*halves), pick(*halves[::-1])

    def stay(d, t):
        return (d, t ^ 1) if (d & 1) == (t >> 1) else None

    def move(d, t):
        return (d, t ^ 1) if (d & 1) != (t >> 1) else None

    one_far = one.cross()
    one.near()
    near_one = Spread(one.near_rows(), up_order)
    near_early = near_one.early()
    x_own, cot_own = Box(reorder(block_input)), Box(reorder(cotangent))

    x_stay = send(x_own, stay)

    hold(x_own, one_far, near_early, x_stay)
    x_home = send(x_own, to_home)
    cot_stay = send(hold(cot_own, x_own), stay)
    far_one = Spread(one.far_rows(), down_order)
    far_early = far_one.early()
    near_late = near_one.late()
    wo = Pack(*halves_of([out_t], part))
    feed_pack = Pack(*halves_of([gate_scaled, up_scaled, down_t], fcut))
    gate_pack, down_pack = Pack(*halves_of([gate_scaled, up_scaled], fcut)), Pack(*halves_of([down_t], fcut))

    hold(x_home, far_early, cot_stay)
    x_move = send(x_home, move)
    x_core = send(x_home, over_core)
    far_late = far_one.late()
    wo_far = wo.cross(x_home)
    wo.near(x_home)
    seg_other = send(hold(segment_ids, x_home), over_core)
    feed_pack.near(x_home)
    near_all = Box(
        lax.all_gather(feed_pack.near_rows(), "dp", axis=0, tiled=True, axis_index_groups=planes)
    )
    seg_row = Box(pick_home(segment_ids, seg_other))
    far_bias = far_one.pieces[0][0, 4 * PAIR + HEAD + fpart + 1 :].astype(F32)
    bias_far = far_bias[:fpart] + far_bias[fpart : 2 * fpart] + far_bias[2 * fpart : 3 * fpart]
    spare = jnp.zeros((HEAD - fpart,), F32)
    bias = Box(jnp.concatenate([pick(forget_bias[:fpart], forget_bias[fpart:]), spare, bias_far, spare])[None, :])
    place = (t & 1) + 2 * core
    pos = jnp.stack([((a ^ place) >> 1) | (((a ^ place) & 1) << 1) for a in range(4)]).astype(jnp.int32)
    wa = Box(near_one.whole())

    hold(x_move, wa, bias, seg_row)
    hold(x_move, far_late, wo_far)
    x_z = Box(pick_home(x_stay, x_move))
    x_both = send(x_z, over_core)
    wb = Box(far_one.whole())
    hold(x_both, wb, x_core)
    wo_a, wo_b = wo.near_rows(), wo.far_rows()
    wo_rows = jnp.concatenate([wo_a[:, :PAIR], wo_b[:, :PAIR], wo_a[:, PAIR:], wo_b[:, PAIR:]], axis=1)
    wo_spread = Spread(wo_rows, up_order)
    wo_sent = wo_spread.direct()
    gate_far = gate_pack.cross(x_both)
    qcols = wa.v.shape[1]

    resid = x_home.v.astype(F32)
    first_scale = unit_rows(resid)[1]
    seg_col = seg_row.v.reshape(-1, 1)
    mixed, x_hat, qkv, logit, lse, cum = attend(
        pos, [x_home.v, x_core.v, x_z.v, x_both.v], wa.v, wb.v, bias.v, seg_row.v, seg_col
    )
    mixed = hold(mixed, wo_sent, gate_far)
    wo_t = wo_spread.whole()

    def half(array, which):
        rows = array.shape[0] // 2
        return array[which * rows : (which + 1) * rows]

    order = {}

    def scatter_group(far, near, at_far=lambda far_sum: None, at_near=lambda near_sum: None, at_end=lambda: (), after_far=None, late_core=False):
        rows = far()
        far_in = send(rows[quarter:].astype(BF16), over_core)
        far_sum = Box((rows[:quarter].astype(F32) + far_in.v.astype(F32)).astype(BF16))
        at_far(far_sum)
        far_got = send(far_sum, over_z)
        rows = Box(near())
        if late_core:
            hold(far_got, rows)
            if after_far:
                after_far(far_got)
            hold(rows, far_got)
        near_in = send(rows.v[quarter:].astype(BF16), over_core)
        near_sum = Box(rows.v[:quarter].astype(F32) + near_in.v.astype(F32))
        at_near(near_sum)
        hold(far_got, near_sum)
        if at_end():
            hold(far_got, at_end())
        return near_sum.v + far_got.v.astype(F32)

    sent = {}

    def weights_on(near_sum):
        sent["gate"] = Spread(gate_pack.far_rows(), up_order)
        sent["early"] = sent["gate"].early()
        sent["down"] = down_pack.cross(near_sum)

    mixed = Box(mixed)
    hidden_res = Box(
        resid
        + scatter_group(
            lambda: nt(half(mixed.v, 1), wo_t),
            lambda: nt(half(mixed.v, 0), wo_t),
            lambda far_sum: hold(far_sum, mixed),
            weights_on,
            lambda: (sent["early"], sent["down"]),
        )
    )
    far_gate = sent["gate"]
    second, second_scale = unit_rows(hidden_res.v)
    second_low = Box(second.astype(BF16))
    second_z = send(second_low, over_z)
    second_core = send(second_low, over_core)
    gate_late = far_gate.late()
    far_down = Spread(down_pack.far_rows(), down_order)
    down_early = far_down.early()
    cot_home = send(hold(cot_own, second_core), to_home)
    hold(near_all, second_core)
    gates_a = Box(reorder_rows(near_all.v[:, : 2 * fcut]))
    downs_a = Box(reorder_rows(near_all.v[:, 2 * fcut :]))
    hold(second_z, gates_a, downs_a)
    hold(second_z, cot_home, gate_late, down_early)
    second_both = send(second_z, over_core)
    cot_move = send(cot_home, move)
    down_late = far_down.late()
    cot_core = send(cot_home, over_core)
    gates_b = Box(far_gate.whole())
    hold(cot_move, second_both, gates_b)
    hold(cot_move, down_late)
    downs_b = Box(far_down.whole())
    cot_z = Box(pick_home(cot_stay, cot_move))
    cot_both = send(cot_z, over_core)
    hold(cot_both, cot_core)

    feed_weights = (gates_a.v, gates_b.v, downs_a.v, downs_b.v)
    made = {}

    def feed_far():
        made["far"] = feed_tokens((second_z.v, second_both.v), (cot_z.v, cot_both.v), feed_weights, 1)
        return made["far"][5]

    def feed_near():
        made["near"] = feed_tokens(
            (second_low.v, second_core.v), (cot_home.v, cot_core.v), feed_weights, 0, made["far"][:5]
        )
        return made["near"][5]

    grad_second = scatter_group(feed_far, feed_near, lambda far_sum: hold(far_sum, second_low, second_core), late_core=True)
    gain_two_part = made["far"][6] + made["near"][6]
    grad_res = Box(cot_home.v.astype(F32) + unit_back(hidden_res.v, second_scale, grad_second))
    branch = Box(grad_res.v.astype(BF16))
    laid = [Box(m) for m in made["near"][:5]]
    hold(branch, laid)
    branch_z = send(branch, over_z)
    hidden, grads_a, grads_b, second_all, cot_all = (m.v for m in laid)
    *b_rows, a_part, mlp_rows = (
        Box(m)
        for m in feed_grads(
            chip.astype(jnp.int32)[None], second_all, cot_all, hidden, grads_a, grads_b, downs_a.v, downs_b.v, chips
        )
    )
    hold(branch_z, b_rows, a_part, mlp_rows)
    hold(branch, branch_z)
    branch_both = send(branch_z, over_core)
    branch_core = send(branch, over_core)
    gb, db = Sum(*b_rows[:2], down_order), Sum(*b_rows[2:], up_order)
    b_out = [gb.out(), db.out()]
    branch_all = Box(rows_of([branch, branch_core, branch_z, branch_both]))

    grad_mixed = Box(nn(branch_all.v, wo_t).astype(BF16))
    mlp_out = Box(scatter_group(lambda: half(mlp_rows.v, 1), lambda: half(mlp_rows.v, 0)))
    hold(branch_all, grad_mixed)
    o_sum = Sum(*halves_apart(tn(branch_all.v, mixed.v).astype(BF16)), down_order)
    o_out = o_sum.out()
    hold(grad_mixed, o_sum.keep)
    grad_near, grad_far, grad_bias = attend_back(
        pos, qkv, logit, seg_row.v, seg_col, lse, cum, grad_mixed.v, qcols, quarter
    )
    grad_near, grad_far, x_hat = Box(grad_near), Box(grad_far), Box(x_hat)
    hold(grad_near, grad_far, b_out, mlp_out)
    out_home = (hidden_res.v + mlp_out.v).astype(BF16)
    out_sent = send(out_home, swap_home)
    b_late = [gb.rest(), db.rest()]
    first_parts = {}
    feed_end = Finish()

    def first_part(which):
        first_parts[which] = nt(half(grad_near.v, which), wa.v) + nt(half(grad_far.v, which), wb.v)
        return first_parts[which]

    def first_near():
        rows = Box(first_part(0))
        hold(x_hat, rows)
        made["grads"] = [Box(g) for g in first_grads(x_hat.v, grad_near.v, grad_far.v, chips)]
        return rows.v

    grad_first = Box(
        scatter_group(
            lambda: first_part(1),
            first_near,
            lambda far_sum: hold(far_sum, grad_near, grad_far, x_hat),
            after_far=lambda far_got: hold(far_got, b_late, out_sent, made["grads"]),
            late_core=True,
        )
    )
    grads = made["grads"]
    qa, qb, gate_cols = Sum(*grads[:2], down_order), Sum(*grads[2:4], up_order), grads[4]
    hold(a_part, grad_first)
    a_own = Box(
        lax.psum_scatter(a_part.v, "dp", scatter_dimension=0, tiled=True, axis_index_groups=planes)
    )
    b_same = feed_end.far_one(jnp.concatenate([gb.own(), db.own()], axis=1))
    q_out = [qa.out(), qb.out()]
    back_home = Box((grad_res.v + unit_back(resid, first_scale, grad_first.v)).astype(BF16))
    back_sent = send(back_home, swap_home)

    hold(gate_cols, back_home)
    forget = jnp.concatenate([gate_cols.v[:, k * PAIR + HEAD : k * PAIR + HEAD + fpart] for k in (0, 1)], axis=1).T
    gain_part = functools.reduce(
        jnp.add, [jnp.sum(half(x_hat.v, w).astype(F32) * first_parts[w], axis=0) for w in (0, 1)]
    )
    gain_row = wa.v[:, 3 * part + fpart].astype(F32)
    small = reorder(jnp.concatenate([forget * gain_row[None, :], gain_part[None], gain_two_part], axis=0))
    small = Box(jnp.concatenate([small, jnp.pad(grad_bias, ((0, 0), (0, width - PAIR)))], axis=0))
    small_there = send(small, over_chip(0))

    hold(small, q_out, small_there, o_out, b_same)
    q_late = [qa.rest(), qb.rest()]
    o_late = o_sum.rest()
    hold(feed_end.other, small)
    b_cross = feed_end.far_two()
    small = Box(small.v + small_there.v)
    hold(small, q_late, o_late, back_sent)
    for bit in range(1, bits):
        small = Box(small.v + send(small, over_chip(bit)).v)
    near, far = small.v[:fpart], small.v[fpart:heads]
    gains, bias_sum = small.v[heads : heads + 2], small.v[heads + 2 :]
    spread_out = ((0, 0), (0, width - fpart))
    bias_near, bias_far = (jnp.pad(bias_sum[:, k * HEAD : k * HEAD + fpart], spread_out) for k in (0, 1))
    far_small = Box(jnp.concatenate([far, bias_far, gains], axis=0))
    hold(far_small, q_late, o_late)
    got = send(far_small, over_half)

    own_out = o_sum.own()
    out_halves = [
        jnp.concatenate(
            [own_out[:, h * PAIR : (h + 1) * PAIR], own_out[:, 2 * PAIR + h * HEAD : 2 * PAIR + (h + 1) * HEAD]], axis=1
        )
        for h in (0, 1)
    ]
    q_end = Finish()
    q_same = q_end.far_one(jnp.concatenate([qb.own(), out_halves[1]], axis=1))
    q_cross = q_end.far_two()
    q_here = q_end.near(jnp.concatenate([qa.own(), out_halves[0]], axis=1))
    hold(a_own, q_same)
    feed_end.near(a_own.v)
    hold(got, q_here, b_cross)
    mine = jnp.concatenate(
        [near + got.v[:fpart], bias_near + got.v[fpart : fpart + 1], gains + got.v[fpart + 1 :]], axis=0
    )
    rest = send(mine, over_core).v
    grad_forget = pick(rows_of([mine[:fpart], rest[:fpart]]), rows_of([rest[:fpart], mine[:fpart]])).T
    bias_mine, bias_rest = mine[fpart, :fpart], rest[fpart, :fpart]
    grad_bias_out = pick(jnp.concatenate([bias_mine, bias_rest]), jnp.concatenate([bias_rest, bias_mine]))
    gains = mine[fpart + 1 :] + rest[fpart + 1 :]
    gains = lax.dynamic_slice_in_dim(gains, d * share, share, 1)
    gains = gains + send(gains, over_z).v
    grad_gain_one = gains[0] / attn_gain.astype(F32)
    grad_gain_two = gains[1] / mlp_gain.astype(F32)
    f_zero, f_one = feed_end.land()
    gate_sum, up_sum, down_sum = (
        jnp.concatenate([f[:, k * fcut : (k + 1) * fcut] for f in (f_zero, f_one)], axis=1) for k in range(3)
    )
    done = [Box(v) for v in (gate_sum * gain_two, up_sum * gain_two, down_sum.T, grad_gain_one, grad_gain_two)]
    hold(q_same, done)
    hold(q_cross, q_same)
    gate_out, up_out, down_out, grad_gain_one, grad_gain_two = (b.v for b in done)
    input_grad = reorder(pick_home(back_home, back_sent)).astype(F32)
    output = reorder(pick_home(out_home, out_sent))
    q_zero, q_one = q_end.land()

    def joined(k):
        if k == 3:
            return jnp.concatenate([q_zero[:, qcols:], q_one[:, qcols:]], axis=1)
        lone = slice(3 * PAIR + k * HEAD, 3 * PAIR + (k + 1) * HEAD)
        pair = slice(k * PAIR, (k + 1) * PAIR)
        return jnp.concatenate([q_zero[:, pair], q_zero[:, lone], q_one[:, pair], q_one[:, lone]], axis=1)

    q_sums = [joined(k) for k in range(4)]

    return (
        output,
        input_grad,
        grad_gain_one,
        q_sums[0] * gain_one,
        q_sums[1] * gain_one,
        q_sums[2] * gain_one,
        grad_forget,
        grad_bias_out,
        q_sums[3].T,
        grad_gain_two,
        gate_out,
        up_out,
        down_out,
    )


def solution(mesh):
    return jax.shard_map(
        per_device,
        mesh=mesh,
        in_specs=(
            P(("dp", "tensor"), None),
            P("dp"),
            P("dp", "tensor"),
            P("dp", "tensor"),
            P("dp", "tensor"),
            P(None, "tensor"),
            P("tensor"),
            P("tensor", "dp"),
            P("dp"),
            P("dp", "tensor"),
            P("dp", "tensor"),
            P("tensor", "dp"),
            P("dp", None),
            P(("dp", "tensor"), None),
        ),
        out_specs=(
            P(("dp", "tensor"), None),
            P(("dp", "tensor"), None),
            P("dp"),
            P("dp", "tensor"),
            P("dp", "tensor"),
            P("dp", "tensor"),
            P(None, "tensor"),
            P("tensor"),
            P("tensor", "dp"),
            P("dp"),
            P("dp", "tensor"),
            P("dp", "tensor"),
            P("tensor", "dp"),
        ),
        check_vma=False,
    )
```

```python
import functools

import jax
import jax.numpy as jnp
from jax import lax
from jax.experimental import pallas as pl
from jax.experimental.pallas import tpu as pltpu
from jax.sharding import PartitionSpec as P

HEAD = 64
PAIR = 2 * HEAD
EPS = 1e-06
F32 = jnp.float32
BF16 = jnp.bfloat16
NT = (((1,), (1,)), ((), ()))
TN = (((0,), (0,)), ((), ()))
AXES = ("dp", "tensor")


def nn(a, b):
    return jnp.dot(a, b, preferred_element_type=F32)


def nt(a, b):
    return lax.dot_general(a, b, NT, preferred_element_type=F32)


def tn(a, b):
    return lax.dot_general(a, b, TN, preferred_element_type=F32)


class Box:
    def __init__(self, v):
        self.v = v


def val(value):
    return value.v if isinstance(value, Box) else value


def boxes(tree):
    if isinstance(tree, Box):
        return [tree]
    assert isinstance(tree, (list, tuple)), type(tree)
    return [b for item in tree for b in boxes(item)]


def send(value, move):
    tensor = lax.axis_size("tensor")
    pairs = []
    for d in range(lax.axis_size("dp")):
        for t in range(tensor):
            to = move(d, t)
            if to is not None:
                pairs.append((d * tensor + t, to[0] * tensor + to[1]))
    return Box(lax.ppermute(val(value), AXES, pairs))


def to_home(d, t):
    return (d ^ 1, t ^ 2) if (d & 1) != (t >> 1) else (d, t)


def swap_home(d, t):
    return (d ^ 1, t ^ 2) if (d & 1) != (t >> 1) else None


def over_core(d, t):
    return (d ^ 1, t)


def over_z(d, t):
    return (d, t ^ 1)


def over_chip(bit):
    return lambda d, t: (d ^ (2 << bit), t)


def over_half(d, t):
    return (d, t ^ 2)


def over_core_half(d, t):
    return (d ^ 1, t ^ 2)


def hold(value, *others):
    held = boxes(others)
    result, new = lax.optimization_barrier((jax.tree.map(val, value, is_leaf=lambda x: isinstance(x, Box)), [b.v for b in held]))
    for b, v in zip(held, new):
        b.v = v
    if isinstance(value, Box):
        value.v = result
        return value
    return result


def meet(critical, *others):
    return hold(hold(critical), *others)


def rows_of(pieces):
    return jnp.concatenate([val(p) for p in pieces], axis=0)


def block_of(pos_ref, at, size):
    return pl.ds(pl.multiple_of(pos_ref[at] * size, size), size)


def lane_of(pair, h):
    return jnp.where(pair == 2, 2 + HEAD * h, HEAD * pair + h)


def pack_kernel(core_ref, query_ref, key_ref, value_ref, forget_ref, gain_ref, bias_ref, mine_ref, other_ref):
    share = gain_ref.shape[1]
    diagonal = lax.broadcasted_iota(jnp.int32, (share, share), 0) == lax.broadcasted_iota(jnp.int32, (share, share), 1)
    gain = jnp.sum(jnp.where(diagonal, gain_ref[...].astype(F32), 0.0), axis=1, keepdims=True)
    lane = lax.broadcasted_iota(jnp.int32, (share, PAIR), 1)
    low_lanes = lane < HEAD
    first = core_ref[0] == 0
    parts = [ref[...].astype(F32) * gain for ref in (query_ref, key_ref, value_ref)]
    forget = forget_ref[...].astype(F32) * gain
    bias = bias_ref[...]
    pieces = []
    for _ in range(3):
        piece = bias.astype(BF16).astype(F32)
        pieces.append(piece)
        bias = bias - piece
    halves = []
    for h in range(2):
        three = [p if h == 0 else pltpu.roll(p, p.shape[1] // 2, 1) for p in parts]
        tiles = [p[:, :PAIR] for p in three]
        lone = [p[:, PAIR : 2 * PAIR] for p in three]
        tiles.append(jnp.where(low_lanes, lone[0], pltpu.roll(lone[1], HEAD, 1)))
        rest = jnp.where(lane < HEAD + 3, pltpu.roll(forget, HEAD - 3 * h, 1), gain)
        for k, piece in enumerate(pieces):
            at = HEAD + 4 + 3 * k
            moved = jnp.broadcast_to(pltpu.roll(piece, at - 3 * h, 1), (share, PAIR))
            rest = jnp.where((lane >= at) & (lane < at + 3), moved, rest)
        rest = jnp.where(lane < HEAD + 13, rest, 0.0)
        tiles.append(jnp.where(low_lanes, lone[2], rest))
        halves.append(tiles)
    for k in range(5):
        at = slice(k * PAIR, (k + 1) * PAIR)
        mine_ref[:, at] = jnp.where(first, halves[0][k], halves[1][k]).astype(BF16)
        other_ref[:, at] = jnp.where(first, halves[1][k], halves[0][k]).astype(BF16)


def forward_kernel(
    quarter, pos_ref, x0_ref, x1_ref, x2_ref, x3_ref, wa_ref, wb_ref, bias_ref, segr_ref, segc_ref,
    mixed_ref, xhat_ref, qkv_ref, logit_ref, lse_ref, cum_ref, cumr_ref, rel_ref,
):
    pair = pl.program_id(0)
    width = 3 * PAIR
    lane = lax.broadcasted_iota(jnp.int32, (quarter, PAIR), 1)
    low_lanes = lane < HEAD
    count = segr_ref.shape[1] // quarter

    @pl.when(pair == 0)
    def _():
        for r, x_ref in enumerate((x0_ref, x1_ref, x2_ref, x3_ref)):
            at = slice(r * quarter, (r + 1) * quarter)
            x = x_ref[...].astype(F32)
            low = (x * lax.rsqrt(jnp.mean(x * x, axis=1, keepdims=True) + EPS)).astype(BF16)
            xhat_ref[at, :] = low
            near_all = nn(low, wa_ref[...])
            far_all = nn(low, wb_ref[...])

            def near(k):
                return near_all[:, k * PAIR : (k + 1) * PAIR]

            def far(k):
                return far_all[:, k * PAIR : (k + 1) * PAIR]

            for k in range(3):
                qkv_ref[at, k * width : k * width + PAIR] = near(k).astype(BF16)
                qkv_ref[at, k * width + PAIR : k * width + 2 * PAIR] = far(k).astype(BF16)

            def both(one, two):
                return jnp.where(low_lanes, one, two).astype(BF16)

            qkv_ref[at, 2 * PAIR : 3 * PAIR] = both(near(3), pltpu.roll(far(3), HEAD, 1))
            qkv_ref[at, width + 2 * PAIR : width + 3 * PAIR] = both(pltpu.roll(near(3), HEAD, 1), far(3))
            qkv_ref[at, 2 * width + 2 * PAIR : 2 * width + 3 * PAIR] = both(near(4), pltpu.roll(far(4), HEAD, 1))
            rel_ref[at, :] = jnp.where(low_lanes, pltpu.roll(near(4), HEAD, 1), far(4)) + bias_ref[...]
        rows = lax.broadcasted_iota(jnp.int32, (quarter, quarter), 0)
        cols = lax.broadcasted_iota(jnp.int32, (quarter, quarter), 1)
        lower = (cols <= rows).astype(F32)
        carry = jnp.zeros((1, PAIR), F32)
        for a in range(count):
            logit = rel_ref[block_of(pos_ref, a, quarter), :]
            here = slice(a * quarter, (a + 1) * quarter)
            logit_ref[here, :] = logit
            logsig = jnp.minimum(logit, 0.0) - jnp.log1p(jnp.exp(-jnp.abs(logit)))
            cum = jnp.dot(lower, logsig, precision=lax.Precision.HIGHEST, preferred_element_type=F32) + carry
            carry = cum[quarter - 1 :, :]
            cum_ref[here, :] = cum
            cumr_ref[:, here] = cum.T
        lse_ref[...] = jnp.zeros(lse_ref.shape, F32)

    def columns(part):
        return pl.ds(pl.multiple_of(part * width + pair * PAIR, PAIR), PAIR)

    diag_rows = lax.broadcasted_iota(jnp.int32, (quarter, quarter), 0)
    diag_cols = lax.broadcasted_iota(jnp.int32, (quarter, quarter), 1)
    for a in range(count):
        query = (qkv_ref[block_of(pos_ref, a, quarter), columns(0)] * 0.125).astype(BF16)
        seg_q = segc_ref[a * quarter : (a + 1) * quarter, :]
        spans = range(max(0, a - 512 // quarter), a + 1)
        outs = []
        for h in range(2):
            head = lane_of(pair, h)
            mine = (lane >= HEAD) if h else low_lanes
            query_h = jnp.where(mine, query, jnp.zeros_like(query))
            scores = []
            for b in spans:
                keys = qkv_ref[block_of(pos_ref, b, quarter), columns(1)]
                s = nt(query_h, keys) - cumr_ref[pl.ds(head, 1), b * quarter : (b + 1) * quarter]
                allowed = seg_q == segr_ref[:, b * quarter : (b + 1) * quarter]
                if a == b:
                    allowed &= diag_cols <= diag_rows
                scores.append(jnp.where(allowed, s, -jnp.inf))
            top = functools.reduce(jnp.maximum, [jnp.max(s, axis=1, keepdims=True) for s in scores])
            expd = [jnp.exp(s - top) for s in scores]
            total = functools.reduce(jnp.add, [jnp.sum(e, axis=1, keepdims=True) for e in expd])
            scale = 1.0 / total
            out = None
            for e, b in zip(expd, spans):
                values = qkv_ref[block_of(pos_ref, b, quarter), columns(2)]
                part = nn((e * scale).astype(BF16), values)
                out = part if out is None else out + part
            outs.append(out)
            lse = top + jnp.log(total)
            at = pl.ds(a * quarter, quarter)
            lse_ref[at, :] = jnp.where(lane == head, lse, lse_ref[at, :])
        mixed_ref[block_of(pos_ref, a, quarter), columns(0)] = jnp.where(low_lanes, outs[0], outs[1]).astype(BF16)


def backward_kernel(
    quarter, pos_ref, qkv_ref, logit_ref, segr_ref, segc_ref, lse_ref, cum_ref, gmix_ref,
    gnear_ref, gfar_ref, gbias_ref, lser_ref, gcol_ref, grow_ref, grad_ref, gk_ref, gv_ref,
):
    pair = pl.program_id(0)
    pairs = pl.num_programs(0)
    width = 3 * PAIR
    lane = lax.broadcasted_iota(jnp.int32, (quarter, PAIR), 1)
    low_lanes = lane < HEAD
    count = segr_ref.shape[1] // quarter

    @pl.when(pair == 0)
    def _():
        for a in range(count):
            at = slice(a * quarter, (a + 1) * quarter)
            lser_ref[:, at] = lse_ref[at, :].T
        gcol_ref[...] = jnp.zeros(gcol_ref.shape, F32)
        grow_ref[...] = jnp.zeros(grow_ref.shape, F32)

    def columns(part):
        return pl.ds(pl.multiple_of(part * width + pair * PAIR, PAIR), PAIR)

    diag_rows = lax.broadcasted_iota(jnp.int32, (quarter, quarter), 0)
    diag_cols = lax.broadcasted_iota(jnp.int32, (quarter, quarter), 1)
    gk_ref[...] = jnp.zeros(gk_ref.shape, F32)
    gv_ref[...] = jnp.zeros(gv_ref.shape, F32)
    for a in range(count):
        here = slice(a * quarter, (a + 1) * quarter)
        query = (qkv_ref[block_of(pos_ref, a, quarter), columns(0)] * 0.125).astype(BF16)
        gout = gmix_ref[block_of(pos_ref, a, quarter), columns(0)]
        seg_q = segr_ref[:, here]
        spans = range(max(0, a - 512 // quarter), a + 1)
        grad_query = None
        for h in range(2):
            head = lane_of(pair, h)
            mine = (lane >= HEAD) if h else low_lanes
            query_h = jnp.where(mine, query, jnp.zeros_like(query))
            gout_h = jnp.where(mine, gout, jnp.zeros_like(gout))
            lse = lser_ref[pl.ds(head, 1), here]
            probs, gprobs = [], []
            inner = None
            for b in spans:
                there = slice(b * quarter, (b + 1) * quarter)
                keys = qkv_ref[block_of(pos_ref, b, quarter), columns(1)]
                values = qkv_ref[block_of(pos_ref, b, quarter), columns(2)]
                cum_k = jnp.sum(jnp.where(lane == head, cum_ref[there, :], 0.0), axis=1, keepdims=True)
                s = nt(keys, query_h) - cum_k
                allowed = segc_ref[there, :] == seg_q
                if a == b:
                    allowed &= diag_rows <= diag_cols
                p = jnp.where(allowed, jnp.exp(s - lse), 0.0)
                g = nt(values, gout_h)
                probs.append(p)
                gprobs.append(g)
                part = jnp.sum(p * g, axis=0, keepdims=True)
                inner = part if inner is None else inner + part
            row_sum = None
            for p, g, b in zip(probs, gprobs, spans):
                there = slice(b * quarter, (b + 1) * quarter)
                keys = (qkv_ref[block_of(pos_ref, b, quarter), columns(1)] * 0.125).astype(BF16)
                keys_h = jnp.where(mine, keys, jnp.zeros_like(keys))
                gs = p * (g - inner)
                part = jnp.sum(gs, axis=0, keepdims=True)
                row_sum = part if row_sum is None else row_sum + part
                col_sum = jnp.sum(gs, axis=1, keepdims=True)
                gcol_ref[there, :] += jnp.where(lane == head, col_sum, 0.0)
                low = gs.astype(BF16)
                gk_ref[there, :] += nn(low, query_h)
                gv_ref[there, :] += nn(p.astype(BF16), gout_h)
                part = tn(low, keys_h)
                grad_query = part if grad_query is None else grad_query + part
            grow_ref[pl.ds(head, 1), here] = row_sum
        grad_ref[block_of(pos_ref, a, quarter), columns(0)] = grad_query
    for a in range(count):
        here = slice(a * quarter, (a + 1) * quarter)
        grad_ref[block_of(pos_ref, a, quarter), columns(1)] = gk_ref[here, :]
        grad_ref[block_of(pos_ref, a, quarter), columns(2)] = gv_ref[here, :]

    @pl.when(pair == pairs - 1)
    def _():
        upper = (diag_cols >= diag_rows).astype(F32)
        carry = jnp.zeros((1, PAIR), F32)
        bias = jnp.zeros((1, PAIR), F32)
        real = (lane % HEAD) < pairs
        for a in reversed(range(count)):
            here = slice(a * quarter, (a + 1) * quarter)
            at = block_of(pos_ref, a, quarter)
            logit = logit_ref[here, :]
            gcum = jnp.where(real, grow_ref[:, here].T - gcol_ref[here, :], 0.0)
            back = jnp.dot(upper, gcum, precision=lax.Precision.HIGHEST, preferred_element_type=F32) + carry
            carry = back[:1, :]
            glogit = jnp.where(real, back * (1.0 / (1.0 + jnp.exp(logit))), 0.0)
            bias = bias + jnp.sum(glogit, axis=0, keepdims=True)

            def grad(part, k):
                return grad_ref[at, part * width + k * PAIR : part * width + (k + 1) * PAIR]

            for k in range(3):
                gnear_ref[at, k * PAIR : (k + 1) * PAIR] = grad(k, 0).astype(BF16)
                gfar_ref[at, k * PAIR : (k + 1) * PAIR] = grad(k, 1).astype(BF16)
            q_last, k_last, v_last = grad(0, 2), grad(1, 2), grad(2, 2)
            k_roll = pltpu.roll(k_last, HEAD, 1)
            gnear_ref[at, 3 * PAIR : 4 * PAIR] = jnp.where(low_lanes, q_last, k_roll).astype(BF16)
            gnear_ref[at, 4 * PAIR :] = jnp.where(low_lanes, v_last, pltpu.roll(glogit, HEAD, 1)).astype(BF16)
            gfar_ref[at, 3 * PAIR : 4 * PAIR] = jnp.where(low_lanes, pltpu.roll(q_last, HEAD, 1), k_last).astype(BF16)
            gfar_ref[at, 4 * PAIR :] = jnp.where(low_lanes, pltpu.roll(v_last, HEAD, 1), glogit).astype(BF16)
        gbias_ref[...] = bias


def full_spec(shape):
    return pl.BlockSpec(shape, lambda *_: (0,) * len(shape))


NO_COST = pl.CostEstimate(flops=0, bytes_accessed=0, transcendentals=0)


def params(mib):
    return pltpu.CompilerParams(vmem_limit_bytes=mib * 2**20, dimension_semantics=("arbitrary",))


def pack_one(core, query, keys, values, forget, gain, bias):
    share = gain.shape[1]
    out = jax.ShapeDtypeStruct((share, 5 * PAIR), BF16)
    return pl.pallas_call(
        pack_kernel,
        grid=(1,),
        out_shape=(out, out),
        in_specs=[
            pl.BlockSpec(memory_space=pltpu.SMEM),
            *(full_spec(w.shape) for w in (query, keys, values, forget, gain, bias)),
        ],
        out_specs=(full_spec(out.shape), full_spec(out.shape)),
        compiler_params=params(4),
        cost_estimate=NO_COST,
    )(core, query, keys, values, forget, gain, bias)


def attend(pos, blocks, wa, wb, bias, seg_row, seg_col):
    quarter, wide = blocks[0].shape
    length = 4 * quarter
    width = 3 * PAIR
    small = jax.ShapeDtypeStruct((length, PAIR), F32)
    outs = (
        jax.ShapeDtypeStruct((length, width), BF16),
        jax.ShapeDtypeStruct((length, wide), BF16),
        jax.ShapeDtypeStruct((length, 3 * width), BF16),
        small,
        small,
        small,
    )
    operands = (*blocks, wa, wb, bias, seg_row, seg_col)
    return pl.pallas_call(
        functools.partial(forward_kernel, quarter),
        grid=(3,),
        out_shape=outs,
        in_specs=[pl.BlockSpec(memory_space=pltpu.SMEM), *(full_spec(o.shape) for o in operands)],
        out_specs=tuple(full_spec(o.shape) for o in outs),
        scratch_shapes=[pltpu.VMEM((PAIR, length), F32), pltpu.VMEM((length, PAIR), F32)],
        compiler_params=params(24),
        cost_estimate=NO_COST,
    )(pos, *operands)


def feed_kernel(s0_ref, s1_ref, c0_ref, c1_ref, ga_ref, gb_ref, da_ref, db_ref, *refs):
    hidden_ref, grada_ref, gradb_ref, second_ref, cot_ref, back_ref, gain_ref = refs[-7:]
    cut = da_ref.shape[1]
    block = s0_ref.shape[0]
    gain = None
    for i, (s_ref, c_ref) in enumerate(((s0_ref, c0_ref), (s1_ref, c1_ref))):
        at = slice(i * block, (i + 1) * block)
        second_ref[at, :] = s_ref[...]
        cot_ref[at, :] = c_ref[...]
        back = None
        for k, (w_ref, d_ref, grad_ref) in enumerate(((ga_ref, da_ref, grada_ref), (gb_ref, db_ref, gradb_ref))):
            both = nn(s_ref[...], w_ref[...])
            grad_hidden = nn(c_ref[...], d_ref[...]).astype(BF16).astype(F32)
            gate, upper = both[:, :cut], both[:, cut:]
            sigma = 1.0 / (1.0 + jnp.exp(-gate))
            swish = gate * sigma
            hidden_ref[at, k * cut : (k + 1) * cut] = (swish * upper).astype(BF16)
            grad_gate = (grad_hidden * upper * sigma * (1.0 + gate * (1.0 - sigma))).astype(BF16)
            grad_up = (grad_hidden * swish).astype(BF16)
            grad_ref[at, :cut] = grad_gate
            grad_ref[at, cut:] = grad_up
            part = nt(grad_gate, w_ref[:, :cut]) + nt(grad_up, w_ref[:, cut:])
            back = part if back is None else back + part
        back_ref[at, :] = back
        part = jnp.sum(s_ref[...].astype(F32) * back, axis=0, keepdims=True)
        gain = part if gain is None else gain + part
    gain_ref[...] = gain


def feed_tokens(second, cot, weights, which, before=()):
    block, wide = second[0].shape
    cut = weights[2].shape[1]
    operands = (*second, *cot, *weights)
    widths = (2 * cut, 2 * cut, 2 * cut, wide, wide)
    outs = tuple(jax.ShapeDtypeStruct((4 * block, w), BF16) for w in widths)
    outs += (jax.ShapeDtypeStruct((2 * block, wide), F32), jax.ShapeDtypeStruct((1, wide), F32))
    return pl.pallas_call(
        feed_kernel,
        grid=(1,),
        out_shape=outs,
        in_specs=[*(full_spec(o.shape) for o in operands)] + [pl.BlockSpec(memory_space=pl.ANY)] * len(before),
        out_specs=(
            *(pl.BlockSpec((2 * block, w), lambda i: (which, 0)) for w in widths),
            full_spec((2 * block, wide)),
            full_spec((1, wide)),
        ),
        input_output_aliases={len(operands) + k: k for k in range(len(before))},
        compiler_params=params(25),
        cost_estimate=NO_COST,
    )(*operands, *before)


def put_half(rows, keep_ref, give_ref):
    first = pl.program_id(0) < pl.num_programs(0) // 2

    @pl.when(first)
    def _():
        keep_ref[...] = rows.astype(BF16)

    @pl.when(jnp.logical_not(first))
    def _():
        give_ref[...] = rows.astype(BF16)


def put_pair(rows, keep_ref, give_ref):
    even = pl.program_id(0) % 2 == 0

    @pl.when(even)
    def _():
        keep_ref[...] = rows.astype(BF16)

    @pl.when(jnp.logical_not(even))
    def _():
        give_ref[...] = rows.astype(BF16)


def half_specs(block, cols, half_of):
    return (
        pl.BlockSpec((block, cols), lambda r, *_: (jnp.minimum(r, half_of - 1), 0)),
        pl.BlockSpec((block, cols), lambda r, *_: (jnp.maximum(r - half_of, 0), 0)),
    )


def pair_specs(block, cols):
    return (pl.BlockSpec((block, cols), lambda r, *_: (r // 2, 0)),) * 2


def feed_grads_kernel(
    chip_ref, second_ref, cot_ref, hidden_ref, ga_ref, gb_ref, da_ref, db_ref,
    keepb_ref, giveb_ref, keepd_ref, gived_ref, outa_ref, part_ref,
):
    cut = da_ref.shape[1]
    second, cot = second_ref[...], cot_ref[...]
    put_half(tn(second, gb_ref[...]), keepb_ref, giveb_ref)
    put_pair(tn(cot, hidden_ref[:, cut:]), keepd_ref, gived_ref)
    outa_ref[:, : 2 * cut] = tn(second, ga_ref[...]).astype(BF16)
    outa_ref[:, 2 * cut :] = tn(cot, hidden_ref[:, :cut]).astype(BF16)
    part = nt(hidden_ref[:, :cut], da_ref[...]) + nt(hidden_ref[:, cut:], db_ref[...])
    part_ref[...] = part.astype(BF16)


def pairs_apart(rows, chips):
    block = rows.shape[0] // chips
    return rows_of([rows[r * block : (r + 1) * block] for r in (*range(0, chips, 2), *range(1, chips, 2))])


def halves_apart(rows):
    cut = rows.shape[0] // 2
    return rows[:cut], rows[cut:]


def feed_grads(chip, second, cot, hidden, ga, gb, da, db, chips):
    length, wide = second.shape
    block = wide // chips
    cut = da.shape[1]
    half_of = chips // 2
    if block % PAIR:
        down = tn(cot, hidden).astype(BF16)
        part = nt(hidden[:, :cut], da) + nt(hidden[:, cut:], db)
        own = jnp.concatenate([tn(second, ga).astype(BF16), down[:, :cut]], axis=1)
        own = [lax.dynamic_slice_in_dim(own, (chip[0] ^ r) * block, block, 0) for r in range(chips)]
        halves = halves_apart(tn(second, gb).astype(BF16)) + halves_apart(pairs_apart(down[:, cut:], chips))
        return *halves, rows_of(own), part.astype(BF16)
    cols = pl.BlockSpec((length, block), lambda r, chip: (0, r))
    rows = pl.BlockSpec((block, cut), lambda r, chip: (r, 0))
    return pl.pallas_call(
        feed_grads_kernel,
        out_shape=(
            *(jax.ShapeDtypeStruct((wide // 2, 2 * cut), BF16),) * 2,
            *(jax.ShapeDtypeStruct((wide // 2, cut), BF16),) * 2,
            jax.ShapeDtypeStruct((wide, 3 * cut), BF16),
            jax.ShapeDtypeStruct((length, wide), BF16),
        ),
        grid_spec=pltpu.PrefetchScalarGridSpec(
            num_scalar_prefetch=1,
            grid=(chips,),
            in_specs=[cols, cols, *(full_spec(o.shape) for o in (hidden, ga, gb)), rows, rows],
            out_specs=(
                *half_specs(block, 2 * cut, half_of),
                *pair_specs(block, cut),
                pl.BlockSpec((block, 3 * cut), lambda r, chip: (r ^ chip[0], 0)),
                pl.BlockSpec((length, block), lambda r, chip: (0, r)),
            ),
        ),
        compiler_params=params(23),
        cost_estimate=NO_COST,
    )(chip, second, cot, hidden, ga, gb, da, db)


def first_grads_kernel(x_ref, near_ref, far_ref, keepn_ref, given_ref, keepf_ref, givef_ref, gate_ref):
    x = x_ref[...]
    near, far = tn(x, near_ref[...]), tn(x, far_ref[...])
    put_half(near, keepn_ref, given_ref)
    put_pair(far, keepf_ref, givef_ref)
    gate_ref[:, :PAIR] = near[:, 4 * PAIR :]
    gate_ref[:, PAIR:] = far[:, 4 * PAIR :]


def first_grads(x_hat, near, far, chips):
    length, wide = x_hat.shape
    block = wide // chips
    cols = near.shape[1]
    half_of = chips // 2
    if block % PAIR:
        near, far = tn(x_hat, near), tn(x_hat, far)
        gate = jnp.concatenate([near[:, 4 * PAIR :], far[:, 4 * PAIR :]], axis=1)
        return *halves_apart(near.astype(BF16)), *halves_apart(pairs_apart(far.astype(BF16), chips)), gate
    return pl.pallas_call(
        first_grads_kernel,
        grid=(chips,),
        out_shape=(
            *(jax.ShapeDtypeStruct((wide // 2, cols), BF16),) * 4,
            jax.ShapeDtypeStruct((wide, 2 * PAIR), F32),
        ),
        in_specs=[pl.BlockSpec((length, block), lambda r: (0, r)), full_spec(near.shape), full_spec(far.shape)],
        out_specs=(
            *half_specs(block, cols, half_of),
            *pair_specs(block, cols),
            pl.BlockSpec((block, 2 * PAIR), lambda r: (r, 0)),
        ),
        compiler_params=params(12),
        cost_estimate=NO_COST,
    )(x_hat, near, far)


def attend_back(pos, qkv, logit, seg_row, seg_col, lse, cum, grad_mixed, cols, quarter):
    length = qkv.shape[0]
    grads = jax.ShapeDtypeStruct((length, cols), BF16)
    return pl.pallas_call(
        functools.partial(backward_kernel, quarter),
        grid=(3,),
        out_shape=(grads, grads, jax.ShapeDtypeStruct((1, PAIR), F32)),
        in_specs=[
            pl.BlockSpec(memory_space=pltpu.SMEM),
            full_spec(qkv.shape),
            full_spec(logit.shape),
            full_spec(seg_row.shape),
            full_spec(seg_col.shape),
            full_spec(lse.shape),
            full_spec(cum.shape),
            full_spec(grad_mixed.shape),
        ],
        out_specs=(full_spec((length, cols)), full_spec((length, cols)), full_spec((1, PAIR))),
        scratch_shapes=[
            pltpu.VMEM((PAIR, length), F32),
            pltpu.VMEM((length, PAIR), F32),
            pltpu.VMEM((PAIR, length), F32),
            pltpu.VMEM((length, 9 * PAIR), F32),
            pltpu.VMEM((length, PAIR), F32),
            pltpu.VMEM((length, PAIR), F32),
        ],
        compiler_params=params(25),
        cost_estimate=NO_COST,
    )(pos, qkv, logit, seg_row, seg_col, lse, cum, grad_mixed)


def unit_rows(value):
    scale = lax.rsqrt(jnp.mean(value * value, axis=-1, keepdims=True) + EPS)
    return value * scale, scale


def unit_back(value, scale, weighted):
    inner = jnp.mean(weighted * value, axis=-1, keepdims=True)
    return scale * weighted - value * (scale * scale * scale) * inner


def per_device(
    block_input, attn_gain, w_query, w_key, w_value, w_forget, forget_bias, w_output,
    mlp_gain, w_gate, w_up, w_down, segment_ids, cotangent,
):
    width = block_input.shape[1]
    quarter = block_input.shape[0]
    heads = w_forget.shape[1]
    share = w_query.shape[0]
    inner = w_output.shape[0]
    hidden_width = w_gate.shape[1]
    chips = lax.axis_size("dp") // 2
    bits = chips.bit_length() - 1
    d = lax.axis_index("dp")
    t = lax.axis_index("tensor")
    core, chip = d & 1, d >> 1
    first = core == 0
    at_home = core == t >> 1
    wide = width // chips
    half_heads = heads // 2

    def pick(one, two):
        return jnp.where(first, val(one), val(two))

    def pick_home(one, two):
        return jnp.where(at_home, val(one), val(two))

    def by_parity(mine, other):
        return pick(rows_of([mine, other]), rows_of([other, mine]))

    def reorder(rows):
        return jnp.concatenate(
            [lax.dynamic_slice_in_dim(rows, (chip ^ r) * wide, wide, 1) for r in range(chips)], axis=1
        )

    def reorder_rows(rows):
        return rows_of([lax.dynamic_slice_in_dim(rows, (chip ^ r) * wide, wide, 0) for r in range(chips)])

    planes = [[2 * k + c for k in range(chips)] for c in (0, 1)]
    up_order, down_order = list(range(bits)), list(reversed(range(bits)))

    class Pack:
        def __init__(self, mine, other):
            self.mine, self.other = mine, other

        def near(self, *others):
            self.near_other = send(hold(self.other, *others) if others else self.other, over_core)
            return self.near_other

        def cross(self, *others):
            mine, other = hold((self.mine, self.other), *others) if others else (self.mine, self.other)
            self.crossed = (send(mine, over_half), send(other, over_core_half))
            return self.crossed

        def near_rows(self):
            return by_parity(self.mine, self.near_other)

        def far_rows(self):
            return by_parity(*self.crossed)

    class Spread:
        def __init__(self, rows, order):
            self.pieces, self.order = {0: rows}, order

        def early(self):
            for bit in self.order:
                self.pieces[1 << bit] = send(self.pieces[0], over_chip(bit))
            return [self.pieces[1 << bit] for bit in self.order]

        def late(self):
            before = set(self.pieces)
            for i, bit in enumerate(self.order):
                passed = sum(1 << b for b in self.order[:i])
                for at in range(1, 1 << bits):
                    if not at & ~passed:
                        self.pieces[at | (1 << bit)] = send(self.pieces[at], over_chip(bit))
            return [v for k, v in self.pieces.items() if k not in before]

        def direct(self):
            for at in range(1, chips):
                self.pieces[at] = send(self.pieces[0], lambda d, t, at=at: (d ^ (2 * at), t))
            return [self.pieces[at] for at in range(1, chips)]

        def whole(self):
            return rows_of([self.pieces[r] for r in range(chips)])

    class Sum:
        def __init__(self, keep, give, order):
            self.order = order
            self.keep, self.give = Box(val(keep)), Box(val(give))

        def made(self):
            return self.keep, self.give

        def out(self):
            self.got = send(self.give, over_chip(self.order[0]))
            return self.got

        def rest(self):
            rows = self.keep.v.astype(F32) + self.got.v.astype(F32)
            for bit in self.order[1:]:
                if self.order == down_order:
                    cut = rows.shape[0] // 2
                    self.keep, give = Box(rows[:cut]), rows[cut:]
                else:
                    blocks = [rows[k : k + wide] for k in range(0, rows.shape[0], wide)]
                    self.keep, give = Box(rows_of(blocks[0::2])), rows_of(blocks[1::2])
                self.last = send(give.astype(BF16), over_chip(bit))
                if bit != self.order[-1]:
                    rows = self.keep.v + self.last.v.astype(F32)
            return self.last

        def own(self):
            return (self.keep.v + self.last.v.astype(F32)).astype(BF16)

    class Finish:
        def near(self, rows):
            self.mine_near, other = pick(rows[:share], rows[share:]), pick(rows[share:], rows[:share])
            self.here = send(other, over_core)
            return self.here

        def far_one(self, rows):
            mine, other = pick(rows[:share], rows[share:]), pick(rows[share:], rows[:share])
            self.other = Box(other)
            self.same = send(mine, over_half)
            return self.same

        def far_two(self):
            self.cross = send(self.other, over_core_half)
            return self.cross

        def land(self):
            mine = self.mine_near.astype(F32) + self.same.v.astype(F32)
            rest = self.here.v.astype(F32) + self.cross.v.astype(F32)
            return pick(mine, rest), pick(rest, mine)

    gain_one = attn_gain.astype(F32)[:, None]
    gain_two = mlp_gain.astype(F32)[:, None]
    part, fpart = inner // 2, half_heads
    fcut = hidden_width // 2
    lanes = ((0, 0), (0, PAIR - heads))
    forget_own = jnp.pad(lax.dynamic_slice_in_dim(w_forget, d * share, share, 0), lanes)
    one = Pack(
        *pack_one(
            core.astype(jnp.int32)[None], w_query, w_key, w_value, forget_own, attn_gain[None, :],
            jnp.pad(forget_bias[None, :], lanes),
        )
    )
    out_t, down_t = w_output.T, w_down.T
    gate_scaled, up_scaled = ((w.astype(F32) * gain_two).astype(BF16) for w in (w_gate, w_up))

    def halves_of(arrays, size):
        halves = [jnp.concatenate([w[:, h * size : (h + 1) * size] for w in arrays], axis=1) for h in (0, 1)]
        return pick(*halves), pick(*halves[::-1])

    def stay(d, t):
        return (d, t ^ 1) if (d & 1) == (t >> 1) else None

    def move(d, t):
        return (d, t ^ 1) if (d & 1) != (t >> 1) else None

    one_far = one.cross()
    one.near()
    near_one = Spread(one.near_rows(), up_order)
    near_early = near_one.early()
    x_own, cot_own = Box(reorder(block_input)), Box(reorder(cotangent))

    x_stay = send(x_own, stay)

    hold(x_own, one_far, near_early, x_stay)
    x_home = send(x_own, to_home)
    cot_stay = send(hold(cot_own, x_own), stay)
    far_one = Spread(one.far_rows(), down_order)
    far_early = far_one.early()
    near_late = near_one.late()
    wo = Pack(*halves_of([out_t], part))
    feed_pack = Pack(*halves_of([gate_scaled, up_scaled, down_t], fcut))
    gate_pack, down_pack = Pack(*halves_of([gate_scaled, up_scaled], fcut)), Pack(*halves_of([down_t], fcut))

    hold(x_home, far_early, cot_stay)
    x_move = send(x_home, move)
    x_core = send(x_home, over_core)
    far_late = far_one.late()
    wo_far = wo.cross(x_home)
    wo.near(x_home)
    seg_other = send(hold(segment_ids, x_home), over_core)
    feed_pack.near(x_home)
    near_all = Box(
        lax.all_gather(feed_pack.near_rows(), "dp", axis=0, tiled=True, axis_index_groups=planes)
    )
    seg_row = Box(pick_home(segment_ids, seg_other))
    far_bias = far_one.pieces[0][0, 4 * PAIR + HEAD + fpart + 1 :].astype(F32)
    bias_far = far_bias[:fpart] + far_bias[fpart : 2 * fpart] + far_bias[2 * fpart : 3 * fpart]
    spare = jnp.zeros((HEAD - fpart,), F32)
    bias = Box(jnp.concatenate([pick(forget_bias[:fpart], forget_bias[fpart:]), spare, bias_far, spare])[None, :])
    place = (t & 1) + 2 * core
    pos = jnp.stack([((a ^ place) >> 1) | (((a ^ place) & 1) << 1) for a in range(4)]).astype(jnp.int32)
    wa = Box(near_one.whole())

    hold(x_move, wa, bias, seg_row)
    hold(x_move, far_late, wo_far)
    x_z = Box(pick_home(x_stay, x_move))
    x_both = send(x_z, over_core)
    wb = Box(far_one.whole())
    hold(x_both, wb, x_core)
    wo_a, wo_b = wo.near_rows(), wo.far_rows()
    wo_rows = jnp.concatenate([wo_a[:, :PAIR], wo_b[:, :PAIR], wo_a[:, PAIR:], wo_b[:, PAIR:]], axis=1)
    wo_spread = Spread(wo_rows, up_order)
    wo_sent = wo_spread.direct()
    gate_far = gate_pack.cross(x_both)
    qcols = wa.v.shape[1]

    resid = x_home.v.astype(F32)
    first_scale = unit_rows(resid)[1]
    seg_col = seg_row.v.reshape(-1, 1)
    mixed, x_hat, qkv, logit, lse, cum = attend(
        pos, [x_home.v, x_core.v, x_z.v, x_both.v], wa.v, wb.v, bias.v, seg_row.v, seg_col
    )
    mixed = hold(mixed, wo_sent, gate_far)
    wo_t = wo_spread.whole()

    def half(array, which):
        rows = array.shape[0] // 2
        return array[which * rows : (which + 1) * rows]

    order = {}

    def scatter_group(far, near, at_far=lambda far_sum: None, at_near=lambda near_sum: None, at_end=lambda: (), after_far=None, late_core=False):
        rows = far()
        far_in = send(rows[quarter:].astype(BF16), over_core)
        far_sum = Box((rows[:quarter].astype(F32) + far_in.v.astype(F32)).astype(BF16))
        at_far(far_sum)
        far_got = send(far_sum, over_z)
        rows = Box(near())
        if late_core:
            hold(far_got, rows)
            if after_far:
                after_far(far_got)
            hold(rows, far_got)
        near_in = send(rows.v[quarter:].astype(BF16), over_core)
        near_sum = Box(rows.v[:quarter].astype(F32) + near_in.v.astype(F32))
        at_near(near_sum)
        hold(far_got, near_sum)
        if at_end():
            hold(far_got, at_end())
        return near_sum.v + far_got.v.astype(F32)

    sent = {}

    def weights_on(near_sum):
        sent["gate"] = Spread(gate_pack.far_rows(), up_order)
        sent["early"] = sent["gate"].early()
        sent["down"] = down_pack.cross(near_sum)

    mixed = Box(mixed)
    hidden_res = Box(
        resid
        + scatter_group(
            lambda: nt(half(mixed.v, 1), wo_t),
            lambda: nt(half(mixed.v, 0), wo_t),
            lambda far_sum: hold(far_sum, mixed),
            weights_on,
            lambda: (sent["early"], sent["down"]),
        )
    )
    far_gate = sent["gate"]
    second, second_scale = unit_rows(hidden_res.v)
    second_low = Box(second.astype(BF16))
    second_z = send(second_low, over_z)
    second_core = send(second_low, over_core)
    gate_late = far_gate.late()
    far_down = Spread(down_pack.far_rows(), down_order)
    down_early = far_down.early()
    hold(cot_own, second_core)
    cot_home = send(cot_own, swap_home)
    hold(near_all, second_core)
    gates_a = Box(reorder_rows(near_all.v[:, : 2 * fcut]))
    downs_a = Box(reorder_rows(near_all.v[:, 2 * fcut :]))
    hold(second_z, gates_a, downs_a)
    hold(second_z, cot_home, gate_late, down_early)
    second_both = send(second_z, over_core)
    cot_home = Box(pick_home(cot_own, cot_home))
    cot_move = send(cot_home, move)
    down_late = far_down.late()
    cot_core = send(cot_home, over_core)
    gates_b = Box(far_gate.whole())
    hold(cot_move, second_both, gates_b)
    hold(cot_move, down_late)
    downs_b = Box(far_down.whole())
    cot_z = Box(pick_home(cot_stay, cot_move))
    cot_both = send(cot_z, over_core)
    hold(cot_both, cot_core)

    feed_weights = (gates_a.v, gates_b.v, downs_a.v, downs_b.v)
    made = {}

    def feed_far():
        made["far"] = feed_tokens((second_z.v, second_both.v), (cot_z.v, cot_both.v), feed_weights, 1)
        return made["far"][5]

    def feed_near():
        made["near"] = feed_tokens(
            (second_low.v, second_core.v), (cot_home.v, cot_core.v), feed_weights, 0, made["far"][:5]
        )
        return made["near"][5]

    grad_second = scatter_group(feed_far, feed_near, lambda far_sum: hold(far_sum, second_low, second_core), late_core=True)
    gain_two_part = made["far"][6] + made["near"][6]
    grad_res = Box(cot_home.v.astype(F32) + unit_back(hidden_res.v, second_scale, grad_second))
    branch = Box(grad_res.v.astype(BF16))
    laid = [Box(m) for m in made["near"][:5]]
    hold(branch, laid)
    branch_z = send(branch, over_z)
    hidden, grads_a, grads_b, second_all, cot_all = (m.v for m in laid)
    *b_rows, a_part, mlp_rows = (
        Box(m)
        for m in feed_grads(
            chip.astype(jnp.int32)[None], second_all, cot_all, hidden, grads_a, grads_b, downs_a.v, downs_b.v, chips
        )
    )
    hold(branch_z, b_rows, a_part, mlp_rows)
    hold(branch, branch_z)
    branch_both = send(branch_z, over_core)
    branch_core = send(branch, over_core)
    gb, db = Sum(*b_rows[:2], down_order), Sum(*b_rows[2:], up_order)
    b_out = [gb.out(), db.out()]
    branch_all = Box(rows_of([branch, branch_core, branch_z, branch_both]))

    grad_mixed = Box(nn(branch_all.v, wo_t).astype(BF16))
    mlp_out = Box(scatter_group(lambda: half(mlp_rows.v, 1), lambda: half(mlp_rows.v, 0)))
    hold(branch_all, grad_mixed)
    o_sum = Sum(*halves_apart(tn(branch_all.v, mixed.v).astype(BF16)), down_order)
    o_out = o_sum.out()
    hold(grad_mixed, o_sum.keep)
    grad_near, grad_far, grad_bias = attend_back(
        pos, qkv, logit, seg_row.v, seg_col, lse, cum, grad_mixed.v, qcols, quarter
    )
    grad_near, grad_far, x_hat = Box(grad_near), Box(grad_far), Box(x_hat)
    hold(grad_near, grad_far, b_out, mlp_out)
    out_home = (hidden_res.v + mlp_out.v).astype(BF16)
    out_sent = send(out_home, swap_home)
    b_late = [gb.rest(), db.rest()]
    first_parts = {}
    feed_end = Finish()

    def first_part(which):
        first_parts[which] = nt(half(grad_near.v, which), wa.v) + nt(half(grad_far.v, which), wb.v)
        return first_parts[which]

    def first_near():
        rows = Box(first_part(0))
        hold(x_hat, rows)
        made["grads"] = [Box(g) for g in first_grads(x_hat.v, grad_near.v, grad_far.v, chips)]
        return rows.v

    grad_first = Box(
        scatter_group(
            lambda: first_part(1),
            first_near,
            lambda far_sum: hold(far_sum, grad_near, grad_far, x_hat),
            after_far=lambda far_got: hold(far_got, b_late, out_sent, made["grads"]),
            late_core=True,
        )
    )
    grads = made["grads"]
    qa, qb, gate_cols = Sum(*grads[:2], down_order), Sum(*grads[2:4], up_order), grads[4]
    hold(a_part, grad_first)
    a_own = Box(
        lax.psum_scatter(a_part.v, "dp", scatter_dimension=0, tiled=True, axis_index_groups=planes)
    )
    b_same = feed_end.far_one(jnp.concatenate([gb.own(), db.own()], axis=1))
    q_out = [qa.out(), qb.out()]
    back_home = Box((grad_res.v + unit_back(resid, first_scale, grad_first.v)).astype(BF16))
    back_sent = send(back_home, swap_home)

    hold(gate_cols, back_home)
    forget = jnp.concatenate([gate_cols.v[:, k * PAIR + HEAD : k * PAIR + HEAD + fpart] for k in (0, 1)], axis=1).T
    gain_part = functools.reduce(
        jnp.add, [jnp.sum(half(x_hat.v, w).astype(F32) * first_parts[w], axis=0) for w in (0, 1)]
    )
    gain_row = wa.v[:, 3 * part + fpart].astype(F32)
    small = reorder(jnp.concatenate([forget * gain_row[None, :], gain_part[None], gain_two_part], axis=0))
    small = Box(jnp.concatenate([small, jnp.pad(grad_bias, ((0, 0), (0, width - PAIR)))], axis=0))
    small_there = send(small, over_chip(0))

    hold(small, q_out, small_there, o_out, b_same)
    q_late = [qa.rest(), qb.rest()]
    o_late = o_sum.rest()
    hold(feed_end.other, small)
    b_cross = feed_end.far_two()
    small = Box(small.v + small_there.v)
    hold(small, q_late, o_late, back_sent)
    for bit in range(1, bits):
        small = Box(small.v + send(small, over_chip(bit)).v)
    near, far = small.v[:fpart], small.v[fpart:heads]
    gains, bias_sum = small.v[heads : heads + 2], small.v[heads + 2 :]
    spread_out = ((0, 0), (0, width - fpart))
    bias_near, bias_far = (jnp.pad(bias_sum[:, k * HEAD : k * HEAD + fpart], spread_out) for k in (0, 1))
    far_small = Box(jnp.concatenate([far, bias_far, gains], axis=0))
    hold(far_small, q_late, o_late)
    got = send(far_small, over_half)

    own_out = o_sum.own()
    out_halves = [
        jnp.concatenate(
            [own_out[:, h * PAIR : (h + 1) * PAIR], own_out[:, 2 * PAIR + h * HEAD : 2 * PAIR + (h + 1) * HEAD]], axis=1
        )
        for h in (0, 1)
    ]
    q_end = Finish()
    q_same = q_end.far_one(jnp.concatenate([qb.own(), out_halves[1]], axis=1))
    q_cross = q_end.far_two()
    q_here = q_end.near(jnp.concatenate([qa.own(), out_halves[0]], axis=1))
    hold(a_own, q_same)
    feed_end.near(a_own.v)
    hold(got, q_here, b_cross)
    mine = jnp.concatenate(
        [near + got.v[:fpart], bias_near + got.v[fpart : fpart + 1], gains + got.v[fpart + 1 :]], axis=0
    )
    rest = send(mine, over_core).v
    grad_forget = pick(rows_of([mine[:fpart], rest[:fpart]]), rows_of([rest[:fpart], mine[:fpart]])).T
    bias_mine, bias_rest = mine[fpart, :fpart], rest[fpart, :fpart]
    grad_bias_out = pick(jnp.concatenate([bias_mine, bias_rest]), jnp.concatenate([bias_rest, bias_mine]))
    gains = mine[fpart + 1 :] + rest[fpart + 1 :]
    gains = lax.dynamic_slice_in_dim(gains, d * share, share, 1)
    gains = gains + send(gains, over_z).v
    grad_gain_one = gains[0] / attn_gain.astype(F32)
    grad_gain_two = gains[1] / mlp_gain.astype(F32)
    f_zero, f_one = feed_end.land()
    gate_sum, up_sum, down_sum = (
        jnp.concatenate([f[:, k * fcut : (k + 1) * fcut] for f in (f_zero, f_one)], axis=1) for k in range(3)
    )
    done = [Box(v) for v in (gate_sum * gain_two, up_sum * gain_two, down_sum.T, grad_gain_one, grad_gain_two)]
    hold(q_same, done)
    hold(q_cross, q_same)
    gate_out, up_out, down_out, grad_gain_one, grad_gain_two = (b.v for b in done)
    input_grad = reorder(pick_home(back_home, back_sent)).astype(F32)
    output = reorder(pick_home(out_home, out_sent))
    q_zero, q_one = q_end.land()

    def joined(k):
        if k == 3:
            return jnp.concatenate([q_zero[:, qcols:], q_one[:, qcols:]], axis=1)
        lone = slice(3 * PAIR + k * HEAD, 3 * PAIR + (k + 1) * HEAD)
        pair = slice(k * PAIR, (k + 1) * PAIR)
        return jnp.concatenate([q_zero[:, pair], q_zero[:, lone], q_one[:, pair], q_one[:, lone]], axis=1)

    q_sums = [joined(k) for k in range(4)]

    return (
        output,
        input_grad,
        grad_gain_one,
        q_sums[0] * gain_one,
        q_sums[1] * gain_one,
        q_sums[2] * gain_one,
        grad_forget,
        grad_bias_out,
        q_sums[3].T,
        grad_gain_two,
        gate_out,
        up_out,
        down_out,
    )


def solution(mesh):
    return jax.shard_map(
        per_device,
        mesh=mesh,
        in_specs=(
            P(("dp", "tensor"), None),
            P("dp"),
            P("dp", "tensor"),
            P("dp", "tensor"),
            P("dp", "tensor"),
            P(None, "tensor"),
            P("tensor"),
            P("tensor", "dp"),
            P("dp"),
            P("dp", "tensor"),
            P("dp", "tensor"),
            P("tensor", "dp"),
            P("dp", None),
            P(("dp", "tensor"), None),
        ),
        out_specs=(
            P(("dp", "tensor"), None),
            P(("dp", "tensor"), None),
            P("dp"),
            P("dp", "tensor"),
            P("dp", "tensor"),
            P("dp", "tensor"),
            P(None, "tensor"),
            P("tensor"),
            P("tensor", "dp"),
            P("dp"),
            P("dp", "tensor"),
            P("dp", "tensor"),
            P("tensor", "dp"),
        ),
        check_vma=False,
    )
```
